32 devices in a mesh: groups: 2 (over x), leaf: 8 (over z, y), rhs: 2 (over core).
Axes of the slice: x: 2, y: 2, z: 4, core: 2. Of those that a mesh axis runs over, the one named last changes fastest.
Arguments:
- vectors: bfloat16 [64, 65536], P('rhs', ('groups', 'leaf')), parts along dimension 1, may hold values from -6 to 6
- tree_order: int32 [65536], P(('groups', 'leaf')), parts along dimension 0, may hold values from 0 to 32767, as said below
- leaf_basis: bfloat16 [32, 65536], P(None, ('groups', 'leaf')), parts along dimension 1, may hold values from -0.75 to 0.75
- near_blocks: bfloat16 [1024, 64, 256], P(('groups', 'leaf')), parts along dimension 0, may hold values from -0.375 to 0.375
- near_lists: int32 [1024, 4], P(('groups', 'leaf')), parts along dimension 0, may hold values from 0 to 511, as said below
- transfers: bfloat16 [32, 32, 2016], P(None, None, ('groups', 'leaf')), parts along dimension 2, may hold values from -0.8984375 to 0.8984375
- couplings: bfloat16 [6, 32, 32, 2016], P(None, None, None, ('groups', 'leaf')), parts along dimension 3, may hold values from -0.4375 to 0.4375
- coupling_lists: int32 [2016, 6], P(('groups', 'leaf')), parts along dimension 0, may hold values from -1 to 511, as said below
- top_transfers: bfloat16 [32, 32, 28], P(None, None, 'groups'), parts along dimension 2, may hold values from -0.8984375 to 0.8984375
- top_couplings: bfloat16 [6, 32, 32, 30], P(None, None, None, 'groups'), parts along dimension 3, may hold values from -0.4375 to 0.4375
- top_lists: int32 [30, 6], P('groups'), parts along dimension 0, may hold values from -1 to 7, as said below
Outputs:
- applied: float32 [64, 65536], P('rhs', ('groups', 'leaf')), parts along dimension 1
The draws below stay inside these ranges and needn't reach their ends.
There are 2 independent parts, one for each index of `groups`. The reference program is written for one: setup_inputs(seed, part) draws one part's arguments, and reference() takes and returns one part's arrays. A program takes and returns all parts, laid end to end along the dimension named above; each array names one. Nothing has to cross between parts.
Inputs may be any that keep to these rules, and one draw needn't show every extreme that they name: tree_order is a permutation of the part's points; tree_order[j] lies in the same block of 32768 positions as j (the points of 8 neighbouring devices along `leaf`). near_lists[i, 0] = i; every entry lies within 8 leaves of i, and that distance is reached. `coupling_lists`: the row of node g of level k (m = 64 >> k) holds used slots first, then -1; a used entry is a node of level k other than g and at most m away from it, and that distance is reached; some node of every level uses all 6 slots. `top_lists`: the row of node j of top level t holds used slots first, then -1; a used entry is a node of that level other than j; a level of one node has none.
All inputs are finite; a program needn't handle non-finite values.
Results may differ from the reference program's by a relative error of at most 0.011.
Values may be sent and summed in bfloat16 or wider, within the bound.
No kernel may reach another device: no remote copies, remote signals or barrier semaphores. Data moves between devices by JAX's collectives and lax.ppermute only.
A program may use at most 128 MiB of HBM per device.

```python
import jax
import jax.numpy as jnp
from jax import lax

LEAF = 64
R = 32
NRHS = 64
NB = 4
K = 6
LEVELS = 6
LEAVES = 64
REACH = 8
NLEAVES = 512
NPTS = 32768
CN_DEV = 126
NTOP = 8
TOPN = 15
N_LEAF = 8


def draw_tree_order(key, part):
    key = jax.random.fold_in(key, 11)
    points_dev = LEAF * LEAVES
    upper = (2 ** 31 - 1) // points_dev
    scores = jax.random.randint(key, (N_LEAF, points_dev), 0, upper) * points_dev + jnp.arange(points_dev, dtype=jnp.int32)[None, :]
    ordering = jnp.argsort(scores, axis=1, stable=True).astype(jnp.int32)
    ordering = ordering + (jnp.arange(N_LEAF, dtype=jnp.int32) * points_dev)[:, None]
    return ordering.reshape(-1).astype(jnp.int32)


def draw_near_lists(key, part):
    key = jax.random.fold_in(key, 12)
    leaf_ids = jnp.arange(NLEAVES, dtype=jnp.int32)
    candidates = 2 * REACH
    upper = (2 ** 31 - 1) // candidates
    scores = jax.random.randint(key, (NLEAVES, candidates), 0, upper) * candidates + jnp.arange(candidates, dtype=jnp.int32)[None, :]
    chosen = lax.top_k(scores, NB - 1)[1].astype(jnp.int32)
    offsets = jnp.where(chosen < REACH, chosen - REACH, chosen - REACH + 1)
    targets = leaf_ids[:, None] + offsets
    outside = (targets < 0) | (targets >= NLEAVES)
    targets = jnp.where(outside, leaf_ids[:, None] - offsets, targets)
    first_leaf = (leaf_ids % LEAVES == 0) & (leaf_ids >= REACH)
    last_leaf = (leaf_ids % LEAVES == LEAVES - 1) & (leaf_ids + REACH < NLEAVES)
    forced = jnp.where(first_leaf, leaf_ids - REACH, jnp.where(last_leaf, leaf_ids + REACH, targets[:, 0]))
    targets = targets.at[:, 0].set(forced)
    return jnp.concatenate([leaf_ids[:, None], targets], axis=1).astype(jnp.int32)


def draw_coupling_lists(key, part):
    key = jax.random.fold_in(key, 13)
    pieces = []
    for tree_depth in range(LEVELS):
        node_count = LEAVES >> tree_depth
        total_nodes = node_count * N_LEAF
        key_offsets, key_used = jax.random.split(jax.random.fold_in(key, tree_depth))
        node_ids = jnp.arange(total_nodes, dtype=jnp.int32)
        offsets = jax.random.randint(key_offsets, (total_nodes, K), -node_count, node_count)
        offsets = jnp.where(offsets >= 0, offsets + 1, offsets)
        targets = node_ids[:, None] + offsets
        outside = (targets < 0) | (targets >= total_nodes)
        targets = jnp.where(outside, node_ids[:, None] - offsets, targets)
        inner = node_ids % node_count
        first_node = (inner == 0) & (node_ids >= node_count)
        last_node = (inner == node_count - 1) & (node_ids + node_count < total_nodes)
        forced = jnp.where(first_node, node_ids - node_count, jnp.where(last_node, node_ids + node_count, targets[:, 0]))
        targets = targets.at[:, 0].set(forced)
        used = jax.random.randint(key_used, (total_nodes,), 1, K + 1)
        used = jnp.where(inner == 0, K, used)
        targets = jnp.where(jnp.arange(K, dtype=jnp.int32)[None, :] < used[:, None], targets, -1)
        pieces.append(targets.reshape(N_LEAF, node_count, K))
    return jnp.concatenate(pieces, axis=1).reshape(N_LEAF * CN_DEV, K).astype(jnp.int32)


def draw_top_lists(key, part):
    key = jax.random.fold_in(key, 14)
    pieces = []
    node_count = NTOP
    tree_depth = 0
    while node_count > 1:
        key_picks, key_used = jax.random.split(jax.random.fold_in(key, tree_depth))
        node_ids = jnp.arange(node_count, dtype=jnp.int32)
        picks = jax.random.randint(key_picks, (node_count, K), 0, node_count - 1)
        picks = jnp.where(picks >= node_ids[:, None], picks + 1, picks)
        picks = picks.at[0, 0].set(node_count - 1)
        used = jax.random.randint(key_used, (node_count,), 1, K + 1)
        used = jnp.where(node_ids == 0, K, used)
        picks = jnp.where(jnp.arange(K, dtype=jnp.int32)[None, :] < used[:, None], picks, -1)
        pieces.append(picks)
        node_count = node_count // 2
        tree_depth = tree_depth + 1
    pieces.append(jnp.full((1, K), -1, jnp.int32))
    return jnp.concatenate(pieces, axis=0).astype(jnp.int32)


def block_levels(key, dims, cuts, smallest, top_value):
    loudness = 1.0
    for position, blocks in cuts:
        heights = jax.random.uniform(jax.random.fold_in(jax.random.fold_in(key, 6), position), (blocks,), jnp.float32, smallest / len(cuts), top_value / len(cuts))
        loudness = loudness * jnp.repeat(jnp.exp(heights), dims[position] // blocks).reshape((-1,) + (1,) * (len(dims) - 1 - position))
    return loudness


def centred(stream_key, extent, scale, bound, shards=(), kind=jnp.bfloat16):
    values = jax.random.normal(stream_key, extent, jnp.float32) * scale
    if len(shards) > 0:
        values = block_levels(stream_key, extent, shards, -0.22, 0.18) * values
    return jnp.clip(values, min=-bound, max=bound).astype(kind)


def setup_inputs(seed: int = 0, part: int = 0) -> dict:
    streams_of = jax.random.split(jax.random.key(seed), 12)
    part_splits = jax.random.split(jax.random.fold_in(streams_of[11], part), 12)
    vectors = centred(part_splits[0], (NRHS, NPTS), 1.0, 6.0, ((0, 2), (1, 8)))
    tree_order = draw_tree_order(jax.random.fold_in(jax.random.fold_in(streams_of[11], part), 71), part)
    leaf_basis = centred(part_splits[2], (R, NPTS), LEAF ** -0.5, 0.75, ((1, 8),))
    near_blocks = centred(part_splits[3], (NLEAVES, LEAF, NB * LEAF), (NB * LEAF) ** -0.5, 0.375, ((0, 8),))
    near_lists = draw_near_lists(jax.random.fold_in(jax.random.fold_in(streams_of[11], part), 71), part)
    transfers = centred(part_splits[5], (R, R, CN_DEV * N_LEAF), 0.1487, 0.8984375, ((2, 8),))
    couplings = centred(part_splits[6], (K, R, R, CN_DEV * N_LEAF), (K * R) ** -0.5, 0.4375, ((3, 8),))
    coupling_lists = draw_coupling_lists(jax.random.fold_in(jax.random.fold_in(streams_of[11], part), 71), part)
    top_transfers = centred(part_splits[8], (R, R, TOPN - 1), 0.1487, 0.8984375)
    top_couplings = centred(part_splits[9], (K, R, R, TOPN), (K * R) ** -0.5, 0.4375)
    top_lists = draw_top_lists(jax.random.fold_in(jax.random.fold_in(streams_of[11], part), 71), part)
    return {"vectors": vectors, "tree_order": tree_order, "leaf_basis": leaf_basis, "near_blocks": near_blocks, "near_lists": near_lists, "transfers": transfers, "couplings": couplings, "coupling_lists": coupling_lists, "top_transfers": top_transfers, "top_couplings": top_couplings, "top_lists": top_lists}


def local_rows(tree_depth):
    node_count = LEAVES >> tree_depth
    node_ids = jnp.arange(node_count * N_LEAF, dtype=jnp.int32)
    return ((node_ids // node_count) * CN_DEV + 2 * LEAVES - 2 * node_count + node_ids % node_count).astype(jnp.int32)


def couple_level(coeffs, matrices, partners):
    summed = jnp.zeros(coeffs.shape, jnp.float32)
    for slot_index in range(partners.shape[1]):
        column_ids = partners[:, slot_index]
        in_use = (column_ids >= 0).astype(jnp.float32)
        picked = jnp.take(coeffs, jnp.maximum(column_ids, 0), axis=2).astype(jnp.float32)
        product = jnp.einsum("abi,hbi->hai", matrices[slot_index].astype(jnp.float32), picked)
        summed = summed + product * in_use[None, None, :]
    return summed


def lift_level(coeffs, matrices):
    lifted = jnp.einsum("abc,hac->hbc", matrices.astype(jnp.float32), coeffs.astype(jnp.float32))
    return lifted.reshape(lifted.shape[0], lifted.shape[1], -1, 2).sum(axis=3).astype(jnp.bfloat16)


def lower_level(field_sum, matrices, downward):
    parents = jnp.repeat(downward, 2, axis=2).astype(jnp.float32)
    return (field_sum + jnp.einsum("abc,hbc->hac", matrices.astype(jnp.float32), parents)).astype(jnp.bfloat16)


def reference(vectors, tree_order, leaf_basis, near_blocks, near_lists, transfers, couplings, coupling_lists, top_transfers, top_couplings, top_lists):
    ordered = jnp.take(vectors, tree_order, axis=1)
    by_leaf = ordered.reshape(NRHS, NLEAVES, LEAF)
    near_part = jnp.zeros((NRHS, NLEAVES, LEAF), jnp.float32)
    for slot_index in range(NB):
        picked = jnp.take(by_leaf, near_lists[:, slot_index], axis=1).astype(jnp.float32)
        block_part = near_blocks[:, :, slot_index * LEAF:(slot_index + 1) * LEAF].astype(jnp.float32)
        near_part = near_part + jnp.einsum("lqp,hlp->hlq", block_part, picked)
    basis_leaves = leaf_basis.reshape(R, NLEAVES, LEAF).astype(jnp.float32)
    coeffs = jnp.einsum("alp,hlp->hal", basis_leaves, by_leaf.astype(jnp.float32)).astype(jnp.bfloat16)
    level_list = []
    for tree_depth in range(LEVELS):
        node_rows = local_rows(tree_depth)
        level_list.append((coeffs, node_rows))
        coeffs = lift_level(coeffs, jnp.take(transfers, node_rows, axis=2))
    top_list = []
    node_count = NTOP
    offset = 0
    while node_count > 1:
        top_list.append((coeffs, offset, node_count))
        coeffs = lift_level(coeffs, top_transfers[:, :, offset:offset + node_count])
        offset = offset + node_count
        node_count = node_count // 2
    downward = couple_level(coeffs, top_couplings[:, :, :, offset:offset + 1], top_lists[offset:offset + 1]).astype(jnp.bfloat16)
    for coeffs_level, offset, node_count in reversed(top_list):
        field_sum = couple_level(coeffs_level, top_couplings[:, :, :, offset:offset + node_count], top_lists[offset:offset + node_count])
        downward = lower_level(field_sum, top_transfers[:, :, offset:offset + node_count], downward)
    for coeffs_level, node_rows in reversed(level_list):
        field_sum = couple_level(coeffs_level, jnp.take(couplings, node_rows, axis=3), jnp.take(coupling_lists, node_rows, axis=0))
        downward = lower_level(field_sum, jnp.take(transfers, node_rows, axis=2), downward)
    far_part = jnp.einsum("alp,hal->hlp", basis_leaves, downward.astype(jnp.float32))
    summed = (near_part + far_part).reshape(NRHS, NPTS)
    return jnp.zeros((NRHS, NPTS), jnp.float32).at[:, tree_order].set(summed)
```

```python
import functools

import jax
import jax.numpy as jnp
from jax import lax
from jax.experimental import pallas as pl
from jax.experimental.pallas import tpu as pltpu
from jax.sharding import PartitionSpec as P

LEVELS = 6
REACH = 8
BF = jnp.bfloat16
F32 = jnp.float32
NT = (((1,), (1,)), ((), ()))
NN = (((1,), (0,)), ((), ()))


def iota(shape, axis):
    return lax.broadcasted_iota(jnp.int32, shape, axis)


def dot(a, b, dims):
    return lax.dot_general(a, b, dims, preferred_element_type=F32)


def gather_lanes(src_ref, lo, hi):
    rows, points = src_ref.shape
    lo = jnp.broadcast_to(lo, (8, 128))
    hi = jnp.broadcast_to(hi, (8, 128))
    picked = [jnp.zeros((8, 128), F32) for _ in range(rows // 8)]
    for chunk in range(points // 128):
        here = hi == chunk
        for r in range(rows // 8):
            values = src_ref[pl.ds(r * 8, 8), pl.ds(chunk * 128, 128)]
            moved = jnp.take_along_axis(values, lo, axis=1, mode="promise_in_bounds")
            picked[r] = jnp.where(here, moved, picked[r])
    return jnp.concatenate(picked, axis=0)


def pad_lanes(x):
    short = 128 - x.shape[1]
    return jnp.concatenate([x, jnp.zeros((x.shape[0], short), x.dtype)], axis=1)


def up_kernel(
    vec_ref, order_ref, basis_ref, transfer_ref,
    ordered_ref, left_ref, right_ref, top_ref, weights_ref, masked_ref,
    vec32, rows32,
):
    columns, points = vec_ref.shape
    rank = basis_ref.shape[0]
    halo = left_ref.shape[1] - 4096
    vec32[...] = vec_ref[...].astype(F32)

    def permute(j, carry):
        ids = lax.rem(order_ref[pl.ds(j, 1), :], points)
        picked = gather_lanes(vec32, ids & 127, ids >> 7)
        ordered_ref[:, pl.ds(pl.multiple_of(j * 128, 128), 128)] = picked.astype(BF)
        return carry

    lax.fori_loop(0, points // 128, permute, 0)

    def relayout(a, carry):
        one = transfer_ref[pl.ds(pl.multiple_of(a * rank, rank), rank), :].astype(F32)
        four = pad_lanes(jnp.concatenate([one] * 4, axis=0))
        rows32[pl.ds(a, 128, stride=rank), :] = four.T
        return carry

    lax.fori_loop(0, rank, relayout, 0)
    mine = (iota((256, 128), 0) >> 6) == (iota((256, 128), 1) >> 5)
    mine_leaf = (iota((128, 256), 0) >> 5) == (iota((128, 256), 1) >> 6)
    coeffs = [None] * 32
    for g in range(16):
        weights_ref[g] = jnp.where(mine, rows32[pl.ds(g * 256, 256), :], 0.0).astype(BF)
        one = basis_ref[:, pl.ds(g * 256, 256)].astype(F32)
        masked = jnp.where(mine_leaf, jnp.concatenate([one] * 4, axis=0), 0.0).astype(BF)
        masked_ref[g] = masked
        coeffs[g] = dot(ordered_ref[:, pl.ds(g * 256, 256)], masked, NT).astype(BF)
    for k in range(15):
        pair = jnp.concatenate([coeffs[2 * k], coeffs[2 * k + 1]], axis=1)
        coeffs[16 + k] = dot(pair, weights_ref[k], NN).astype(BF)
    coeffs[31] = dot(coeffs[30], weights_ref[15, :128, :], NN).astype(BF)
    top_ref[0] = dot(coeffs[31], weights_ref[15, 128:, :], NN).astype(BF)
    for g in range(32):
        left_ref[:, pl.ds(halo + g * 128, 128)] = coeffs[g]
        right_ref[:, pl.ds(halo + g * 128, 128)] = coeffs[g]
    left_ref[:, :halo] = ordered_ref[:, :halo]
    right_ref[:, :halo] = ordered_ref[:, points - halo :]


def near_group(leaves_ref, lists_ref, blocks, first, base, columns):
    lane_left = iota((columns, 128), 1) < 64
    picked = []
    for i in range(4):
        spots = [lists_ref[s, first + i] - base for s in range(4)]
        halves = []
        for s in (0, 2):
            even = leaves_ref[spots[s]].astype(F32)
            odd = leaves_ref[spots[s + 1] ^ 1].astype(F32)
            halves.append(jnp.where(lane_left, even, odd))
        picked.append(jnp.concatenate(halves, axis=1))
    moving = jnp.concatenate(picked, axis=0).astype(BF)
    out = dot(moving, blocks, NT)
    leaf_of_lane = iota((columns, 256), 1) >> 6
    total = jnp.where(leaf_of_lane == 0, out[:columns], 0.0)
    for i in range(1, 4):
        total = jnp.where(leaf_of_lane == i, out[i * columns : (i + 1) * columns], total)
    return total


def place_leaves(leaves_ref, first, chunk):
    leaves_ref[first] = chunk
    leaves_ref[first + 1] = pltpu.roll(chunk.astype(F32), 64, 1).astype(BF)


def inner_kernel(
    ordered_ref, blocks_ref, near_ref, order_ref, coupling_ref, lists_ref, weights_ref, masked_ref,
    near_out, matrices_ref, spots_ref, inverse_ref, reach_ref,
    leaves, rows32, wide,
):
    columns, points = ordered_ref.shape
    rank = 32
    count = blocks_ref.shape[0]
    device = lax.axis_index("leaf")

    def invert(j, total):
        ids = lax.rem(order_ref[pl.ds(j, 1), :], points)
        high, low = ids >> 7, ids & 127
        lane = iota((32, 128), 1).astype(F32)
        hit = iota((32, 128), 0) == jnp.broadcast_to(high, (32, 128))
        block = jnp.where(hit, j.astype(F32), 0.0)
        within = jnp.where(hit, lane, 0.0)
        left = jnp.concatenate([block, within], axis=0).astype(BF)
        right = jnp.where(iota((128, 128), 0) == jnp.broadcast_to(low, (128, 128)), 1.0, 0.0).astype(BF)
        return total + dot(left, right, NT)

    inverse_ref[...] = lax.fori_loop(
        0, points // 128, invert, jnp.zeros((64, 128), F32)
    ).astype(jnp.int32)

    node = iota((1, 128), 1)
    size = jnp.full((1, 128), count, jnp.int32)
    start = jnp.zeros((1, 128), jnp.int32)
    offset = 0
    for level in range(LEVELS):
        size = jnp.where(node >= offset, count >> level, size)
        start = jnp.where(node >= offset, offset, start)
        offset += count >> level
    entries = pad_lanes(lists_ref[...])
    for s in range(6):
        entry = entries[s : s + 1]
        place = entry - device * size + size
        side = jnp.where(place >= size, 1, 0) + jnp.where(place >= 2 * size, 1, 0)
        spot = side * 128 + start + place - side * size
        spot = (spot & ~3) | ((spot - s) & 3)
        used = (entry >= 0) & (node < offset)
        spots_ref[pl.ds(s, 1), :] = jnp.where(used, spot, 3 * 128)
    spots_ref[pl.ds(6, 2), :] = jnp.zeros((2, 128), jnp.int32)

    def relayout(a, carry):
        at = pl.multiple_of(a * rank, rank)
        one = [coupling_ref[s, pl.ds(at, rank), :].astype(F32) for s in range(6)]
        full = jnp.concatenate(one + [jnp.zeros_like(one[0])] * 2, axis=0)
        turned = pad_lanes(full).T
        rows32[pl.ds(a, 128, stride=rank), :] = turned[:, :128]
        wide[pl.ds(a, 128, stride=rank), :] = turned[:, 128:]
        return carry

    lax.fori_loop(0, rank, relayout, 0)

    def narrow(g, carry):
        at = pl.multiple_of(g * 128, 128)
        both = jnp.concatenate([rows32[pl.ds(at, 128), :], wide[pl.ds(at, 128), :]], axis=1)
        matrices_ref[g] = both.astype(BF)
        return carry

    lax.fori_loop(0, 32, narrow, 0)

    def place(c, carry):
        chunk = ordered_ref[:, pl.ds(pl.multiple_of(c * 128, 128), 128)]
        place_leaves(leaves, c * 2, chunk)
        return carry

    lax.fori_loop(0, count // 2, place, 0)
    edge = REACH // 4
    near_out[:, : edge * 256] = jnp.zeros((columns, edge * 256), F32)
    near_out[:, points - edge * 256 :] = jnp.zeros((columns, edge * 256), F32)

    def near(g, carry):
        blocks = blocks_ref[pl.ds(g * 4, 4)].reshape(256, 256)
        at = pl.multiple_of(g * 256, 256)
        near_out[:, pl.ds(at, 256)] = near_group(
            leaves, near_ref, blocks, g * 4, device * count, columns
        )
        return carry

    lax.fori_loop(edge, count // 4 - edge, near, 0)

    unit = jnp.where(iota((rank, 128), 1) == iota((rank, 128), 0) + 64, 1.0, 0.0).astype(BF)
    down = [None] * 32
    down[31] = dot(unit, weights_ref[15, 128:, :], NT).astype(BF)
    down[30] = dot(down[31], weights_ref[15, :128, :], NT).astype(BF)
    for k in reversed(range(15)):
        pair = dot(down[16 + k], weights_ref[k], NT).astype(BF)
        down[2 * k], down[2 * k + 1] = pair[:, :128], pair[:, 128:]
    for g in range(16):
        at_points = dot(down[g], masked_ref[g], NN)
        reach_ref[:, pl.ds(g * 256, 256)] = at_points.astype(BF)


def outer_kernel(
    ordered_ref, own_ref, before_ref, after_ref, near_in, blocks_ref, near_ref, matrices_ref,
    spots_ref, inverse_ref, weights_ref, masked_ref, reach_ref,
    partial_ref, reach_out,
    leaves, nodes, far, summed, edges, sems,
):
    columns, points = ordered_ref.shape
    halo = before_ref.shape[1] - 4096
    device = lax.axis_index("leaf")
    count = points // 64
    copies = [
        pltpu.make_async_copy(blocks_ref.at[pl.ds(at, REACH)], edges.at[i], sems.at[i])
        for i, at in enumerate((0, count - REACH))
    ]
    for copy in copies:
        copy.start()

    for c in range(halo // 128):
        place_leaves(leaves, c * 2, before_ref[:, pl.ds(c * 128, 128)])
        place_leaves(leaves, REACH + count + c * 2, after_ref[:, pl.ds(c * 128, 128)])

    def place(c, carry):
        chunk = ordered_ref[:, pl.ds(pl.multiple_of(c * 128, 128), 128)]
        place_leaves(leaves, REACH + c * 2, chunk)
        return carry

    lax.fori_loop(0, count // 2, place, 0)

    nodes[pl.ds(384, 4)] = jnp.zeros((4, columns, 128), BF)
    for side, ref in enumerate((before_ref, own_ref, after_ref)):

        def turn(g, carry, side=side, ref=ref):
            chunk = ref[:, pl.ds(pl.multiple_of(halo + g * 128, 128), 128)].astype(F32)
            for r in range(4):
                turned = chunk if r == 0 else pltpu.roll(chunk, 128 - 32 * r, 1)
                nodes[side * 128 + g * 4 + r] = turned.astype(BF)
            return carry

        lax.fori_loop(0, 32, turn, 0)

    lane_group = iota((columns, 128), 1) >> 5

    def couple(g, carry):
        picked = []
        for i in range(4):
            parts = [nodes[spots_ref[s, g * 4 + i]].astype(F32) for s in range(6)]
            front = parts[0]
            for s in range(1, 4):
                front = jnp.where(lane_group == s, parts[s], front)
            back = jnp.where(lane_group == 1, parts[5], parts[4])
            back = jnp.where(lane_group < 2, back, 0.0)
            picked.append(jnp.concatenate([front, back], axis=1))
        out = dot(jnp.concatenate(picked, axis=0).astype(BF), matrices_ref[g], NT)
        total = out[:columns]
        for i in range(1, 4):
            total = jnp.where(lane_group == i, out[i * columns : (i + 1) * columns], total)
        far[:, pl.ds(pl.multiple_of(g * 128, 128), 128)] = total
        return carry

    lax.fori_loop(0, 32, couple, 0)

    for copy in copies:
        copy.wait()
    down = [None] * 32
    down[31] = far[:, pl.ds(31 * 128, 128)].astype(BF)
    down[30] = (far[:, pl.ds(30 * 128, 128)] + dot(down[31], weights_ref[15, :128, :], NT)).astype(BF)
    for k in reversed(range(15)):
        pair = far[:, pl.ds(k * 256, 256)] + dot(down[16 + k], weights_ref[k], NT)
        pair = pair.astype(BF)
        down[2 * k], down[2 * k + 1] = pair[:, :128], pair[:, 128:]
    groups = count // 4
    for g in range(groups):
        total = dot(down[g], masked_ref[g], NN)
        if g < REACH // 4 or g >= groups - REACH // 4:
            if g < REACH // 4:
                blocks = edges[0, pl.ds(g * 4, 4)].reshape(256, 256)
            else:
                blocks = edges[1, pl.ds((g - groups) * 4 + REACH, 4)].reshape(256, 256)
            total = total + near_group(leaves, near_ref, blocks, g * 4, device * count - REACH, columns)
        else:
            total = total + near_in[:, pl.ds(g * 256, 256)]
        summed[:columns, pl.ds(g * 256, 256)] = total
        summed[columns:, pl.ds(g * 256, 256)] = reach_ref[:, pl.ds(g * 256, 256)].astype(F32)

    def restore(j, carry):
        high = inverse_ref[pl.ds(j, 1), :]
        low = inverse_ref[pl.ds(j + 32, 1), :]
        picked = gather_lanes(summed, low, high)
        at = pl.ds(pl.multiple_of(j * 128, 128), 128)
        partial_ref[:, at] = picked[:columns]
        reach_out[:, at] = picked[columns:].astype(BF)
        return carry

    lax.fori_loop(0, points // 128, restore, 0)


def top_kernel(
    gathered_ref, transfer_ref, coupling_ref, lists_ref, partial_ref, reach_ref, out_ref, coeffs,
):
    node_count = gathered_ref.shape[0]
    columns = gathered_ref.shape[1]
    device = lax.axis_index("leaf")
    total = 2 * node_count - 1
    for q in range(node_count):
        coeffs[q ^ device] = gathered_ref[q][:, 64:96].astype(F32)
    start, count = 0, node_count
    while count > 1:
        for j in range(count // 2):
            lifted = dot(coeffs[start + 2 * j].astype(BF), transfer_ref[start + 2 * j], NN)
            lifted += dot(coeffs[start + 2 * j + 1].astype(BF), transfer_ref[start + 2 * j + 1], NN)
            coeffs[start + count + j] = lifted.astype(BF).astype(F32)
        start, count = start + count, count // 2
    coeffs[total] = jnp.zeros((columns, 32), F32)
    starts, start, count = [], 0, node_count
    while count >= 1:
        starts.append((start, count))
        start, count = start + count, count // 2
    down = None
    for level, (start, count) in reversed(list(enumerate(starts))):
        node = start + (device >> level)
        field = None
        for s in range(6):
            entry = lists_ref[s, node]
            spot = jnp.where(entry >= 0, start + entry, total)
            term = dot(coeffs[spot].astype(BF), coupling_ref[s, node], NT)
            field = term if field is None else field + term
        if down is not None:
            field = field + dot(down, transfer_ref[node], NT)
        down = field.astype(BF)

    points = out_ref.shape[1]
    for c in range(points // 512):
        at = pl.ds(c * 512, 512)
        out_ref[:, at] = partial_ref[:, at] + dot(down, reach_ref[:, at], NN)


VMEM = pl.BlockSpec(memory_space=pltpu.VMEM)
SMEM = pl.BlockSpec(memory_space=pltpu.SMEM)


def call(kernel, outs, scratch, specs, flops, name, args, out_specs=None):
    size = sum(a.size * a.dtype.itemsize for a in args)
    return pl.pallas_call(
        kernel,
        out_shape=[jax.ShapeDtypeStruct(s, t) for s, t in outs],
        in_specs=specs,
        out_specs=[VMEM] * len(outs) if out_specs is None else out_specs,
        scratch_shapes=scratch,
        compiler_params=pltpu.CompilerParams(vmem_limit_bytes=36 * 2**20),
        cost_estimate=pl.CostEstimate(flops=flops, bytes_accessed=size, transcendentals=0),
        name=name,
    )(*args)


def local(
    vectors, tree_order, leaf_basis, near_blocks, near_lists, transfers, couplings, coupling_lists,
    top_transfers, top_couplings, top_lists,
):
    columns, points = vectors.shape
    rank = leaf_basis.shape[0]
    devices = lax.axis_size("leaf")
    halo = REACH * near_blocks.shape[1]
    packed = halo + 128 * rank
    order = tree_order.reshape(points // 128, 128)
    near_t = jnp.transpose(near_lists)
    lists_t = jnp.transpose(coupling_lists)
    moves = transfers.reshape(rank * rank, -1)
    matrices = couplings.reshape(6, rank * rank, -1)

    ordered, to_left, to_right, top, weights, masked = call(
        up_kernel,
        [
            ((columns, points), BF), ((columns, packed), BF), ((columns, packed), BF),
            ((1, columns, 128), BF), ((16, 256, 128), BF), ((16, 128, 256), BF),
        ],
        [pltpu.VMEM((columns, points), F32), pltpu.VMEM((128 * rank, 128), F32)],
        [VMEM] * 4, 10**9, "up", (vectors, order, leaf_basis, moves),
    )
    reached = 1
    gathered = top
    while reached < devices:
        swap = [(i, i ^ reached) for i in range(devices)]
        gathered = jnp.concatenate([gathered, lax.ppermute(gathered, "leaf", swap)], axis=0)
        reached *= 2
    upward = [(i, i + 1) for i in range(devices - 1)]
    before = lax.ppermute(to_right, "leaf", upward)
    after = lax.ppermute(to_left, "leaf", [(j, i) for i, j in upward])

    near_part, coupling_rows, spots, inverse, reach = call(
        inner_kernel,
        [
            ((columns, points), F32), ((32, 128, 256), BF), ((8, 128), jnp.int32),
            ((64, 128), jnp.int32), ((rank, points), BF),
        ],
        [
            pltpu.VMEM((points // 64, columns, 128), BF), pltpu.VMEM((128 * rank, 128), F32),
            pltpu.VMEM((128 * rank, 128), F32),
        ],
        [VMEM, VMEM, SMEM, VMEM, VMEM, VMEM, VMEM, VMEM], 6 * 10**9, "inner",
        (ordered, near_blocks, near_t, order, matrices, lists_t, weights, masked),
    )
    partial, reach_back = call(
        outer_kernel,
        [((columns, points), F32), ((rank, points), BF)],
        [
            pltpu.VMEM((points // 64 + 2 * REACH, columns, 128), BF),
            pltpu.VMEM((388, columns, 128), BF), pltpu.VMEM((columns, 4096), F32),
            pltpu.VMEM((columns + rank, points), F32),
            pltpu.VMEM((2, REACH) + near_blocks.shape[1:], BF), pltpu.SemaphoreType.DMA((2,)),
        ],
        [
            VMEM, VMEM, VMEM, VMEM, VMEM,
            pl.BlockSpec(memory_space=pl.ANY), SMEM, VMEM, SMEM, VMEM, VMEM, VMEM, VMEM,
        ], 4 * 10**9, "outer",
        (
            ordered, to_left, before, after, near_part, near_blocks, near_t, coupling_rows,
            spots, inverse, weights, masked, reach,
        ),
    )
    (applied,) = call(
        top_kernel,
        [((columns, points), F32)],
        [pltpu.VMEM((2 * devices, columns, 32), F32)],
        [VMEM, VMEM, VMEM, SMEM, VMEM, VMEM], 10**9, "top",
        (
            gathered, jnp.transpose(top_transfers, (2, 0, 1)), jnp.transpose(top_couplings, (0, 3, 1, 2)),
            jnp.transpose(top_lists), partial, reach_back,
        ),
    )
    return applied


def solution(mesh):
    placed = (
        P("rhs", ("groups", "leaf")),
        P(("groups", "leaf")),
        P(None, ("groups", "leaf")),
        P(("groups", "leaf"), None, None),
        P(("groups", "leaf"), None),
        P(None, None, ("groups", "leaf")),
        P(None, None, None, ("groups", "leaf")),
        P(("groups", "leaf"), None),
        P(None, None, "groups"),
        P(None, None, None, "groups"),
        P("groups", None),
    )
    return jax.shard_map(
        local, mesh=mesh, in_specs=placed, out_specs=P("rhs", ("groups", "leaf")), check_vma=False
    )
```

```python
import functools

import jax
import jax.numpy as jnp
from jax import lax
from jax.experimental import pallas as pl
from jax.experimental.pallas import tpu as pltpu
from jax.sharding import PartitionSpec as P

LEVELS = 6
REACH = 8
BF = jnp.bfloat16
F32 = jnp.float32
NT = (((1,), (1,)), ((), ()))
NN = (((1,), (0,)), ((), ()))


def iota(shape, axis):
    return lax.broadcasted_iota(jnp.int32, shape, axis)


def dot(a, b, dims):
    return lax.dot_general(a, b, dims, preferred_element_type=F32)


def pad_lanes(x):
    short = 128 - x.shape[1]
    return jnp.concatenate([x, jnp.zeros((x.shape[0], short), x.dtype)], axis=1)


def one_hot(ids):
    return jnp.where(iota((256, 256), 0) == jnp.broadcast_to(ids, (256, 256)), 1.0, 0.0).astype(BF)


def pick(stacked, hot, high, rows):
    out = dot(stacked, hot, NN)
    high = jnp.broadcast_to(high, (rows, 256))
    total = out[:rows]
    for block in range(1, stacked.shape[0] // rows):
        total = jnp.where(high == block, out[block * rows : (block + 1) * rows], total)
    return total


def up_kernel(
    vec_hbm, order_hbm, basis_hbm, transfer_hbm,
    ordered_ref, left_ref, right_ref, top_ref, weights_ref, masked_ref, inverse_ref,
    vec_ref, order_ref, basis_ref, transfer_ref, stacked, rows32, sems,
):
    columns, points = vec_ref.shape
    rank = basis_ref.shape[0]
    chunks = points // 256
    halo = left_ref.shape[1] - 4096
    pairs = (
        (transfer_hbm, transfer_ref), (order_hbm, order_ref), (vec_hbm, vec_ref), (basis_hbm, basis_ref),
    )
    copies = [pltpu.make_async_copy(src, dst, sems.at[i]) for i, (src, dst) in enumerate(pairs)]
    for copy in copies:
        copy.start()

    copies[0].wait()
    lane, row = iota((128, 256), 1), iota((128, 256), 0)
    family = (lane & 7) == ((row >> 1) & 7)
    spread = [
        jnp.where(iota((128, 256), 0) == (iota((128, 256), 1) >> 3) + 32 * q, 1.0, 0.0).astype(BF)
        for q in range(4)
    ]
    for m in range(rank // 4):
        turned = pad_lanes(transfer_ref[pl.ds(m * 4 * rank, 4 * rank), :].astype(F32)).T.astype(BF)
        for q in range(4):
            rows32[m * 4 + q] = jnp.where(family, dot(turned, spread[q], NN), 0.0)
    for k in range(16):
        weights_ref[k] = rows32[:, k * 8 : k * 8 + 8, :].reshape(256, 256).astype(BF)

    copies[1].wait()
    copies[2].wait()
    for block in range(chunks):
        stacked[block * columns : (block + 1) * columns, :] = vec_ref[:, block * 256 : (block + 1) * 256]
    within = iota((16, 256), 1).astype(F32)
    inverse = jnp.zeros((32, 256), F32)
    for c in range(chunks):
        ids = jnp.concatenate([order_ref[2 * c : 2 * c + 1, :], order_ref[2 * c + 1 : 2 * c + 2, :]], axis=1)
        ids = lax.rem(ids, points)
        high, low = ids >> 8, ids & 255
        hot = one_hot(low)
        ordered_ref[:, c * 256 : (c + 1) * 256] = pick(stacked[...], hot, high, columns).astype(BF)
        hit = iota((16, 256), 0) == jnp.broadcast_to(high, (16, 256))
        marks = jnp.concatenate([jnp.where(hit, float(c), 0.0), jnp.where(hit, within, 0.0)], axis=0)
        inverse = inverse + dot(marks.astype(BF), hot, NT)
    inverse_ref[...] = inverse.astype(jnp.int32)

    copies[3].wait()
    mine = (iota((256, 512), 0) & 7) == (iota((256, 512), 1) >> 6)
    coeffs = [None] * 16
    for g in range(points // 512):
        one = basis_ref[:, g * 512 : (g + 1) * 512].astype(F32)
        eight = jnp.broadcast_to(one[:, None, :], (rank, 8, 512)).reshape(256, 512)
        masked = jnp.where(mine, eight, 0.0).astype(BF)
        masked_ref[g] = masked
        coeffs[g] = dot(ordered_ref[:, g * 512 : (g + 1) * 512], masked, NT).astype(BF)
    for n in range(7):
        lifted = dot(coeffs[2 * n], weights_ref[2 * n], NN) + dot(coeffs[2 * n + 1], weights_ref[2 * n + 1], NN)
        coeffs[8 + n] = lifted.astype(BF)
    four = dot(coeffs[14], weights_ref[14], NN)
    five = dot(four.astype(BF), weights_ref[15], NN)
    six = dot((four + five).astype(BF), weights_ref[15], NN)
    coeffs[15] = (four + six).astype(BF)
    root = jnp.where(iota((256, 128), 0) == iota((256, 128), 1) * 8 + 6, 1.0, 0.0).astype(BF)
    top_ref[0] = dot(coeffs[15], root, NN).astype(BF)
    for g in range(16):
        left_ref[:, halo + g * 256 : halo + (g + 1) * 256] = coeffs[g]
        right_ref[:, halo + g * 256 : halo + (g + 1) * 256] = coeffs[g]
    left_ref[:, :halo] = ordered_ref[:, :halo]
    right_ref[:, :halo] = ordered_ref[:, points - halo :]


def near_group(leaves_ref, lists_ref, blocks, first, base, columns):
    lane_left = iota((columns, 128), 1) < 64
    picked = []
    for i in range(4):
        spots = [lists_ref[s, first + i] - base for s in range(4)]
        halves = []
        for s in (0, 2):
            even = leaves_ref[spots[s]]
            odd = leaves_ref[spots[s + 1] ^ 1]
            halves.append(jnp.where(lane_left, even, odd))
        picked.append(jnp.concatenate(halves, axis=1))
    moving = jnp.concatenate(picked, axis=0).astype(BF)
    out = dot(moving, blocks, NT)
    leaf_of_lane = iota((columns, 256), 1) >> 6
    total = out[:columns]
    for i in range(1, 4):
        total = jnp.where(leaf_of_lane == i, out[i * columns : (i + 1) * columns], total)
    return total


def place_leaves(leaves_ref, first, chunk):
    chunk = chunk.astype(F32)
    leaves_ref[first] = chunk
    leaves_ref[first + 1] = pltpu.roll(chunk, 64, 1)


def inner_kernel(
    ordered_ref, blocks_ref, near_ref, coupling_ref, lists_ref, weights_ref, masked_ref, inverse_ref,
    near_out, matrices_ref, spots_ref, hot_ref, reach_ref,
    leaves, rows32, stacked,
):
    columns, points = ordered_ref.shape
    rank = 32
    count = blocks_ref.shape[0]
    device = lax.axis_index("leaf")

    node = iota((1, 128), 1)
    size = jnp.full((1, 128), count, jnp.int32)
    start = jnp.zeros((1, 128), jnp.int32)
    offset = 0
    for level in range(LEVELS):
        size = jnp.where(node >= offset, count >> level, size)
        start = jnp.where(node >= offset, offset, start)
        offset += count >> level
    entries = pad_lanes(lists_ref[...])
    for s in range(6):
        entry = entries[s : s + 1]
        place = entry - device * size + size
        side = jnp.where(place >= size, 1, 0) + jnp.where(place >= 2 * size, 1, 0)
        spot = side * 128 + start + place - side * size
        used = (entry >= 0) & (node < offset)
        spots_ref[pl.ds(s, 1), :] = jnp.where(used, spot, 3 * 128)
    spots_ref[pl.ds(6, 2), :] = jnp.zeros((2, 128), jnp.int32)

    def relayout(a, carry):
        at = pl.multiple_of(a * rank, rank)
        one = [coupling_ref[s, pl.ds(at, rank), :].astype(F32) for s in range(6)]
        full = jnp.concatenate(one + [jnp.zeros_like(one[0])] * 2, axis=0)
        rows32[a] = pad_lanes(full).T
        return carry

    lax.fori_loop(0, rank, relayout, 0)

    def narrow(g, carry):
        at = pl.multiple_of(g * 8, 8)
        matrices_ref[g] = rows32[:, pl.ds(at, 8), :].reshape(256, 256).astype(BF)
        return carry

    lax.fori_loop(0, 16, narrow, 0)

    def place(c, carry):
        chunk = ordered_ref[:, pl.ds(pl.multiple_of(c * 128, 128), 128)]
        place_leaves(leaves, c * 2, chunk)
        return carry

    lax.fori_loop(0, count // 2, place, 0)
    edge = REACH // 4
    near_out[:, : edge * 256] = jnp.zeros((columns, edge * 256), F32)
    near_out[:, points - edge * 256 :] = jnp.zeros((columns, edge * 256), F32)

    def near(g, carry):
        blocks = blocks_ref[pl.ds(g * 4, 4)].reshape(256, 256)
        at = pl.multiple_of(g * 256, 256)
        near_out[:, pl.ds(at, 256)] = near_group(
            leaves, near_ref, blocks, g * 4, device * count, columns
        )
        return carry

    lax.fori_loop(edge, count // 4 - edge, near, 0)

    unit = jnp.where(iota((rank, 256), 1) == iota((rank, 256), 0) * 8 + 6, 1.0, 0.0)
    five = dot(unit.astype(BF), weights_ref[15], NT)
    down = [None] * 16
    down[15] = dot((unit + five).astype(BF), weights_ref[15], NT).astype(BF)
    for k in reversed(range(15)):
        down[k] = dot(down[8 + k // 2], weights_ref[k], NT).astype(BF)
    for g in range(points // 512):
        at_points = dot(down[g], masked_ref[g], NN).astype(BF)
        stacked[2 * g * rank : (2 * g + 1) * rank, :] = at_points[:, :256]
        stacked[(2 * g + 1) * rank : (2 * g + 2) * rank, :] = at_points[:, 256:]
    for c in range(points // 256):
        hot = one_hot(inverse_ref[16 + c : 17 + c, :])
        hot_ref[c] = hot
        reach_ref[:, c * 256 : (c + 1) * 256] = pick(
            stacked[...], hot, inverse_ref[c : c + 1, :], rank
        ).astype(BF)


def outer_kernel(
    ordered_ref, own_ref, before_ref, after_ref, near_in, blocks_ref, near_ref, matrices_ref,
    spots_ref, inverse_ref, weights_ref, masked_ref, hot_ref,
    partial_ref,
    leaves, nodes, far, stacked, stacked_nodes, edges, sems,
):
    columns, points = ordered_ref.shape
    halo = before_ref.shape[1] - 4096
    device = lax.axis_index("leaf")
    count = points // 64
    copies = [
        pltpu.make_async_copy(blocks_ref.at[pl.ds(at, REACH)], edges.at[i], sems.at[i])
        for i, at in enumerate((0, count - REACH))
    ]
    for copy in copies:
        copy.start()

    for c in range(halo // 128):
        place_leaves(leaves, c * 2, before_ref[:, pl.ds(c * 128, 128)])
        place_leaves(leaves, REACH + count + c * 2, after_ref[:, pl.ds(c * 128, 128)])

    def place(c, carry):
        chunk = ordered_ref[:, pl.ds(pl.multiple_of(c * 128, 128), 128)]
        place_leaves(leaves, REACH + c * 2, chunk)
        return carry

    lax.fori_loop(0, count // 2, place, 0)

    nodes[3 * 128] = jnp.zeros((columns, 128), F32)
    lane, row = iota((256, 1024), 1), iota((256, 1024), 0)
    spread = jnp.where(row == (lane & 31) * 8 + (lane >> 7), 1.0, 0.0).astype(BF)
    for side, ref in enumerate((before_ref, own_ref, after_ref)):
        for n in range(16):
            stacked_nodes[n * columns : (n + 1) * columns, :] = ref[:, halo + n * 256 : halo + (n + 1) * 256]
        for c in range(0, 8, 2):
            out = dot(stacked_nodes[...], spread[:, c * 128 : (c + 2) * 128], NN)
            for n in range(16):
                both = out[n * columns : (n + 1) * columns]
                nodes[side * 128 + n * 8 + c] = both[:, :128]
                nodes[side * 128 + n * 8 + c + 1] = both[:, 128:]

    lane_group = iota((columns, 128), 1) >> 5
    lane_node = iota((columns, 256), 1) & 7

    def couple(g, carry):
        picked = []
        for i in range(8):
            parts = [nodes[spots_ref[s, g * 8 + i]] for s in range(6)]
            front = parts[0]
            for s in range(1, 4):
                front = jnp.where(lane_group == s, parts[s], front)
            back = jnp.where(lane_group == 1, parts[5], parts[4])
            back = jnp.where(lane_group < 2, back, 0.0)
            picked.append(jnp.concatenate([front, back], axis=1))
        out = dot(jnp.concatenate(picked, axis=0).astype(BF), matrices_ref[g], NT)
        total = out[:columns]
        for i in range(1, 8):
            total = jnp.where(lane_node == i, out[i * columns : (i + 1) * columns], total)
        far[:, pl.ds(pl.multiple_of(g * 256, 256), 256)] = total
        return carry

    lax.fori_loop(0, 16, couple, 0)

    for copy in copies:
        copy.wait()
    down = [None] * 16
    last = far[:, 15 * 256 :]
    five = jnp.where(lane_node >= 4, last, 0.0).astype(BF)
    down[15] = (last + dot(five, weights_ref[15], NT)).astype(BF)
    for k in reversed(range(15)):
        down[k] = (far[:, k * 256 : (k + 1) * 256] + dot(down[8 + k // 2], weights_ref[k], NT)).astype(BF)
    groups = count // 4
    edge = REACH // 4
    for g in range(groups):
        if g < edge:
            blocks = edges[0, g * 4 : g * 4 + 4].reshape(256, 256)
        elif g >= groups - edge:
            at = (g - groups + edge) * 4
            blocks = edges[1, at : at + 4].reshape(256, 256)
        else:
            blocks = None
        if blocks is None:
            near = near_in[:, g * 256 : (g + 1) * 256]
        else:
            near = near_group(leaves, near_ref, blocks, g * 4, device * count - REACH, columns)
        if g % 2 == 0:
            at_points = dot(down[g // 2], masked_ref[g // 2], NN)
        half = at_points[:, g % 2 * 256 : (g % 2 + 1) * 256]
        stacked[g * columns : (g + 1) * columns, :] = (near + half).astype(BF)

    for c in range(points // 256):
        partial_ref[:, c * 256 : (c + 1) * 256] = pick(
            stacked[...], hot_ref[c], inverse_ref[c : c + 1, :], columns
        )


def top_kernel(
    gathered_ref, transfer_ref, coupling_ref, lists_ref, partial_ref, reach_ref, out_ref, coeffs,
):
    node_count = gathered_ref.shape[0]
    columns = gathered_ref.shape[1]
    device = lax.axis_index("leaf")
    total = 2 * node_count - 1
    for q in range(node_count):
        coeffs[q ^ device] = gathered_ref[q][:, :32].astype(F32)
    start, count = 0, node_count
    while count > 1:
        for j in range(count // 2):
            lifted = dot(coeffs[start + 2 * j].astype(BF), transfer_ref[start + 2 * j], NN)
            lifted += dot(coeffs[start + 2 * j + 1].astype(BF), transfer_ref[start + 2 * j + 1], NN)
            coeffs[start + count + j] = lifted.astype(BF).astype(F32)
        start, count = start + count, count // 2
    coeffs[total] = jnp.zeros((columns, 32), F32)
    starts, start, count = [], 0, node_count
    while count >= 1:
        starts.append((start, count))
        start, count = start + count, count // 2
    down = None
    for level, (start, count) in reversed(list(enumerate(starts))):
        node = start + (device >> level)
        field = None
        for s in range(6):
            entry = lists_ref[s, node]
            spot = jnp.where(entry >= 0, start + entry, total)
            term = dot(coeffs[spot].astype(BF), coupling_ref[s, node], NT)
            field = term if field is None else field + term
        if down is not None:
            field = field + dot(down, transfer_ref[node], NT)
        down = field.astype(BF)

    points = out_ref.shape[1]
    for c in range(points // 512):
        at = pl.ds(c * 512, 512)
        out_ref[:, at] = partial_ref[:, at] + dot(down, reach_ref[:, at], NN)


VMEM = pl.BlockSpec(memory_space=pltpu.VMEM)
SMEM = pl.BlockSpec(memory_space=pltpu.SMEM)


def call(kernel, outs, scratch, specs, flops, name, args, out_specs=None):
    size = sum(a.size * a.dtype.itemsize for a in args)
    return pl.pallas_call(
        kernel,
        out_shape=[jax.ShapeDtypeStruct(s, t) for s, t in outs],
        in_specs=specs,
        out_specs=[VMEM] * len(outs) if out_specs is None else out_specs,
        scratch_shapes=scratch,
        compiler_params=pltpu.CompilerParams(vmem_limit_bytes=36 * 2**20),
        cost_estimate=pl.CostEstimate(flops=flops, bytes_accessed=size, transcendentals=0),
        name=name,
    )(*args)


def local(
    vectors, tree_order, leaf_basis, near_blocks, near_lists, transfers, couplings, coupling_lists,
    top_transfers, top_couplings, top_lists,
):
    columns, points = vectors.shape
    rank = leaf_basis.shape[0]
    devices = lax.axis_size("leaf")
    halo = REACH * near_blocks.shape[1]
    packed = halo + 128 * rank
    order = tree_order.reshape(points // 128, 128)
    near_t = jnp.transpose(near_lists)
    lists_t = jnp.transpose(coupling_lists)
    moves = transfers.reshape(rank * rank, -1)
    matrices = couplings.reshape(6, rank * rank, -1)

    ordered, to_left, to_right, top, weights, masked, inverse = call(
        up_kernel,
        [
            ((columns, points), BF), ((columns, packed), BF), ((columns, packed), BF), ((1, columns, 128), BF),
            ((16, 256, 256), BF), ((points // 512, 256, 512), BF), ((32, 256), jnp.int32),
        ],
        [
            pltpu.VMEM(vectors.shape, BF), pltpu.VMEM(order.shape, jnp.int32),
            pltpu.VMEM(leaf_basis.shape, BF), pltpu.VMEM(moves.shape, BF),
            pltpu.VMEM((points // 256 * columns, 256), BF), pltpu.VMEM((rank, 128, 256), F32),
            pltpu.SemaphoreType.DMA((4,)),
        ],
        [pl.BlockSpec(memory_space=pl.ANY)] * 4, 10**9, "up", (vectors, order, leaf_basis, moves),
    )
    reached = 1
    gathered = top
    while reached < devices:
        swap = [(i, i ^ reached) for i in range(devices)]
        gathered = jnp.concatenate([gathered, lax.ppermute(gathered, "leaf", swap)], axis=0)
        reached *= 2
    upward = [(i, i + 1) for i in range(devices - 1)]
    before = lax.ppermute(to_right, "leaf", upward)
    after = lax.ppermute(to_left, "leaf", [(j, i) for i, j in upward])

    near_part, coupling_rows, spots, hot, reach = call(
        inner_kernel,
        [
            ((columns, points), F32), ((16, 256, 256), BF), ((8, 128), jnp.int32),
            ((points // 256, 256, 256), BF), ((rank, points), BF),
        ],
        [
            pltpu.VMEM((points // 64, columns, 128), F32), pltpu.VMEM((rank, 128, 256), F32),
            pltpu.VMEM((points // 256 * rank, 256), BF),
        ],
        [VMEM, VMEM, SMEM, VMEM, VMEM, VMEM, VMEM, VMEM], 6 * 10**9, "inner",
        (ordered, near_blocks, near_t, matrices, lists_t, weights, masked, inverse),
    )
    (partial,) = call(
        outer_kernel,
        [((columns, points), F32)],
        [
            pltpu.VMEM((points // 64 + 2 * REACH, columns, 128), F32),
            pltpu.VMEM((385, columns, 128), F32), pltpu.VMEM((columns, 4096), F32),
            pltpu.VMEM((points // 256 * columns, 256), BF), pltpu.VMEM((16 * columns, 256), BF),
            pltpu.VMEM((2, REACH) + near_blocks.shape[1:], BF), pltpu.SemaphoreType.DMA((2,)),
        ],
        [
            VMEM, VMEM, VMEM, VMEM, VMEM, pl.BlockSpec(memory_space=pl.ANY), SMEM, VMEM,
            SMEM, VMEM, VMEM, VMEM, VMEM,
        ], 4 * 10**9, "outer",
        (
            ordered, to_left, before, after, near_part, near_blocks, near_t, coupling_rows,
            spots, inverse, weights, masked, hot,
        ),
    )
    (applied,) = call(
        top_kernel,
        [((columns, points), F32)],
        [pltpu.VMEM((2 * devices, columns, 32), F32)],
        [VMEM, VMEM, VMEM, SMEM, VMEM, VMEM], 10**9, "top",
        (
            gathered, jnp.transpose(top_transfers, (2, 0, 1)), jnp.transpose(top_couplings, (0, 3, 1, 2)),
            jnp.transpose(top_lists), partial, reach,
        ),
    )
    return applied


def solution(mesh):
    placed = (
        P("rhs", ("groups", "leaf")),
        P(("groups", "leaf")),
        P(None, ("groups", "leaf")),
        P(("groups", "leaf"), None, None),
        P(("groups", "leaf"), None),
        P(None, None, ("groups", "leaf")),
        P(None, None, None, ("groups", "leaf")),
        P(("groups", "leaf"), None),
        P(None, None, "groups"),
        P(None, None, None, "groups"),
        P("groups", None),
    )
    return jax.shard_map(
        local, mesh=mesh, in_specs=placed, out_specs=P("rhs", ("groups", "leaf")), check_vma=False
    )
```

```python
import functools

import jax
import jax.numpy as jnp
from jax import lax
from jax.experimental import pallas as pl
from jax.experimental.pallas import tpu as pltpu
from jax.sharding import PartitionSpec as P

LEVELS = 6
REACH = 8
BF = jnp.bfloat16
F32 = jnp.float32
NT = (((1,), (1,)), ((), ()))
NN = (((1,), (0,)), ((), ()))


def iota(shape, axis):
    return lax.broadcasted_iota(jnp.int32, shape, axis)


def dot(a, b, dims):
    return lax.dot_general(a, b, dims, preferred_element_type=F32)


def pad_lanes(x):
    short = 128 - x.shape[1]
    return jnp.concatenate([x, jnp.zeros((x.shape[0], short), x.dtype)], axis=1)


def one_hot(ids):
    return jnp.where(iota((256, 256), 0) == jnp.broadcast_to(ids, (256, 256)), 1.0, 0.0).astype(BF)


def pick(stacked, hot, high, rows):
    out = dot(stacked, hot, NN)
    high = jnp.broadcast_to(high, (rows, 256))
    total = out[:rows]
    for block in range(1, stacked.shape[0] // rows):
        total = jnp.where(high == block, out[block * rows : (block + 1) * rows], total)
    return total


def up_kernel(
    vec_hbm, order_hbm, basis_hbm, transfer_hbm,
    ordered_ref, first_ref, second_ref, top_ref, weights_ref, masked_ref, inverse_ref,
    vec_ref, order_ref, basis_ref, transfer_ref, stacked, rows32, sems,
):
    columns, points = vec_ref.shape
    rank = basis_ref.shape[0]
    chunks = points // 256
    halo = first_ref.shape[1] - 4096
    odd = lax.axis_index("leaf") % 2 == 1
    pairs = (
        (transfer_hbm, transfer_ref), (order_hbm, order_ref), (vec_hbm, vec_ref), (basis_hbm, basis_ref),
    )
    copies = [pltpu.make_async_copy(src, dst, sems.at[i]) for i, (src, dst) in enumerate(pairs)]
    for copy in copies:
        copy.start()

    copies[0].wait()
    lane, row = iota((128, 256), 1), iota((128, 256), 0)
    family = (lane & 7) == ((row >> 1) & 7)
    spread = [
        jnp.where(iota((128, 256), 0) == (iota((128, 256), 1) >> 3) + 32 * q, 1.0, 0.0).astype(BF)
        for q in range(4)
    ]
    for m in range(rank // 4):
        turned = pad_lanes(transfer_ref[pl.ds(m * 4 * rank, 4 * rank), :].astype(F32)).T.astype(BF)
        for q in range(4):
            rows32[m * 4 + q] = jnp.where(family, dot(turned, spread[q], NN), 0.0)
    for k in range(16):
        weights_ref[k] = rows32[:, k * 8 : k * 8 + 8, :].reshape(256, 256).astype(BF)

    copies[1].wait()
    copies[2].wait()
    for block in range(chunks):
        stacked[block * columns : (block + 1) * columns, :] = vec_ref[:, block * 256 : (block + 1) * 256]
    within = iota((16, 256), 1).astype(F32)
    inverse = jnp.zeros((32, 256), F32)
    for c in range(chunks):
        ids = jnp.concatenate([order_ref[2 * c : 2 * c + 1, :], order_ref[2 * c + 1 : 2 * c + 2, :]], axis=1)
        ids = lax.rem(ids, points)
        high, low = ids >> 8, ids & 255
        hot = one_hot(low)
        ordered_ref[:, c * 256 : (c + 1) * 256] = pick(stacked[...], hot, high, columns).astype(BF)
        hit = iota((16, 256), 0) == jnp.broadcast_to(high, (16, 256))
        marks = jnp.concatenate([jnp.where(hit, float(c), 0.0), jnp.where(hit, within, 0.0)], axis=0)
        inverse = inverse + dot(marks.astype(BF), hot, NT)
    inverse_ref[...] = inverse.astype(jnp.int32)

    copies[3].wait()
    mine = (iota((256, 512), 0) & 7) == (iota((256, 512), 1) >> 6)
    coeffs = [None] * 16
    for g in range(points // 512):
        one = basis_ref[:, g * 512 : (g + 1) * 512].astype(F32)
        eight = jnp.broadcast_to(one[:, None, :], (rank, 8, 512)).reshape(256, 512)
        masked = jnp.where(mine, eight, 0.0).astype(BF)
        masked_ref[g] = masked
        coeffs[g] = dot(ordered_ref[:, g * 512 : (g + 1) * 512], masked, NT).astype(BF)
    for n in range(7):
        lifted = dot(coeffs[2 * n], weights_ref[2 * n], NN) + dot(coeffs[2 * n + 1], weights_ref[2 * n + 1], NN)
        coeffs[8 + n] = lifted.astype(BF)
    four = dot(coeffs[14], weights_ref[14], NN)
    five = dot(four.astype(BF), weights_ref[15], NN)
    six = dot((four + five).astype(BF), weights_ref[15], NN)
    coeffs[15] = (four + six).astype(BF)
    root = jnp.where(iota((256, 128), 0) == iota((256, 128), 1) * 8 + 6, 1.0, 0.0).astype(BF)
    tile = dot(coeffs[15], root, NN).astype(BF)
    for q in range(top_ref.shape[0]):
        top_ref[q] = tile
    for g in range(16):
        first_ref[:, halo + g * 256 : halo + (g + 1) * 256] = coeffs[g]
        second_ref[:, halo + g * 256 : halo + (g + 1) * 256] = coeffs[g]
    low_edge, high_edge = ordered_ref[:, :halo], ordered_ref[:, points - halo :]

    @pl.when(odd)
    def _():
        first_ref[:, :halo] = low_edge
        second_ref[:, :halo] = high_edge

    @pl.when(jnp.logical_not(odd))
    def _():
        first_ref[:, :halo] = high_edge
        second_ref[:, :halo] = low_edge


def near_group(leaves_ref, lists_ref, blocks, first, base, columns):
    lane_left = iota((columns, 128), 1) < 64
    picked = []
    for i in range(4):
        spots = [lists_ref[s, first + i] - base for s in range(4)]
        halves = []
        for s in (0, 2):
            even = leaves_ref[spots[s]]
            odd = leaves_ref[spots[s + 1] ^ 1]
            halves.append(jnp.where(lane_left, even, odd))
        picked.append(jnp.concatenate(halves, axis=1))
    moving = jnp.concatenate(picked, axis=0).astype(BF)
    out = dot(moving, blocks, NT)
    leaf_of_lane = iota((columns, 256), 1) >> 6
    total = out[:columns]
    for i in range(1, 4):
        total = jnp.where(leaf_of_lane == i, out[i * columns : (i + 1) * columns], total)
    return total


def place_leaves(leaves_ref, first, chunk):
    chunk = chunk.astype(F32)
    leaves_ref[first] = chunk
    leaves_ref[first + 1] = pltpu.roll(chunk, 64, 1)


def matrices_kernel(coupling_ref, lists_ref, matrices_ref, spots_ref, rows32):
    rank = 32
    device = lax.axis_index("leaf")
    count = 64

    node = iota((1, 128), 1)
    size = jnp.full((1, 128), count, jnp.int32)
    start = jnp.zeros((1, 128), jnp.int32)
    offset = 0
    for level in range(LEVELS):
        size = jnp.where(node >= offset, count >> level, size)
        start = jnp.where(node >= offset, offset, start)
        offset += count >> level
    entries = pad_lanes(lists_ref[...])
    for s in range(6):
        entry = entries[s : s + 1]
        place = entry - device * size + size
        side = jnp.where(place >= size, 1, 0) + jnp.where(place >= 2 * size, 1, 0)
        spot = side * 128 + start + place - side * size
        used = (entry >= 0) & (node < offset)
        spots_ref[pl.ds(s, 1), :] = jnp.where(used, spot, 3 * 128)
    spots_ref[pl.ds(6, 2), :] = jnp.zeros((2, 128), jnp.int32)

    for a in range(rank):
        one = [coupling_ref[s, a * rank : (a + 1) * rank, :].astype(F32) for s in range(6)]
        full = pad_lanes(jnp.concatenate(one, axis=0))
        turned = jnp.concatenate([full[:128].T, pad_lanes(full[128:].T)], axis=1)
        rows32[a] = turned
    for g in range(16):
        matrices_ref[g] = rows32[:, g * 8 : g * 8 + 8, :].reshape(256, 256).astype(BF)


def near_kernel(ordered_ref, blocks_ref, near_ref, near_out, leaves):
    columns, points = ordered_ref.shape
    count = blocks_ref.shape[0]
    device = lax.axis_index("leaf")
    for c in range(count // 2):
        place_leaves(leaves, c * 2, ordered_ref[:, c * 128 : (c + 1) * 128])
    edge = REACH // 4
    near_out[:, : edge * 256] = jnp.zeros((columns, edge * 256), F32)
    near_out[:, points - edge * 256 :] = jnp.zeros((columns, edge * 256), F32)

    def near(g, carry):
        blocks = blocks_ref[pl.ds(g * 4, 4)].reshape(256, 256)
        at = pl.multiple_of(g * 256, 256)
        near_out[:, pl.ds(at, 256)] = near_group(
            leaves, near_ref, blocks, g * 4, device * count, columns
        )
        return carry

    lax.fori_loop(edge, count // 4 - edge, near, 0, unroll=4)


def reach_kernel(weights_ref, masked_ref, inverse_ref, hot_ref, reach_ref, stacked):
    rank, points = reach_ref.shape
    unit = jnp.where(iota((rank, 256), 1) == iota((rank, 256), 0) * 8 + 6, 1.0, 0.0)
    five = dot(unit.astype(BF), weights_ref[15], NT)
    down = [None] * 16
    down[15] = dot((unit + five).astype(BF), weights_ref[15], NT).astype(BF)
    for k in reversed(range(15)):
        down[k] = dot(down[8 + k // 2], weights_ref[k], NT).astype(BF)
    for g in range(points // 512):
        at_points = dot(down[g], masked_ref[g], NN).astype(BF)
        stacked[2 * g * rank : (2 * g + 1) * rank, :] = at_points[:, :256]
        stacked[(2 * g + 1) * rank : (2 * g + 2) * rank, :] = at_points[:, 256:]
    for c in range(points // 256):
        hot = one_hot(inverse_ref[16 + c : 17 + c, :])
        hot_ref[c] = hot
        reach_ref[:, c * 256 : (c + 1) * 256] = pick(
            stacked[...], hot, inverse_ref[c : c + 1, :], rank
        ).astype(BF)


def outer_kernel(
    ordered_ref, own_ref, first_ref, second_ref, near_in, blocks_ref, near_ref, matrices_ref,
    spots_ref, inverse_ref, weights_ref, masked_ref, hot_ref,
    partial_ref,
    leaves, nodes, far, stacked, stacked_nodes, edges, sems,
):
    columns, points = ordered_ref.shape
    halo = first_ref.shape[1] - 4096
    device = lax.axis_index("leaf")
    count = points // 64
    copies = [
        pltpu.make_async_copy(blocks_ref.at[pl.ds(at, REACH)], edges.at[i], sems.at[i])
        for i, at in enumerate((0, count - REACH))
    ]
    for copy in copies:
        copy.start()

    odd = device % 2
    for ref, right in ((first_ref, 1 - odd), (second_ref, odd)):
        for c in range(halo // 128):
            place_leaves(leaves, right * (REACH + count) + c * 2, ref[:, c * 128 : (c + 1) * 128])
    near_ends = REACH * 64 * 2 // 128
    for c in list(range(near_ends)) + list(range(count // 2 - near_ends, count // 2)):
        place_leaves(leaves, REACH + c * 2, ordered_ref[:, c * 128 : (c + 1) * 128])

    nodes[3 * 128] = jnp.zeros((columns, 128), F32)
    lane, row = iota((256, 1024), 1), iota((256, 1024), 0)
    spread = jnp.where(row == (lane & 31) * 8 + (lane >> 7), 1.0, 0.0).astype(BF)
    for side, ref in ((1, own_ref), (2 - 2 * odd, first_ref), (2 * odd, second_ref)):
        for n in range(16):
            stacked_nodes[n * columns : (n + 1) * columns, :] = ref[:, halo + n * 256 : halo + (n + 1) * 256]
        for c in range(0, 8, 2):
            out = dot(stacked_nodes[...], spread[:, c * 128 : (c + 2) * 128], NN)
            for n in range(16):
                both = out[n * columns : (n + 1) * columns]
                nodes[side * 128 + n * 8 + c] = both[:, :128]
                nodes[side * 128 + n * 8 + c + 1] = both[:, 128:]

    lane_group = iota((columns, 128), 1) >> 5
    lane_node = iota((columns, 256), 1) & 7

    def couple(g, carry):
        picked = []
        for i in range(8):
            parts = [nodes[spots_ref[s, g * 8 + i]] for s in range(6)]
            front = parts[0]
            for s in range(1, 4):
                front = jnp.where(lane_group == s, parts[s], front)
            back = jnp.where(lane_group == 1, parts[5], parts[4])
            back = jnp.where(lane_group < 2, back, 0.0)
            picked.append(jnp.concatenate([front, back], axis=1))
        out = dot(jnp.concatenate(picked, axis=0).astype(BF), matrices_ref[g], NT)
        total = out[:columns]
        for i in range(1, 8):
            total = jnp.where(lane_node == i, out[i * columns : (i + 1) * columns], total)
        far[:, pl.ds(pl.multiple_of(g * 256, 256), 256)] = total
        return carry

    lax.fori_loop(0, 16, couple, 0, unroll=4)

    for copy in copies:
        copy.wait()
    down = [None] * 16
    last = far[:, 15 * 256 :]
    five = jnp.where(lane_node >= 4, last, 0.0).astype(BF)
    down[15] = (last + dot(five, weights_ref[15], NT)).astype(BF)
    for k in reversed(range(15)):
        down[k] = (far[:, k * 256 : (k + 1) * 256] + dot(down[8 + k // 2], weights_ref[k], NT)).astype(BF)
    groups = count // 4
    edge = REACH // 4
    for g in range(groups):
        if g < edge:
            blocks = edges[0, g * 4 : g * 4 + 4].reshape(256, 256)
        elif g >= groups - edge:
            at = (g - groups + edge) * 4
            blocks = edges[1, at : at + 4].reshape(256, 256)
        else:
            blocks = None
        if blocks is None:
            near = near_in[:, g * 256 : (g + 1) * 256]
        else:
            near = near_group(leaves, near_ref, blocks, g * 4, device * count - REACH, columns)
        if g % 2 == 0:
            at_points = dot(down[g // 2], masked_ref[g // 2], NN)
        half = at_points[:, g % 2 * 256 : (g % 2 + 1) * 256]
        stacked[g * columns : (g + 1) * columns, :] = (near + half).astype(BF)

    for c in range(points // 256):
        partial_ref[:, c * 256 : (c + 1) * 256] = pick(
            stacked[...], hot_ref[c], inverse_ref[c : c + 1, :], columns
        )


def top_kernel(
    gathered_ref, transfer_ref, coupling_ref, lists_ref, partial_ref, reach_ref, out_ref, coeffs,
):
    node_count = gathered_ref.shape[0]
    columns = gathered_ref.shape[1]
    device = lax.axis_index("leaf")
    total = 2 * node_count - 1
    for q in range(node_count):
        coeffs[q] = gathered_ref[q][:, :32].astype(F32)
    start, count = 0, node_count
    while count > 1:
        for j in range(count // 2):
            lifted = dot(coeffs[start + 2 * j].astype(BF), transfer_ref[start + 2 * j], NN)
            lifted += dot(coeffs[start + 2 * j + 1].astype(BF), transfer_ref[start + 2 * j + 1], NN)
            coeffs[start + count + j] = lifted.astype(BF).astype(F32)
        start, count = start + count, count // 2
    coeffs[total] = jnp.zeros((columns, 32), F32)
    starts, start, count = [], 0, node_count
    while count >= 1:
        starts.append((start, count))
        start, count = start + count, count // 2
    down = None
    for level, (start, count) in reversed(list(enumerate(starts))):
        node = start + (device >> level)
        field = None
        for s in range(6):
            entry = lists_ref[s, node]
            spot = jnp.where(entry >= 0, start + entry, total)
            term = dot(coeffs[spot].astype(BF), coupling_ref[s, node], NT)
            field = term if field is None else field + term
        if down is not None:
            field = field + dot(down, transfer_ref[node], NT)
        down = field.astype(BF)

    points = out_ref.shape[1]
    for c in range(points // 512):
        at = pl.ds(c * 512, 512)
        out_ref[:, at] = partial_ref[:, at] + dot(down, reach_ref[:, at], NN)


VMEM = pl.BlockSpec(memory_space=pltpu.VMEM)
SMEM = pl.BlockSpec(memory_space=pltpu.SMEM)


def in_hbm(x):
    return pltpu.with_memory_space_constraint(x, pltpu.HBM)


def call(kernel, outs, scratch, specs, flops, name, args, mib=36):
    size = sum(a.size * a.dtype.itemsize for a in args)
    return pl.pallas_call(
        kernel,
        out_shape=[jax.ShapeDtypeStruct(s, t) for s, t in outs],
        in_specs=specs,
        out_specs=[VMEM] * len(outs),
        scratch_shapes=scratch,
        compiler_params=pltpu.CompilerParams(vmem_limit_bytes=mib * 2**20),
        cost_estimate=pl.CostEstimate(flops=flops, bytes_accessed=size, transcendentals=0),
        name=name,
    )(*args)


def local(
    vectors, tree_order, leaf_basis, near_blocks, near_lists, transfers, couplings, coupling_lists,
    top_transfers, top_couplings, top_lists,
):
    columns, points = vectors.shape
    rank = leaf_basis.shape[0]
    devices = lax.axis_size("leaf")
    halo = REACH * near_blocks.shape[1]
    packed = halo + 128 * rank
    order = tree_order.reshape(points // 128, 128)
    near_t = jnp.transpose(near_lists)
    lists_t = jnp.transpose(coupling_lists)
    moves = transfers.reshape(rank * rank, -1)
    matrices = couplings.reshape(6, rank * rank, -1)

    ordered, first, second, top, weights, masked, inverse = call(
        up_kernel,
        [
            ((columns, points), BF), ((columns, packed), BF), ((columns, packed), BF), ((devices, columns, 128), BF),
            ((16, 256, 256), BF), ((points // 512, 256, 512), BF), ((32, 256), jnp.int32),
        ],
        [
            pltpu.VMEM(vectors.shape, BF), pltpu.VMEM(order.shape, jnp.int32),
            pltpu.VMEM(leaf_basis.shape, BF), pltpu.VMEM(moves.shape, BF),
            pltpu.VMEM((points // 256 * columns, 256), BF), pltpu.VMEM((rank, 128, 256), F32),
            pltpu.SemaphoreType.DMA((4,)),
        ],
        [pl.BlockSpec(memory_space=pl.ANY)] * 4, 10**9, "up",
        tuple(in_hbm(x) for x in (vectors, order, leaf_basis, moves)),
    )
    gathered = lax.all_to_all(top, "leaf", 0, 0)
    evens = [(i, i + 1) for i in range(0, devices - 1, 2)]
    odds = [(i, i + 1) for i in range(1, devices - 1, 2)]
    from_first = lax.ppermute(first, "leaf", evens + [(j, i) for i, j in evens])
    from_second = lax.ppermute(second, "leaf", odds + [(j, i) for i, j in odds])

    coupling_rows, spots = call(
        matrices_kernel, [((16, 256, 256), BF), ((8, 128), jnp.int32)],
        [pltpu.VMEM((rank, 128, 256), F32)],
        [VMEM, VMEM], 3 * 10**9, "matrices", (matrices, lists_t),
    )
    (near_part,) = call(
        near_kernel, [((columns, points), F32)],
        [pltpu.VMEM((points // 64, columns, 128), F32)],
        [VMEM, VMEM, SMEM], 3 * 10**9, "near", (ordered, near_blocks, near_t),
    )
    hot, reach = call(
        reach_kernel, [((points // 256, 256, 256), BF), ((rank, points), BF)],
        [pltpu.VMEM((points // 256 * rank, 256), BF)],
        [VMEM, VMEM, VMEM], 4 * 10**9, "reach", (weights, masked, inverse),
    )
    (partial,) = call(
        outer_kernel,
        [((columns, points), F32)],
        [
            pltpu.VMEM((points // 64 + 2 * REACH, columns, 128), F32),
            pltpu.VMEM((385, columns, 128), F32), pltpu.VMEM((columns, 4096), F32),
            pltpu.VMEM((points // 256 * columns, 256), BF), pltpu.VMEM((16 * columns, 256), BF),
            pltpu.VMEM((2, REACH) + near_blocks.shape[1:], BF), pltpu.SemaphoreType.DMA((2,)),
        ],
        [
            VMEM, VMEM, VMEM, VMEM, VMEM, pl.BlockSpec(memory_space=pl.ANY), SMEM, VMEM,
            SMEM, VMEM, VMEM, VMEM, VMEM,
        ], 4 * 10**9, "outer",
        (
            ordered, first, from_first, from_second, near_part, in_hbm(near_blocks), near_t, coupling_rows,
            spots, inverse, weights, masked, hot,
        ),
    )
    (applied,) = call(
        top_kernel,
        [((columns, points), F32)],
        [pltpu.VMEM((2 * devices, columns, 32), F32)],
        [VMEM, VMEM, VMEM, SMEM, VMEM, VMEM], 10**9, "top",
        (
            gathered, jnp.transpose(top_transfers, (2, 0, 1)), jnp.transpose(top_couplings, (0, 3, 1, 2)),
            jnp.transpose(top_lists), partial, reach,
        ),
    )
    return applied


def solution(mesh):
    placed = (
        P("rhs", ("groups", "leaf")),
        P(("groups", "leaf")),
        P(None, ("groups", "leaf")),
        P(("groups", "leaf"), None, None),
        P(("groups", "leaf"), None),
        P(None, None, ("groups", "leaf")),
        P(None, None, None, ("groups", "leaf")),
        P(("groups", "leaf"), None),
        P(None, None, "groups"),
        P(None, None, None, "groups"),
        P("groups", None),
    )
    return jax.shard_map(
        local, mesh=mesh, in_specs=placed, out_specs=P("rhs", ("groups", "leaf")), check_vma=False
    )
```

```python
import functools

import jax
import jax.numpy as jnp
from jax import lax
from jax.experimental import pallas as pl
from jax.experimental.pallas import tpu as pltpu
from jax.sharding import PartitionSpec as P

LEVELS = 6
REACH = 8
BF = jnp.bfloat16
F32 = jnp.float32
NT = (((1,), (1,)), ((), ()))
NN = (((1,), (0,)), ((), ()))


def iota(shape, axis):
    return lax.broadcasted_iota(jnp.int32, shape, axis)


def dot(a, b, dims):
    return lax.dot_general(a, b, dims, preferred_element_type=F32)


def pad_lanes(x):
    short = 128 - x.shape[1]
    return jnp.concatenate([x, jnp.zeros((x.shape[0], short), x.dtype)], axis=1)


def one_hot(ids):
    return jnp.where(iota((256, 256), 0) == jnp.broadcast_to(ids, (256, 256)), 1.0, 0.0).astype(BF)


def pick(stacked, hot, high, rows):
    out = dot(stacked, hot, NN)
    high = jnp.broadcast_to(high, (rows, 256))
    total = out[:rows]
    for block in range(1, stacked.shape[0] // rows):
        total = jnp.where(high == block, out[block * rows : (block + 1) * rows], total)
    return total


def up_kernel(
    vec_hbm, order_hbm, basis_hbm, transfer_hbm,
    ordered_ref, first_ref, second_ref, top_ref, weights_ref, masked_ref, inverse_ref,
    vec_ref, order_ref, basis_ref, transfer_ref, stacked, rows32, sems,
):
    columns, points = vec_ref.shape
    rank = basis_ref.shape[0]
    chunks = points // 256
    halo = first_ref.shape[1] - 4096
    odd = lax.axis_index("leaf") % 2 == 1
    pairs = (
        (transfer_hbm, transfer_ref), (order_hbm, order_ref), (vec_hbm, vec_ref), (basis_hbm, basis_ref),
    )
    copies = [pltpu.make_async_copy(src, dst, sems.at[i]) for i, (src, dst) in enumerate(pairs)]
    for copy in copies:
        copy.start()

    copies[0].wait()
    lane, row = iota((128, 256), 1), iota((128, 256), 0)
    family = (lane & 7) == ((row >> 1) & 7)
    spread = [
        jnp.where(iota((128, 256), 0) == (iota((128, 256), 1) >> 3) + 32 * q, 1.0, 0.0).astype(BF)
        for q in range(4)
    ]
    for m in range(rank // 4):
        turned = pad_lanes(transfer_ref[pl.ds(m * 4 * rank, 4 * rank), :].astype(F32)).T.astype(BF)
        for q in range(4):
            rows32[m * 4 + q] = jnp.where(family, dot(turned, spread[q], NN), 0.0)
    for k in range(16):
        weights_ref[k] = rows32[:, k * 8 : k * 8 + 8, :].reshape(256, 256).astype(BF)

    copies[1].wait()
    copies[2].wait()
    for block in range(chunks):
        stacked[block * columns : (block + 1) * columns, :] = vec_ref[:, block * 256 : (block + 1) * 256]
    within = iota((16, 256), 1).astype(F32)
    inverse = jnp.zeros((32, 256), F32)
    for c in range(chunks):
        ids = jnp.concatenate([order_ref[2 * c : 2 * c + 1, :], order_ref[2 * c + 1 : 2 * c + 2, :]], axis=1)
        ids = lax.rem(ids, points)
        high, low = ids >> 8, ids & 255
        hot = one_hot(low)
        ordered_ref[:, c * 256 : (c + 1) * 256] = pick(stacked[...], hot, high, columns).astype(BF)
        hit = iota((16, 256), 0) == jnp.broadcast_to(high, (16, 256))
        marks = jnp.concatenate([jnp.where(hit, float(c), 0.0), jnp.where(hit, within, 0.0)], axis=0)
        inverse = inverse + dot(marks.astype(BF), hot, NT)
    inverse_ref[...] = inverse.astype(jnp.int32)

    copies[3].wait()
    mine = (iota((256, 512), 0) & 7) == (iota((256, 512), 1) >> 6)
    coeffs = [None] * 16
    for g in range(points // 512):
        one = basis_ref[:, g * 512 : (g + 1) * 512].astype(F32)
        eight = jnp.broadcast_to(one[:, None, :], (rank, 8, 512)).reshape(256, 512)
        masked = jnp.where(mine, eight, 0.0).astype(BF)
        masked_ref[g] = masked
        coeffs[g] = dot(ordered_ref[:, g * 512 : (g + 1) * 512], masked, NT).astype(BF)
    for n in range(7):
        lifted = dot(coeffs[2 * n], weights_ref[2 * n], NN) + dot(coeffs[2 * n + 1], weights_ref[2 * n + 1], NN)
        coeffs[8 + n] = lifted.astype(BF)
    four = dot(coeffs[14], weights_ref[14], NN)
    five = dot(four.astype(BF), weights_ref[15], NN)
    six = dot((four + five).astype(BF), weights_ref[15], NN)
    coeffs[15] = (four + six).astype(BF)
    root = jnp.where(iota((256, 128), 0) == iota((256, 128), 1) * 8 + 6, 1.0, 0.0).astype(BF)
    top_ref[...] = dot(coeffs[15], root, NN).astype(BF)
    for g in range(16):
        first_ref[:, halo + g * 256 : halo + (g + 1) * 256] = coeffs[g]
        second_ref[:, halo + g * 256 : halo + (g + 1) * 256] = coeffs[g]
    low_edge, high_edge = ordered_ref[:, :halo], ordered_ref[:, points - halo :]

    @pl.when(odd)
    def _():
        first_ref[:, :halo] = low_edge
        second_ref[:, :halo] = high_edge

    @pl.when(jnp.logical_not(odd))
    def _():
        first_ref[:, :halo] = high_edge
        second_ref[:, :halo] = low_edge


def near_group(leaves_ref, lists_ref, blocks, first, base, columns):
    lane_left = iota((columns, 128), 1) < 64
    picked = []
    for i in range(4):
        spots = [lists_ref[s, first + i] - base for s in range(4)]
        halves = []
        for s in (0, 2):
            even = leaves_ref[spots[s]]
            odd = leaves_ref[spots[s + 1] ^ 1]
            halves.append(jnp.where(lane_left, even, odd))
        picked.append(jnp.concatenate(halves, axis=1))
    moving = jnp.concatenate(picked, axis=0).astype(BF)
    out = dot(moving, blocks, NT)
    leaf_of_lane = iota((columns, 256), 1) >> 6
    total = out[:columns]
    for i in range(1, 4):
        total = jnp.where(leaf_of_lane == i, out[i * columns : (i + 1) * columns], total)
    return total


def place_leaves(leaves_ref, first, chunk):
    chunk = chunk.astype(F32)
    leaves_ref[first] = chunk
    leaves_ref[first + 1] = pltpu.roll(chunk, 64, 1)


def matrices_kernel(
    coupling_ref, lists_ref, inverse_ref, top_ref, matrices_ref, spots_ref, hot_ref, copies_ref, rows32,
):
    rank = 32
    device = lax.axis_index("leaf")
    count = 64

    for q in range(copies_ref.shape[0]):
        copies_ref[q] = top_ref[...]
    for c in range(hot_ref.shape[0]):
        hot_ref[c] = one_hot(inverse_ref[16 + c : 17 + c, :])

    node = iota((1, 128), 1)
    size = jnp.full((1, 128), count, jnp.int32)
    start = jnp.zeros((1, 128), jnp.int32)
    offset = 0
    for level in range(LEVELS):
        size = jnp.where(node >= offset, count >> level, size)
        start = jnp.where(node >= offset, offset, start)
        offset += count >> level
    entries = pad_lanes(lists_ref[...])
    for s in range(6):
        entry = entries[s : s + 1]
        place = entry - device * size + size
        side = jnp.where(place >= size, 1, 0) + jnp.where(place >= 2 * size, 1, 0)
        spot = side * 128 + start + place - side * size
        used = (entry >= 0) & (node < offset)
        spots_ref[pl.ds(s, 1), :] = jnp.where(used, spot, 3 * 128)
    spots_ref[pl.ds(6, 2), :] = jnp.zeros((2, 128), jnp.int32)

    for a in range(rank):
        one = [coupling_ref[s, a * rank : (a + 1) * rank, :].astype(F32) for s in range(6)]
        full = pad_lanes(jnp.concatenate(one, axis=0))
        turned = jnp.concatenate([full[:128].T, pad_lanes(full[128:].T)], axis=1)
        rows32[a] = turned
    for g in range(16):
        matrices_ref[g] = rows32[:, g * 8 : g * 8 + 8, :].reshape(256, 256).astype(BF)


def near_kernel(ordered_ref, blocks_ref, near_ref, near_out, leaves):
    columns, points = ordered_ref.shape
    count = blocks_ref.shape[0]
    device = lax.axis_index("leaf")
    for c in range(count // 2):
        place_leaves(leaves, c * 2, ordered_ref[:, c * 128 : (c + 1) * 128])
    edge = REACH // 4
    near_out[:, : edge * 256] = jnp.zeros((columns, edge * 256), F32)
    near_out[:, points - edge * 256 :] = jnp.zeros((columns, edge * 256), F32)

    def near(g, carry):
        blocks = blocks_ref[pl.ds(g * 4, 4)].reshape(256, 256)
        at = pl.multiple_of(g * 256, 256)
        near_out[:, pl.ds(at, 256)] = near_group(
            leaves, near_ref, blocks, g * 4, device * count, columns
        )
        return carry

    lax.fori_loop(edge, count // 4 - edge, near, 0, unroll=4)


def root_part(gathered_ref, transfer_ref, coupling_ref, lists_ref, coeffs, device):
    node_count, columns = gathered_ref.shape[:2]
    total = 2 * node_count - 1
    coeffs[total] = jnp.zeros((columns, 32), F32)
    values = [gathered_ref[q][:, :32] for q in range(node_count)]
    start, count = 0, node_count
    starts = [(0, node_count)]
    for j in range(node_count):
        coeffs[j] = values[j].astype(F32)
    while count > 1:
        for j in range(count // 2):
            left, right = start + 2 * j, start + 2 * j + 1
            lifted = dot(values[left], transfer_ref[left], NN) + dot(values[right], transfer_ref[right], NN)
            values.append(lifted.astype(BF))
            coeffs[start + count + j] = values[-1].astype(F32)
        start, count = start + count, count // 2
        starts.append((start, count))
    fields = []
    for level, (start, count) in enumerate(starts):
        node = start + (device >> level)
        field = None
        for s in range(6):
            entry = lists_ref[s, node]
            spot = jnp.where(entry >= 0, start + entry, total)
            term = dot(coeffs[spot].astype(BF), coupling_ref[s, node], NT)
            field = term if field is None else field + term
        fields.append((node, field))
    down = fields.pop()[1].astype(BF)
    for node, field in reversed(fields):
        down = (field + dot(down, transfer_ref[node], NT)).astype(BF)
    return down


def outer_kernel(
    ordered_ref, own_ref, first_ref, second_ref, near_in, blocks_ref, near_ref, matrices_ref,
    spots_ref, inverse_ref, weights_ref, masked_ref, hot_ref,
    gathered_ref, top_transfer_ref, top_coupling_ref, top_lists_ref,
    applied_ref,
    leaves, nodes, far, stacked, stacked_nodes, edges, coeffs, sems,
):
    columns, points = ordered_ref.shape
    halo = first_ref.shape[1] - 4096
    device = lax.axis_index("leaf")
    count = points // 64
    copies = [
        pltpu.make_async_copy(blocks_ref.at[pl.ds(at, REACH)], edges.at[i], sems.at[i])
        for i, at in enumerate((0, count - REACH))
    ]
    for copy in copies:
        copy.start()

    root = root_part(gathered_ref, top_transfer_ref, top_coupling_ref, top_lists_ref, coeffs, device)
    sixth = jnp.where(iota((32, 256), 1) == iota((32, 256), 0) * 8 + 6, 1.0, 0.0).astype(BF)
    six = dot(root, sixth, NN)

    odd = device % 2
    for ref, right in ((first_ref, 1 - odd), (second_ref, odd)):
        for c in range(halo // 128):
            place_leaves(leaves, right * (REACH + count) + c * 2, ref[:, c * 128 : (c + 1) * 128])
    near_ends = REACH * 64 * 2 // 128
    for c in list(range(near_ends)) + list(range(count // 2 - near_ends, count // 2)):
        place_leaves(leaves, REACH + c * 2, ordered_ref[:, c * 128 : (c + 1) * 128])

    nodes[3 * 128] = jnp.zeros((columns, 128), F32)
    lane, row = iota((256, 1024), 1), iota((256, 1024), 0)
    spread = jnp.where(row == (lane & 31) * 8 + (lane >> 7), 1.0, 0.0).astype(BF)
    for side, ref in ((1, own_ref), (2 - 2 * odd, first_ref), (2 * odd, second_ref)):
        for n in range(16):
            stacked_nodes[n * columns : (n + 1) * columns, :] = ref[:, halo + n * 256 : halo + (n + 1) * 256]
        for c in range(0, 8, 2):
            out = dot(stacked_nodes[...], spread[:, c * 128 : (c + 2) * 128], NN)
            for n in range(16):
                both = out[n * columns : (n + 1) * columns]
                nodes[side * 128 + n * 8 + c] = both[:, :128]
                nodes[side * 128 + n * 8 + c + 1] = both[:, 128:]

    lane_group = iota((columns, 128), 1) >> 5
    lane_node = iota((columns, 256), 1) & 7

    for g in range(16):
        picked = []
        for i in range(8):
            parts = [nodes[spots_ref[s, g * 8 + i]] for s in range(6)]
            front = parts[0]
            for s in range(1, 4):
                front = jnp.where(lane_group == s, parts[s], front)
            back = jnp.where(lane_group == 1, parts[5], parts[4])
            back = jnp.where(lane_group < 2, back, 0.0)
            picked.append(jnp.concatenate([front, back], axis=1))
        out = dot(jnp.concatenate(picked, axis=0).astype(BF), matrices_ref[g], NT)
        total = out[:columns]
        for i in range(1, 8):
            total = jnp.where(lane_node == i, out[i * columns : (i + 1) * columns], total)
        far[:, g * 256 : (g + 1) * 256] = total

    for copy in copies:
        copy.wait()
    down = [None] * 16
    last = far[:, 15 * 256 :]
    five = last + dot(six.astype(BF), weights_ref[15], NT)
    five = jnp.where(lane_node >= 4, five, 0.0) + six
    down[15] = (last + dot(five.astype(BF), weights_ref[15], NT)).astype(BF)
    for k in reversed(range(15)):
        down[k] = (far[:, k * 256 : (k + 1) * 256] + dot(down[8 + k // 2], weights_ref[k], NT)).astype(BF)
    groups = count // 4
    edge = REACH // 4
    for g in range(groups):
        if g < edge:
            blocks = edges[0, g * 4 : g * 4 + 4].reshape(256, 256)
        elif g >= groups - edge:
            at = (g - groups + edge) * 4
            blocks = edges[1, at : at + 4].reshape(256, 256)
        else:
            blocks = None
        if blocks is None:
            near = near_in[:, g * 256 : (g + 1) * 256]
        else:
            near = near_group(leaves, near_ref, blocks, g * 4, device * count - REACH, columns)
        if g % 2 == 0:
            at_points = dot(down[g // 2], masked_ref[g // 2], NN)
        half = at_points[:, g % 2 * 256 : (g % 2 + 1) * 256]
        stacked[g * columns : (g + 1) * columns, :] = (near + half).astype(BF)

    for c in range(points // 256):
        applied_ref[:, c * 256 : (c + 1) * 256] = pick(
            stacked[...], hot_ref[c], inverse_ref[c : c + 1, :], columns
        )


VMEM = pl.BlockSpec(memory_space=pltpu.VMEM)
SMEM = pl.BlockSpec(memory_space=pltpu.SMEM)


def in_hbm(x):
    return pltpu.with_memory_space_constraint(x, pltpu.HBM)


def call(kernel, outs, scratch, specs, flops, name, args, mib=16):
    size = sum(a.size * a.dtype.itemsize for a in args)
    return pl.pallas_call(
        kernel,
        out_shape=[jax.ShapeDtypeStruct(s, t) for s, t in outs],
        in_specs=specs,
        out_specs=[VMEM] * len(outs),
        scratch_shapes=scratch,
        compiler_params=pltpu.CompilerParams(vmem_limit_bytes=mib * 2**20),
        cost_estimate=pl.CostEstimate(flops=flops, bytes_accessed=size, transcendentals=0),
        name=name,
    )(*args)


def local(
    vectors, tree_order, leaf_basis, near_blocks, near_lists, transfers, couplings, coupling_lists,
    top_transfers, top_couplings, top_lists,
):
    columns, points = vectors.shape
    rank = leaf_basis.shape[0]
    devices = lax.axis_size("leaf")
    halo = REACH * near_blocks.shape[1]
    packed = halo + 128 * rank
    order = tree_order.reshape(points // 128, 128)
    near_t = jnp.transpose(near_lists)
    lists_t = jnp.transpose(coupling_lists)
    moves = transfers.reshape(rank * rank, -1)
    matrices = couplings.reshape(6, rank * rank, -1)

    ordered, first, second, top, weights, masked, inverse = call(
        up_kernel,
        [
            ((columns, points), BF), ((columns, packed), BF), ((columns, packed), BF), ((columns, 128), BF),
            ((16, 256, 256), BF), ((points // 512, 256, 512), BF), ((32, 256), jnp.int32),
        ],
        [
            pltpu.VMEM(vectors.shape, BF), pltpu.VMEM(order.shape, jnp.int32),
            pltpu.VMEM(leaf_basis.shape, BF), pltpu.VMEM(moves.shape, BF),
            pltpu.VMEM((points // 256 * columns, 256), BF), pltpu.VMEM((rank, 128, 256), F32),
            pltpu.SemaphoreType.DMA((4,)),
        ],
        [pl.BlockSpec(memory_space=pl.ANY)] * 4, 10**9, "up",
        tuple(in_hbm(x) for x in (vectors, order, leaf_basis, moves)),
    )
    evens = [(i, i + 1) for i in range(0, devices - 1, 2)]
    odds = [(i, i + 1) for i in range(1, devices - 1, 2)]
    from_first = lax.ppermute(first, "leaf", evens + [(j, i) for i, j in evens])
    from_second = lax.ppermute(second, "leaf", odds + [(j, i) for i, j in odds])

    coupling_rows, spots, hot, copies = call(
        matrices_kernel,
        [
            ((16, 256, 256), BF), ((8, 128), jnp.int32), ((points // 256, 256, 256), BF),
            ((devices, columns, 128), BF),
        ],
        [pltpu.VMEM((rank, 128, 256), F32)],
        [VMEM] * 4, 3 * 10**9, "matrices", (matrices, lists_t, inverse, top),
    )
    gathered = lax.all_to_all(copies, "leaf", 0, 0)
    (near_part,) = call(
        near_kernel, [((columns, points), F32)],
        [pltpu.VMEM((points // 64, columns, 128), F32)],
        [VMEM, VMEM, SMEM], 3 * 10**9, "near", (ordered, near_blocks, near_t),
    )
    (applied,) = call(
        outer_kernel,
        [((columns, points), F32)],
        [
            pltpu.VMEM((points // 64 + 2 * REACH, columns, 128), F32),
            pltpu.VMEM((385, columns, 128), F32), pltpu.VMEM((columns, 4096), F32),
            pltpu.VMEM((points // 256 * columns, 256), BF), pltpu.VMEM((16 * columns, 256), BF),
            pltpu.VMEM((2, REACH) + near_blocks.shape[1:], BF),
            pltpu.VMEM((2 * devices, columns, 32), F32), pltpu.SemaphoreType.DMA((2,)),
        ],
        [VMEM] * 5 + [pl.BlockSpec(memory_space=pl.ANY), SMEM, VMEM, SMEM] + [VMEM] * 7 + [SMEM],
        4 * 10**9, "outer",
        (
            ordered, first, from_first, from_second, near_part, in_hbm(near_blocks), near_t, coupling_rows,
            spots, inverse, weights, masked, hot, gathered, jnp.transpose(top_transfers, (2, 0, 1)),
            jnp.transpose(top_couplings, (0, 3, 1, 2)), jnp.transpose(top_lists),
        ),
    )
    return applied


def solution(mesh):
    placed = (
        P("rhs", ("groups", "leaf")),
        P(("groups", "leaf")),
        P(None, ("groups", "leaf")),
        P(("groups", "leaf"), None, None),
        P(("groups", "leaf"), None),
        P(None, None, ("groups", "leaf")),
        P(None, None, None, ("groups", "leaf")),
        P(("groups", "leaf"), None),
        P(None, None, "groups"),
        P(None, None, None, "groups"),
        P("groups", None),
    )
    return jax.shard_map(
        local, mesh=mesh, in_specs=placed, out_specs=P("rhs", ("groups", "leaf")), check_vma=False
    )
```

```python
import functools

import jax
import jax.numpy as jnp
from jax import lax
from jax.experimental import pallas as pl
from jax.experimental.pallas import tpu as pltpu
from jax.sharding import PartitionSpec as P

LEVELS = 6
REACH = 8
BF = jnp.bfloat16
F32 = jnp.float32
NT = (((1,), (1,)), ((), ()))
NN = (((1,), (0,)), ((), ()))


def iota(shape, axis):
    return lax.broadcasted_iota(jnp.int32, shape, axis)


def dot(a, b, dims):
    return lax.dot_general(a, b, dims, preferred_element_type=F32)


def pad_lanes(x):
    short = 128 - x.shape[1]
    return jnp.concatenate([x, jnp.zeros((x.shape[0], short), x.dtype)], axis=1)


def one_hot(ids):
    return jnp.where(iota((256, 256), 0) == jnp.broadcast_to(ids, (256, 256)), 1.0, 0.0).astype(BF)


def split_ids(order_ref, c, points):
    ids = jnp.concatenate([order_ref[2 * c : 2 * c + 1, :], order_ref[2 * c + 1 : 2 * c + 2, :]], axis=1)
    ids = lax.rem(ids, points)
    return ids >> 8, ids & 255


def pick(stacked, hot, high, rows):
    out = dot(stacked, hot, NN)
    high = jnp.broadcast_to(high, (rows, 256))
    total = out[:rows]
    for block in range(1, stacked.shape[0] // rows):
        total = jnp.where(high == block, out[block * rows : (block + 1) * rows], total)
    return total


def leaf_kernel(
    vec_hbm, order_hbm, basis_hbm, ordered_ref, message_ref, masked_ref,
    vec_ref, order_ref, basis_ref, stacked, sems,
):
    columns, points = vec_ref.shape
    rank = basis_ref.shape[0]
    halo = REACH * 64
    pairs = ((order_hbm, order_ref), (vec_hbm, vec_ref), (basis_hbm, basis_ref))
    copies = [pltpu.make_async_copy(src, dst, sems.at[i]) for i, (src, dst) in enumerate(pairs)]
    for copy in copies:
        copy.start()
    copies[0].wait()
    copies[1].wait()
    for block in range(points // 256):
        stacked[block * columns : (block + 1) * columns, :] = vec_ref[:, block * 256 : (block + 1) * 256]
    for c in range(points // 256):
        high, low = split_ids(order_ref, c, points)
        ordered_ref[:, c * 256 : (c + 1) * 256] = pick(stacked[...], one_hot(low), high, columns).astype(BF)

    copies[2].wait()
    mine = (iota((256, 512), 0) & 7) == (iota((256, 512), 1) >> 6)
    for g in range(points // 512):
        one = basis_ref[:, g * 512 : (g + 1) * 512].astype(F32)
        eight = jnp.broadcast_to(one[:, None, :], (rank, 8, 512)).reshape(256, 512)
        masked = jnp.where(mine, eight, 0.0).astype(BF)
        masked_ref[g] = masked
        coeffs = dot(ordered_ref[:, g * 512 : (g + 1) * 512], masked, NT).astype(BF)
        message_ref[:, 2 * halo + g * 256 : 2 * halo + (g + 1) * 256] = coeffs
    message_ref[:, :halo] = ordered_ref[:, :halo]
    message_ref[:, halo : 2 * halo] = ordered_ref[:, points - halo :]


def lift_kernel(message_ref, transfer_ref, lifted_ref, top_ref, weights_ref, rows32):
    rank = 32
    base = 2 * REACH * 64

    lane, row = iota((128, 256), 1), iota((128, 256), 0)
    family = (lane & 7) == ((row >> 1) & 7)
    spread = [
        jnp.where(iota((128, 256), 0) == (iota((128, 256), 1) >> 3) + 32 * q, 1.0, 0.0).astype(BF)
        for q in range(4)
    ]
    for m in range(rank // 4):
        turned = pad_lanes(transfer_ref[m * 4 * rank : (m + 1) * 4 * rank, :].astype(F32)).T.astype(BF)
        for q in range(4):
            rows32[m * 4 + q] = jnp.where(family, dot(turned, spread[q], NN), 0.0)
    for k in range(16):
        weights_ref[k] = rows32[:, k * 8 : k * 8 + 8, :].reshape(256, 256).astype(BF)
    coeffs = [message_ref[:, base + g * 256 : base + (g + 1) * 256] for g in range(8)] + [None] * 8
    for n in range(7):
        lifted = dot(coeffs[2 * n], weights_ref[2 * n], NN) + dot(coeffs[2 * n + 1], weights_ref[2 * n + 1], NN)
        coeffs[8 + n] = lifted.astype(BF)
    four = dot(coeffs[14], weights_ref[14], NN)
    five = dot(four.astype(BF), weights_ref[15], NN)
    six = dot((four + five).astype(BF), weights_ref[15], NN)
    coeffs[15] = (four + six).astype(BF)
    root = jnp.where(iota((256, 128), 0) == iota((256, 128), 1) * 8 + 6, 1.0, 0.0).astype(BF)
    top_ref[0] = dot(coeffs[15], root, NN).astype(BF)
    for g in range(8):
        lifted_ref[:, g * 256 : (g + 1) * 256] = coeffs[8 + g]


def near_group(leaves_ref, lists_ref, blocks, first, base, columns):
    lane_left = iota((columns, 128), 1) < 64
    picked = []
    for i in range(4):
        spots = [lists_ref[s, first + i] - base for s in range(4)]
        halves = []
        for s in (0, 2):
            even = leaves_ref[spots[s]]
            odd = leaves_ref[spots[s + 1] ^ 1]
            halves.append(jnp.where(lane_left, even, odd))
        picked.append(jnp.concatenate(halves, axis=1))
    moving = jnp.concatenate(picked, axis=0).astype(BF)
    out = dot(moving, blocks, NT)
    leaf_of_lane = iota((columns, 256), 1) >> 6
    total = out[:columns]
    for i in range(1, 4):
        total = jnp.where(leaf_of_lane == i, out[i * columns : (i + 1) * columns], total)
    return total


def place_leaves(leaves_ref, first, chunk):
    chunk = chunk.astype(F32)
    leaves_ref[first] = chunk
    leaves_ref[first + 1] = pltpu.roll(chunk, 64, 1)


def matrices_kernel(
    coupling_ref, lists_ref, order_ref, matrices_ref, spots_ref, hot_ref, blocks_ref, rows32,
):
    rank = 32
    device = lax.axis_index("leaf")
    count = 64
    chunks = hot_ref.shape[0]

    within = iota((16, 256), 1).astype(F32)
    inverse = jnp.zeros((32, 256), F32)
    for c in range(chunks):
        high, low = split_ids(order_ref, c, chunks * 256)
        hit = iota((16, 256), 0) == jnp.broadcast_to(high, (16, 256))
        marks = jnp.concatenate([jnp.where(hit, float(c), 0.0), jnp.where(hit, within, 0.0)], axis=0)
        inverse = inverse + dot(marks.astype(BF), one_hot(low), NT)
    inverse = inverse.astype(jnp.int32)
    blocks_ref[...] = inverse[:16]
    for c in range(chunks):
        hot_ref[c] = one_hot(inverse[16 + c : 17 + c, :])

    node = iota((1, 128), 1)
    size = jnp.full((1, 128), count, jnp.int32)
    start = jnp.zeros((1, 128), jnp.int32)
    offset = 0
    for level in range(LEVELS):
        size = jnp.where(node >= offset, count >> level, size)
        start = jnp.where(node >= offset, offset, start)
        offset += count >> level
    entries = pad_lanes(lists_ref[...])
    for s in range(6):
        entry = entries[s : s + 1]
        place = entry - device * size + size
        side = jnp.where(place >= size, 1, 0) + jnp.where(place >= 2 * size, 1, 0)
        spot = side * 128 + start + place - side * size
        used = (entry >= 0) & (node < offset)
        spots_ref[pl.ds(s, 1), :] = jnp.where(used, spot, 3 * 128)
    spots_ref[pl.ds(6, 2), :] = jnp.zeros((2, 128), jnp.int32)

    for a in range(rank):
        one = [coupling_ref[s, a * rank : (a + 1) * rank, :].astype(F32) for s in range(6)]
        full = pad_lanes(jnp.concatenate(one, axis=0))
        turned = jnp.concatenate([full[:128].T, pad_lanes(full[128:].T)], axis=1)
        rows32[a] = turned
    for g in range(16):
        matrices_ref[g] = rows32[:, g * 8 : g * 8 + 8, :].reshape(256, 256).astype(BF)


def near_kernel(ordered_ref, blocks_ref, near_ref, near_out, leaves):
    columns, points = ordered_ref.shape
    count = blocks_ref.shape[0]
    device = lax.axis_index("leaf")
    for c in range(count // 2):
        place_leaves(leaves, c * 2, ordered_ref[:, c * 128 : (c + 1) * 128])
    edge = REACH // 4
    near_out[:, : edge * 256] = jnp.zeros((columns, edge * 256), F32)
    near_out[:, points - edge * 256 :] = jnp.zeros((columns, edge * 256), F32)

    def near(g, carry):
        blocks = blocks_ref[pl.ds(g * 4, 4)].reshape(256, 256)
        at = pl.multiple_of(g * 256, 256)
        near_out[:, pl.ds(at, 256)] = near_group(
            leaves, near_ref, blocks, g * 4, device * count, columns
        )
        return carry

    lax.fori_loop(edge, count // 4 - edge, near, 0, unroll=4)


def root_kernel(near_ref, far_ref, transfer_ref, coupling_ref, lists_ref, six_ref, coeffs):
    node_count, columns = 2 * near_ref.shape[0], near_ref.shape[1]
    device = lax.axis_index("leaf")
    total = 2 * node_count - 1
    coeffs[total] = jnp.zeros((columns, 32), F32)
    for q in range(node_count):
        ref = near_ref if q < node_count // 2 else far_ref
        coeffs[q ^ device] = ref[q % (node_count // 2)][:, :32].astype(F32)
    values = [coeffs[j].astype(BF) for j in range(node_count)]
    start, count = 0, node_count
    starts = [(0, node_count)]
    while count > 1:
        for j in range(count // 2):
            left, right = start + 2 * j, start + 2 * j + 1
            lifted = dot(values[left], transfer_ref[left], NN) + dot(values[right], transfer_ref[right], NN)
            values.append(lifted.astype(BF))
            coeffs[start + count + j] = values[-1].astype(F32)
        start, count = start + count, count // 2
        starts.append((start, count))
    fields = []
    for level, (start, count) in enumerate(starts):
        node = start + (device >> level)
        field = None
        for s in range(6):
            entry = lists_ref[s, node]
            spot = jnp.where(entry >= 0, start + entry, total)
            term = dot(coeffs[spot].astype(BF), coupling_ref[s, node], NT)
            field = term if field is None else field + term
        fields.append((node, field))
    down = fields.pop()[1].astype(BF)
    for node, field in reversed(fields):
        down = (field + dot(down, transfer_ref[node], NT)).astype(BF)
    sixth = jnp.where(iota((32, 256), 1) == iota((32, 256), 0) * 8 + 6, 1.0, 0.0).astype(BF)
    six_ref[...] = dot(down, sixth, NN)


def outer_kernel(
    ordered_ref, own0_ref, own1_ref, first0_ref, first1_ref, second0_ref, second1_ref, near_in, blocks_ref,
    near_ref, matrices_ref, spots_ref, inverse_ref, weights_ref, masked_ref, hot_ref, six_ref,
    applied_ref,
    leaves, nodes, far, stacked, stacked_nodes, edges, sems,
):
    columns, points = ordered_ref.shape
    halo = REACH * 64
    device = lax.axis_index("leaf")
    count = points // 64
    copies = [
        pltpu.make_async_copy(blocks_ref.at[pl.ds(at, REACH)], edges.at[i], sems.at[i])
        for i, at in enumerate((0, count - REACH))
    ]
    for copy in copies:
        copy.start()

    odd = device % 2
    for ref, right in ((first0_ref, 1 - odd), (second0_ref, odd)):
        for c in range(halo // 128):
            at = pl.multiple_of((1 - right) * halo + c * 128, 128)
            place_leaves(leaves, right * (REACH + count) + c * 2, ref[:, pl.ds(at, 128)])
    near_ends = REACH * 64 * 2 // 128
    for c in list(range(near_ends)) + list(range(count // 2 - near_ends, count // 2)):
        place_leaves(leaves, REACH + c * 2, ordered_ref[:, c * 128 : (c + 1) * 128])

    nodes[3 * 128] = jnp.zeros((columns, 128), F32)
    lane, row = iota((256, 1024), 1), iota((256, 1024), 0)
    spread = jnp.where(row == (lane & 31) * 8 + (lane >> 7), 1.0, 0.0).astype(BF)
    sources = (
        (1, own0_ref, own1_ref), (2 - 2 * odd, first0_ref, first1_ref), (2 * odd, second0_ref, second1_ref),
    )
    for side, ref0, ref1 in sources:
        for n in range(8):
            at = 2 * halo + n * 256
            stacked_nodes[n * columns : (n + 1) * columns, :] = ref0[:, at : at + 256]
            stacked_nodes[(8 + n) * columns : (9 + n) * columns, :] = ref1[:, n * 256 : (n + 1) * 256]
        for c in range(0, 8, 2):
            out = dot(stacked_nodes[...], spread[:, c * 128 : (c + 2) * 128], NN)
            for n in range(16):
                both = out[n * columns : (n + 1) * columns]
                nodes[side * 128 + n * 8 + c] = both[:, :128]
                nodes[side * 128 + n * 8 + c + 1] = both[:, 128:]

    lane_group = iota((columns, 128), 1) >> 5
    lane_node = iota((columns, 256), 1) & 7

    for g in range(16):
        picked = []
        for i in range(8):
            parts = [nodes[spots_ref[s, g * 8 + i]] for s in range(6)]
            front = parts[0]
            for s in range(1, 4):
                front = jnp.where(lane_group == s, parts[s], front)
            back = jnp.where(lane_group == 1, parts[5], parts[4])
            back = jnp.where(lane_group < 2, back, 0.0)
            picked.append(jnp.concatenate([front, back], axis=1))
        out = dot(jnp.concatenate(picked, axis=0).astype(BF), matrices_ref[g], NT)
        total = out[:columns]
        for i in range(1, 8):
            total = jnp.where(lane_node == i, out[i * columns : (i + 1) * columns], total)
        far[:, g * 256 : (g + 1) * 256] = total

    for copy in copies:
        copy.wait()
    six = six_ref[...]
    down = [None] * 16
    last = far[:, 15 * 256 :]
    five = last + dot(six.astype(BF), weights_ref[15], NT)
    five = jnp.where(lane_node >= 4, five, 0.0) + six
    down[15] = (last + dot(five.astype(BF), weights_ref[15], NT)).astype(BF)
    for k in reversed(range(15)):
        down[k] = (far[:, k * 256 : (k + 1) * 256] + dot(down[8 + k // 2], weights_ref[k], NT)).astype(BF)
    groups = count // 4
    edge = REACH // 4
    for g in range(groups):
        if g < edge:
            blocks = edges[0, g * 4 : g * 4 + 4].reshape(256, 256)
        elif g >= groups - edge:
            at = (g - groups + edge) * 4
            blocks = edges[1, at : at + 4].reshape(256, 256)
        else:
            blocks = None
        if blocks is None:
            near = near_in[:, g * 256 : (g + 1) * 256]
        else:
            near = near_group(leaves, near_ref, blocks, g * 4, device * count - REACH, columns)
        if g % 2 == 0:
            at_points = dot(down[g // 2], masked_ref[g // 2], NN)
        half = at_points[:, g % 2 * 256 : (g % 2 + 1) * 256]
        stacked[g * columns : (g + 1) * columns, :] = (near + half).astype(BF)

    for c in range(points // 256):
        applied_ref[:, c * 256 : (c + 1) * 256] = pick(
            stacked[...], hot_ref[c], inverse_ref[c : c + 1, :], columns
        )


VMEM = pl.BlockSpec(memory_space=pltpu.VMEM)
SMEM = pl.BlockSpec(memory_space=pltpu.SMEM)


def in_hbm(x):
    return pltpu.with_memory_space_constraint(x, pltpu.HBM)


def call(kernel, outs, scratch, specs, flops, name, args, mib=16):
    size = sum(a.size * a.dtype.itemsize for a in args)
    return pl.pallas_call(
        kernel,
        out_shape=[jax.ShapeDtypeStruct(s, t) for s, t in outs],
        in_specs=specs,
        out_specs=[VMEM] * len(outs),
        scratch_shapes=scratch,
        compiler_params=pltpu.CompilerParams(vmem_limit_bytes=mib * 2**20),
        cost_estimate=pl.CostEstimate(flops=flops, bytes_accessed=size, transcendentals=0),
        name=name,
    )(*args)


def local(
    vectors, tree_order, leaf_basis, near_blocks, near_lists, transfers, couplings, coupling_lists,
    top_transfers, top_couplings, top_lists,
):
    columns, points = vectors.shape
    rank = leaf_basis.shape[0]
    devices = lax.axis_size("leaf")
    halo = REACH * near_blocks.shape[1]
    order = tree_order.reshape(points // 128, 128)
    near_t = jnp.transpose(near_lists)
    lists_t = jnp.transpose(coupling_lists)
    moves = transfers.reshape(rank * rank, -1)
    matrices = couplings.reshape(6, rank * rank, -1)

    any_spec = pl.BlockSpec(memory_space=pl.ANY)
    ordered, own0, masked = call(
        leaf_kernel,
        [((columns, points), BF), ((columns, 2 * halo + 2048), BF), ((points // 512, 256, 512), BF)],
        [
            pltpu.VMEM(vectors.shape, BF), pltpu.VMEM(order.shape, jnp.int32),
            pltpu.VMEM(leaf_basis.shape, BF), pltpu.VMEM((points // 256 * columns, 256), BF),
            pltpu.SemaphoreType.DMA((3,)),
        ],
        [any_spec] * 3, 10**9, "leaf", tuple(in_hbm(x) for x in (vectors, order, leaf_basis)),
    )
    pairs = [(i, i ^ 1) for i in range(devices)]
    onward = [(i, i + 2) for i in range(0, devices - 2, 2)] + [(i, i - 2) for i in range(3, devices, 2)]
    first0 = lax.ppermute(own0, "leaf", pairs)
    own1, top, weights = call(
        lift_kernel,
        [((columns, 2048), BF), ((1, columns, 128), BF), ((16, 256, 256), BF)],
        [pltpu.VMEM((rank, 128, 256), F32)], [VMEM, VMEM], 10**9, "lift", (own0, moves),
    )
    first1 = lax.ppermute(own1, "leaf", pairs)
    coupling_rows, spots, hot, blocks = call(
        matrices_kernel,
        [
            ((16, 256, 256), BF), ((8, 128), jnp.int32), ((points // 256, 256, 256), BF),
            ((points // 256, 256), jnp.int32),
        ],
        [pltpu.VMEM((rank, 128, 256), F32)],
        [VMEM] * 3, 3 * 10**9, "matrices", (matrices, lists_t, order),
    )
    first0, blocks = lax.optimization_barrier((first0, blocks))
    second0 = lax.ppermute(first0, "leaf", onward)
    reached, held = 1, [top]
    while reached < devices:
        near_half = held[0] if len(held) == 1 else jnp.concatenate(held, axis=0)
        far_half = lax.ppermute(near_half, "leaf", [(i, i ^ reached) for i in range(devices)])
        held = [near_half, far_half]
        reached *= 2

    first0, ordered_late = lax.optimization_barrier((first0, ordered))
    (near_part,) = call(
        near_kernel, [((columns, points), F32)],
        [pltpu.VMEM((points // 64, columns, 128), F32)],
        [VMEM, VMEM, SMEM], 3 * 10**9, "near", (ordered_late, near_blocks, near_t),
    )
    first1, near_part = lax.optimization_barrier((first1, near_part))
    second1 = lax.ppermute(first1, "leaf", onward)
    (six,) = call(
        root_kernel, [((columns, 256), F32)], [pltpu.VMEM((2 * devices, columns, 32), F32)],
        [VMEM] * 4 + [SMEM], 10**9, "root",
        (
            *held, jnp.transpose(top_transfers, (2, 0, 1)), jnp.transpose(top_couplings, (0, 3, 1, 2)),
            jnp.transpose(top_lists),
        ),
    )
    (applied,) = call(
        outer_kernel,
        [((columns, points), F32)],
        [
            pltpu.VMEM((points // 64 + 2 * REACH, columns, 128), F32),
            pltpu.VMEM((385, columns, 128), F32), pltpu.VMEM((columns, 4096), F32),
            pltpu.VMEM((points // 256 * columns, 256), BF), pltpu.VMEM((16 * columns, 256), BF),
            pltpu.VMEM((2, REACH) + near_blocks.shape[1:], BF), pltpu.SemaphoreType.DMA((2,)),
        ],
        [VMEM] * 8 + [any_spec, SMEM, VMEM, SMEM] + [VMEM] * 5,
        4 * 10**9, "outer",
        (
            ordered, own0, own1, first0, first1, second0, second1, near_part, in_hbm(near_blocks),
            near_t, coupling_rows, spots, blocks, weights, masked, hot, six,
        ),
    )
    return applied


def solution(mesh):
    placed = (
        P("rhs", ("groups", "leaf")),
        P(("groups", "leaf")),
        P(None, ("groups", "leaf")),
        P(("groups", "leaf"), None, None),
        P(("groups", "leaf"), None),
        P(None, None, ("groups", "leaf")),
        P(None, None, None, ("groups", "leaf")),
        P(("groups", "leaf"), None),
        P(None, None, "groups"),
        P(None, None, None, "groups"),
        P("groups", None),
    )
    return jax.shard_map(
        local, mesh=mesh, in_specs=placed, out_specs=P("rhs", ("groups", "leaf")), check_vma=False
    )
```

```python
import functools

import jax
import jax.numpy as jnp
from jax import lax
from jax.experimental import pallas as pl
from jax.experimental.pallas import tpu as pltpu
from jax.sharding import PartitionSpec as P

LEVELS = 6
REACH = 8
BF = jnp.bfloat16
F32 = jnp.float32
NT = (((1,), (1,)), ((), ()))
NN = (((1,), (0,)), ((), ()))


def iota(shape, axis):
    return lax.broadcasted_iota(jnp.int32, shape, axis)


def dot(a, b, dims):
    return lax.dot_general(a, b, dims, preferred_element_type=F32)


def pad_lanes(x):
    short = 128 - x.shape[1]
    return jnp.concatenate([x, jnp.zeros((x.shape[0], short), x.dtype)], axis=1)


def one_hot(ids):
    ids = jnp.broadcast_to(ids.astype(F32), (16, 256)).astype(BF)
    rows = iota((256, 256), 0).astype(F32).astype(BF)
    return jnp.where(rows == jnp.concatenate([ids] * 16, axis=0), jnp.ones((), BF), jnp.zeros((), BF))


def split_ids(order_ref, c, points):
    ids = jnp.concatenate([order_ref[2 * c : 2 * c + 1, :], order_ref[2 * c + 1 : 2 * c + 2, :]], axis=1)
    ids = lax.rem(ids, points)
    return ids >> 8, ids & 255


def pick(stacked, hot, high, rows):
    out = dot(stacked, hot, NN)
    high = jnp.broadcast_to(high, (rows, 256))
    total = out[:rows]
    for block in range(1, stacked.shape[0] // rows):
        total = jnp.where(high == block, out[block * rows : (block + 1) * rows], total)
    return total


def leaf_kernel(
    vec_hbm, order_hbm, basis_hbm, ordered_ref, message_ref, masked_ref,
    vec_ref, order_ref, basis_ref, stacked, sems,
):
    columns, points = vec_ref.shape
    rank = basis_ref.shape[0]
    halo = REACH * 64
    pairs = ((order_hbm, order_ref), (vec_hbm, vec_ref), (basis_hbm, basis_ref))
    copies = [pltpu.make_async_copy(src, dst, sems.at[i]) for i, (src, dst) in enumerate(pairs)]
    for copy in copies:
        copy.start()
    copies[0].wait()
    copies[1].wait()
    for block in range(points // 256):
        stacked[block * columns : (block + 1) * columns, :] = vec_ref[:, block * 256 : (block + 1) * 256]
    for c in range(points // 256):
        high, low = split_ids(order_ref, c, points)
        ordered_ref[:, c * 256 : (c + 1) * 256] = pick(stacked[...], one_hot(low), high, columns).astype(BF)

    copies[2].wait()
    mine = (iota((256, 512), 0) & 7) == (iota((256, 512), 1) >> 6)
    for g in range(points // 512):
        one = basis_ref[:, g * 512 : (g + 1) * 512].astype(F32)
        eight = jnp.broadcast_to(one[:, None, :], (rank, 8, 512)).reshape(256, 512)
        masked = jnp.where(mine, eight, 0.0).astype(BF)
        masked_ref[g] = masked
        coeffs = dot(ordered_ref[:, g * 512 : (g + 1) * 512], masked, NT).astype(BF)
        message_ref[:, 2 * halo + g * 256 : 2 * halo + (g + 1) * 256] = coeffs
    message_ref[:, :halo] = ordered_ref[:, :halo]
    message_ref[:, halo : 2 * halo] = ordered_ref[:, points - halo :]


def lift_kernel(message_ref, transfer_ref, lifted_ref, top_ref, weights_ref, rows32):
    rank = 32
    base = 2 * REACH * 64

    lane, row = iota((128, 256), 1), iota((128, 256), 0)
    family = (lane & 7) == ((row >> 1) & 7)
    spread = [
        jnp.where(iota((128, 256), 0) == (iota((128, 256), 1) >> 3) + 32 * q, 1.0, 0.0).astype(BF)
        for q in range(4)
    ]
    for m in range(rank // 4):
        turned = pad_lanes(transfer_ref[m * 4 * rank : (m + 1) * 4 * rank, :].astype(F32)).T.astype(BF)
        for q in range(4):
            rows32[m * 4 + q] = jnp.where(family, dot(turned, spread[q], NN), 0.0)
    for k in range(16):
        weights_ref[k] = rows32[:, k * 8 : k * 8 + 8, :].reshape(256, 256).astype(BF)
    coeffs = [message_ref[:, base + g * 256 : base + (g + 1) * 256] for g in range(8)] + [None] * 8
    for n in range(7):
        lifted = dot(coeffs[2 * n], weights_ref[2 * n], NN) + dot(coeffs[2 * n + 1], weights_ref[2 * n + 1], NN)
        coeffs[8 + n] = lifted.astype(BF)
    four = dot(coeffs[14], weights_ref[14], NN)
    five = dot(four.astype(BF), weights_ref[15], NN)
    six = dot((four + five).astype(BF), weights_ref[15], NN)
    coeffs[15] = (four + six).astype(BF)
    width = top_ref.shape[1]
    slot = lax.axis_index("leaf") // 2 * rank
    row, lane = iota((256, width), 0), iota((256, width), 1) - slot
    root = jnp.where((row == lane * 8 + 6) & (lane >= 0), 1.0, 0.0).astype(BF)
    top_ref[...] = dot(coeffs[15], root, NN).astype(BF)
    lifted_ref[:, 2048:] = jnp.zeros((lifted_ref.shape[0], width), BF)
    for g in range(8):
        lifted_ref[:, g * 256 : (g + 1) * 256] = coeffs[8 + g]


def lane_numbers(rows):
    return iota((rows, 128), 1).astype(F32).astype(BF)


def near_group(leaves_ref, lists_ref, blocks, first, base, columns):
    lane_left = lane_numbers(columns) < 64
    picked = []
    for i in range(4):
        spots = [lists_ref[s, first + i] - base for s in range(4)]
        halves = []
        for s in (0, 2):
            even = leaves_ref[spots[s]]
            odd = leaves_ref[spots[s + 1] ^ 1]
            halves.append(jnp.where(lane_left, even, odd))
        picked.append(jnp.concatenate(halves, axis=1))
    out = dot(jnp.concatenate(picked, axis=0), blocks, NT)
    leaf_of_lane = iota((columns, 256), 1) >> 6
    total = out[:columns]
    for i in range(1, 4):
        total = jnp.where(leaf_of_lane == i, out[i * columns : (i + 1) * columns], total)
    return total


def place_leaves(leaves_ref, first, chunk):
    leaves_ref[first] = chunk
    leaves_ref[first + 1] = pltpu.roll(chunk.astype(F32), 64, 1).astype(BF)


def matrices_kernel(
    coupling_ref, lists_ref, order_ref, matrices_ref, spots_ref, hot_ref, blocks_ref, rows32,
):
    rank = 32
    device = lax.axis_index("leaf")
    count = 64
    chunks = hot_ref.shape[0]

    within = iota((16, 256), 1).astype(F32)
    inverse = jnp.zeros((32, 256), F32)
    for c in range(chunks):
        high, low = split_ids(order_ref, c, chunks * 256)
        hit = iota((16, 256), 0) == jnp.broadcast_to(high, (16, 256))
        marks = jnp.concatenate([jnp.where(hit, float(c), 0.0), jnp.where(hit, within, 0.0)], axis=0)
        inverse = inverse + dot(marks.astype(BF), one_hot(low), NT)
    inverse = inverse.astype(jnp.int32)
    blocks_ref[...] = inverse[:16]
    for c in range(chunks):
        hot_ref[c] = one_hot(inverse[16 + c : 17 + c, :])

    node = iota((1, 128), 1)
    size = jnp.full((1, 128), count, jnp.int32)
    start = jnp.zeros((1, 128), jnp.int32)
    offset = 0
    for level in range(LEVELS):
        size = jnp.where(node >= offset, count >> level, size)
        start = jnp.where(node >= offset, offset, start)
        offset += count >> level
    entries = pad_lanes(lists_ref[...])
    for s in range(6):
        entry = entries[s : s + 1]
        place = entry - device * size + size
        side = jnp.where(place >= size, 1, 0) + jnp.where(place >= 2 * size, 1, 0)
        spot = side * 128 + start + place - side * size
        used = (entry >= 0) & (node < offset)
        spots_ref[pl.ds(s, 1), :] = jnp.where(used, spot, 3 * 128)
    spots_ref[pl.ds(6, 2), :] = jnp.zeros((2, 128), jnp.int32)

    for a in range(rank):
        one = [coupling_ref[s, a * rank : (a + 1) * rank, :].astype(F32) for s in range(6)]
        full = pad_lanes(jnp.concatenate(one, axis=0))
        turned = jnp.concatenate([full[:128].T, pad_lanes(full[128:].T)], axis=1)
        rows32[a] = turned
    for g in range(16):
        matrices_ref[g] = rows32[:, g * 8 : g * 8 + 8, :].reshape(256, 256).astype(BF)


def near_kernel(ordered_ref, blocks_ref, near_ref, near_out, leaves):
    columns, points = ordered_ref.shape
    count = blocks_ref.shape[0]
    device = lax.axis_index("leaf")
    for c in range(count // 2):
        place_leaves(leaves, c * 2, ordered_ref[:, c * 128 : (c + 1) * 128])
    edge = REACH // 4
    near_out[:, : edge * 256] = jnp.zeros((columns, edge * 256), F32)
    near_out[:, points - edge * 256 :] = jnp.zeros((columns, edge * 256), F32)

    def near(g, carry):
        blocks = blocks_ref[pl.ds(g * 4, 4)].reshape(256, 256)
        at = pl.multiple_of(g * 256, 256)
        near_out[:, pl.ds(at, 256)] = near_group(
            leaves, near_ref, blocks, g * 4, device * count, columns
        )
        return carry

    lax.fori_loop(edge, count // 4 - edge, near, 0, unroll=4)


def root_kernel(own_ref, other_ref, transfer_ref, coupling_ref, lists_ref, six_ref, coeffs):
    columns, rank = own_ref.shape[0], 32
    node_count = lists_ref.shape[1] // 2 + 1
    device = lax.axis_index("leaf")
    total = 2 * node_count - 1
    coeffs[total] = jnp.zeros((columns, rank), F32)
    for q in range(node_count):
        ref = own_ref if q % 2 == 0 else other_ref
        at = 2048 + q // 2 * rank
        coeffs[q ^ (device & 1)] = ref[:, at : at + rank].astype(F32)
    values = [coeffs[j].astype(BF) for j in range(node_count)]
    start, count = 0, node_count
    starts = [(0, node_count)]
    while count > 1:
        for j in range(count // 2):
            left, right = start + 2 * j, start + 2 * j + 1
            lifted = dot(values[left], transfer_ref[left], NN) + dot(values[right], transfer_ref[right], NN)
            values.append(lifted.astype(BF))
            coeffs[start + count + j] = values[-1].astype(F32)
        start, count = start + count, count // 2
        starts.append((start, count))
    fields = []
    for level, (start, count) in enumerate(starts):
        node = start + (device >> level)
        field = None
        for s in range(6):
            entry = lists_ref[s, node]
            spot = jnp.where(entry >= 0, start + entry, total)
            term = dot(coeffs[spot].astype(BF), coupling_ref[s, node], NT)
            field = term if field is None else field + term
        fields.append((node, field))
    down = fields.pop()[1].astype(BF)
    for node, field in reversed(fields):
        down = (field + dot(down, transfer_ref[node], NT)).astype(BF)
    sixth = jnp.where(iota((32, 256), 1) == iota((32, 256), 0) * 8 + 6, 1.0, 0.0).astype(BF)
    six_ref[...] = dot(down, sixth, NN)


def outer_kernel(
    ordered_ref, own0_ref, own1_ref, first0_ref, first1_ref, second0_ref, second1_ref, near_in, blocks_ref,
    near_ref, matrices_ref, spots_ref, inverse_ref, weights_ref, masked_ref, hot_ref, six_ref,
    applied_hbm,
    applied_ref, leaves, nodes, far, stacked, stacked_nodes, edges, sems, out_sems,
):
    columns, points = ordered_ref.shape
    halo = REACH * 64
    device = lax.axis_index("leaf")
    count = points // 64
    copies = [
        pltpu.make_async_copy(blocks_ref.at[pl.ds(at, REACH)], edges.at[i], sems.at[i])
        for i, at in enumerate((0, count - REACH))
    ]
    for copy in copies:
        copy.start()

    odd = device % 2
    for ref, right in ((first0_ref, 1 - odd), (second0_ref, odd)):
        for c in range(halo // 128):
            at = pl.multiple_of((1 - right) * halo + c * 128, 128)
            place_leaves(leaves, right * (REACH + count) + c * 2, ref[:, pl.ds(at, 128)])
    near_ends = REACH * 64 * 2 // 128
    for c in list(range(near_ends)) + list(range(count // 2 - near_ends, count // 2)):
        place_leaves(leaves, REACH + c * 2, ordered_ref[:, c * 128 : (c + 1) * 128])

    nodes[3 * 128] = jnp.zeros((columns, 128), BF)
    lane, row = iota((256, 1024), 1), iota((256, 1024), 0)
    spread = jnp.where(row == (lane & 31) * 8 + (lane >> 7), 1.0, 0.0).astype(BF)
    sources = (
        (1, own0_ref, own1_ref), (2 - 2 * odd, first0_ref, first1_ref), (2 * odd, second0_ref, second1_ref),
    )
    for side, ref0, ref1 in sources:
        for n in range(8):
            at = 2 * halo + n * 256
            stacked_nodes[n * columns : (n + 1) * columns, :] = ref0[:, at : at + 256]
            stacked_nodes[(8 + n) * columns : (9 + n) * columns, :] = ref1[:, n * 256 : (n + 1) * 256]
        for c in range(0, 8, 2):
            out = dot(stacked_nodes[...], spread[:, c * 128 : (c + 2) * 128], NN)
            for n in range(16):
                both = out[n * columns : (n + 1) * columns].astype(BF)
                nodes[side * 128 + n * 8 + c] = both[:, :128]
                nodes[side * 128 + n * 8 + c + 1] = both[:, 128:]

    lane = lane_numbers(columns)
    lane_node = iota((columns, 256), 1) & 7

    for g in range(16):
        picked = []
        for i in range(8):
            parts = [nodes[spots_ref[s, g * 8 + i]] for s in range(6)]
            front = jnp.where(lane < 32, parts[0], parts[1])
            front = jnp.where(lane < 64, front, jnp.where(lane < 96, parts[2], parts[3]))
            back = jnp.where(lane < 32, parts[4], parts[5])
            back = jnp.where(lane < 64, back, jnp.zeros((), BF))
            picked.append(jnp.concatenate([front, back], axis=1))
        out = dot(jnp.concatenate(picked, axis=0), matrices_ref[g], NT)
        total = out[:columns]
        for i in range(1, 8):
            total = jnp.where(lane_node == i, out[i * columns : (i + 1) * columns], total)
        far[:, g * 256 : (g + 1) * 256] = total

    for copy in copies:
        copy.wait()
    six = six_ref[...]
    down = [None] * 16
    last = far[:, 15 * 256 :]
    five = last + dot(six.astype(BF), weights_ref[15], NT)
    five = jnp.where(lane_node >= 4, five, 0.0) + six
    down[15] = (last + dot(five.astype(BF), weights_ref[15], NT)).astype(BF)
    for k in reversed(range(15)):
        down[k] = (far[:, k * 256 : (k + 1) * 256] + dot(down[8 + k // 2], weights_ref[k], NT)).astype(BF)
    groups = count // 4
    edge = REACH // 4
    for g in range(groups):
        if g < edge:
            blocks = edges[0, g * 4 : g * 4 + 4].reshape(256, 256)
        elif g >= groups - edge:
            at = (g - groups + edge) * 4
            blocks = edges[1, at : at + 4].reshape(256, 256)
        else:
            blocks = None
        if blocks is None:
            near = near_in[:, g * 256 : (g + 1) * 256]
        else:
            near = near_group(leaves, near_ref, blocks, g * 4, device * count - REACH, columns)
        if g % 2 == 0:
            at_points = dot(down[g // 2], masked_ref[g // 2], NN)
        half = at_points[:, g % 2 * 256 : (g % 2 + 1) * 256]
        stacked[g * columns : (g + 1) * columns, :] = (near + half).astype(BF)

    writes = []
    for c in range(points // 256):
        applied_ref[:, c * 256 : (c + 1) * 256] = pick(
            stacked[...], hot_ref[c], inverse_ref[c : c + 1, :], columns
        )
        if c % 4 == 3:
            at = pl.ds((c - 3) * 256, 1024)
            writes.append(pltpu.make_async_copy(applied_ref.at[:, at], applied_hbm.at[:, at], out_sems.at[c // 4]))
            writes[-1].start()
    for write in writes:
        write.wait()


VMEM = pl.BlockSpec(memory_space=pltpu.VMEM)
SMEM = pl.BlockSpec(memory_space=pltpu.SMEM)


def in_hbm(x):
    return pltpu.with_memory_space_constraint(x, pltpu.HBM)


def call(kernel, outs, scratch, specs, flops, name, args, mib=16, out_specs=None):
    size = sum(a.size * a.dtype.itemsize for a in args)
    return pl.pallas_call(
        kernel,
        out_shape=[jax.ShapeDtypeStruct(s, t) for s, t in outs],
        in_specs=specs,
        out_specs=out_specs or [VMEM] * len(outs),
        scratch_shapes=scratch,
        compiler_params=pltpu.CompilerParams(vmem_limit_bytes=mib * 2**20),
        cost_estimate=pl.CostEstimate(flops=flops, bytes_accessed=0, transcendentals=0),
        name=name,
    )(*args)


def local(
    vectors, tree_order, leaf_basis, near_blocks, near_lists, transfers, couplings, coupling_lists,
    top_transfers, top_couplings, top_lists,
):
    columns, points = vectors.shape
    rank = leaf_basis.shape[0]
    devices = lax.axis_size("leaf")
    halo = REACH * near_blocks.shape[1]
    order = tree_order.reshape(points // 128, 128)
    near_t = jnp.transpose(near_lists)
    lists_t = jnp.transpose(coupling_lists)
    moves = transfers.reshape(rank * rank, -1)
    matrices = couplings.reshape(6, rank * rank, -1)

    any_spec = pl.BlockSpec(memory_space=pl.ANY)
    tile = max(devices // 2 * rank, 128)
    ordered, own0, masked = call(
        leaf_kernel,
        [((columns, points), BF), ((columns, 2 * halo + 2048), BF), ((points // 512, 256, 512), BF)],
        [
            pltpu.VMEM(vectors.shape, BF), pltpu.VMEM(order.shape, jnp.int32),
            pltpu.VMEM(leaf_basis.shape, BF), pltpu.VMEM((points // 256 * columns, 256), BF),
            pltpu.SemaphoreType.DMA((3,)),
        ],
        [any_spec] * 3, 10**9, "leaf", tuple(in_hbm(x) for x in (vectors, order, leaf_basis)),
    )
    pairs = [(i, i ^ 1) for i in range(devices)]
    onward = [(i, i + 2) for i in range(0, devices - 2, 2)] + [(i, i - 2) for i in range(3, devices, 2)]
    first0 = lax.ppermute(own0, "leaf", pairs)
    own1, top, weights = call(
        lift_kernel,
        [((columns, 2048 + tile), BF), ((columns, tile), BF), ((16, 256, 256), BF)],
        [pltpu.VMEM((rank, 128, 256), F32)], [VMEM, VMEM], 10**9, "lift", (own0, moves),
    )
    steps = [1 << k for k in reversed(range(1, devices.bit_length() - 1))]

    def step(tile_sum, reached):
        return tile_sum + lax.ppermute(tile_sum, "leaf", [(i, i ^ reached) for i in range(devices)])

    coupling_rows, spots, hot, blocks = call(
        matrices_kernel,
        [
            ((16, 256, 256), BF), ((8, 128), jnp.int32), ((points // 256, 256, 256), BF),
            ((points // 256, 256), jnp.int32),
        ],
        [pltpu.VMEM((rank, 128, 256), F32)],
        [VMEM] * 3, 10**7, "matrices", (matrices, lists_t, order),
    )
    for reached in steps[:-1]:
        top = step(top, reached)
    first0, top, blocks, ordered_late = lax.optimization_barrier((first0, top, blocks, ordered))
    second0 = lax.ppermute(first0, "leaf", onward)
    for reached in steps[-1:]:
        top = step(top, reached)
    (near_part,) = call(
        near_kernel, [((columns, points), F32)],
        [pltpu.VMEM((points // 64, columns, 128), BF)],
        [VMEM, VMEM, SMEM], 10**7, "near", (ordered_late, near_blocks, near_t),
    )
    own1 = lax.dynamic_update_slice(own1, top, (0, 2048))
    own1, near_part = lax.optimization_barrier((own1, near_part))
    first1 = lax.ppermute(own1, "leaf", pairs)
    first1, second0 = lax.optimization_barrier((first1, second0))
    second1 = lax.ppermute(first1, "leaf", onward)
    (six,) = call(
        root_kernel, [((columns, 256), F32)], [pltpu.VMEM((2 * devices, columns, 32), F32)],
        [VMEM] * 4 + [SMEM], 10**6, "root",
        (
            own1, first1, jnp.transpose(top_transfers, (2, 0, 1)), jnp.transpose(top_couplings, (0, 3, 1, 2)),
            jnp.transpose(top_lists),
        ),
    )
    (applied,) = call(
        outer_kernel,
        [((columns, points), F32)],
        [
            pltpu.VMEM((columns, points), F32), pltpu.VMEM((points // 64 + 2 * REACH, columns, 128), BF),
            pltpu.VMEM((385, columns, 128), BF), pltpu.VMEM((columns, 4096), F32),
            pltpu.VMEM((points // 256 * columns, 256), BF), pltpu.VMEM((16 * columns, 256), BF),
            pltpu.VMEM((2, REACH) + near_blocks.shape[1:], BF), pltpu.SemaphoreType.DMA((2,)),
            pltpu.SemaphoreType.DMA((points // 1024,)),
        ],
        [VMEM] * 8 + [any_spec, SMEM, VMEM, SMEM] + [VMEM] * 5,
        4 * 10**9, "outer",
        (
            ordered, own0, own1, first0, first1, second0, second1, near_part, in_hbm(near_blocks),
            near_t, coupling_rows, spots, blocks, weights, masked, hot, six,
        ),
        out_specs=[any_spec],
    )
    return applied


def solution(mesh):
    placed = (
        P("rhs", ("groups", "leaf")),
        P(("groups", "leaf")),
        P(None, ("groups", "leaf")),
        P(("groups", "leaf"), None, None),
        P(("groups", "leaf"), None),
        P(None, None, ("groups", "leaf")),
        P(None, None, None, ("groups", "leaf")),
        P(("groups", "leaf"), None),
        P(None, None, "groups"),
        P(None, None, None, "groups"),
        P("groups", None),
    )
    return jax.shard_map(
        local, mesh=mesh, in_specs=placed, out_specs=P("rhs", ("groups", "leaf")), check_vma=False
    )
```

```python
import functools

import jax
import jax.numpy as jnp
from jax import lax
from jax.experimental import pallas as pl
from jax.experimental.pallas import tpu as pltpu
from jax.sharding import PartitionSpec as P

LEVELS = 6
REACH = 8
BF = jnp.bfloat16
F32 = jnp.float32
NT = (((1,), (1,)), ((), ()))
NN = (((1,), (0,)), ((), ()))


def iota(shape, axis):
    return lax.broadcasted_iota(jnp.int32, shape, axis)


def dot(a, b, dims):
    return lax.dot_general(a, b, dims, preferred_element_type=F32)


def pad_lanes(x):
    short = 128 - x.shape[1]
    return jnp.concatenate([x, jnp.zeros((x.shape[0], short), x.dtype)], axis=1)


def one_hot(ids):
    ids = jnp.broadcast_to(ids.astype(F32), (16, 256)).astype(BF)
    rows = iota((256, 256), 0).astype(F32).astype(BF)
    return jnp.where(rows == jnp.concatenate([ids] * 16, axis=0), jnp.ones((), BF), jnp.zeros((), BF))


def split_ids(order_ref, c, points):
    ids = jnp.concatenate([order_ref[2 * c : 2 * c + 1, :], order_ref[2 * c + 1 : 2 * c + 2, :]], axis=1)
    ids = lax.rem(ids, points)
    return ids >> 8, ids & 255


def pick(stacked, hot, high, rows):
    out = dot(stacked, hot, NN)
    high = jnp.broadcast_to(high, (rows, 256))
    total = out[:rows]
    for block in range(1, stacked.shape[0] // rows):
        total = jnp.where(high == block, out[block * rows : (block + 1) * rows], total)
    return total


def leaf_kernel(
    vec_hbm, order_hbm, basis_hbm, ordered_ref, message_ref, masked_ref,
    vec_ref, order_ref, basis_ref, stacked, sems,
):
    columns, points = vec_ref.shape
    rank = basis_ref.shape[0]
    halo = REACH * 64
    pairs = ((order_hbm, order_ref), (vec_hbm, vec_ref), (basis_hbm, basis_ref))
    copies = [pltpu.make_async_copy(src, dst, sems.at[i]) for i, (src, dst) in enumerate(pairs)]
    for copy in copies:
        copy.start()
    copies[0].wait()
    copies[1].wait()
    for block in range(points // 256):
        stacked[block * columns : (block + 1) * columns, :] = vec_ref[:, block * 256 : (block + 1) * 256]
    for c in range(points // 256):
        high, low = split_ids(order_ref, c, points)
        ordered_ref[:, c * 256 : (c + 1) * 256] = pick(stacked[...], one_hot(low), high, columns).astype(BF)

    copies[2].wait()
    mine = (iota((256, 512), 0) & 7) == (iota((256, 512), 1) >> 6)
    for g in range(points // 512):
        one = basis_ref[:, g * 512 : (g + 1) * 512].astype(F32)
        eight = jnp.broadcast_to(one[:, None, :], (rank, 8, 512)).reshape(256, 512)
        masked = jnp.where(mine, eight, 0.0).astype(BF)
        masked_ref[g] = masked
        coeffs = dot(ordered_ref[:, g * 512 : (g + 1) * 512], masked, NT).astype(BF)
        message_ref[:, 2 * halo + g * 256 : 2 * halo + (g + 1) * 256] = coeffs
    message_ref[:, :halo] = ordered_ref[:, :halo]
    message_ref[:, halo : 2 * halo] = ordered_ref[:, points - halo :]


def lift_kernel(message_ref, transfer_ref, lifted_ref, top_ref, weights_ref, rows32):
    rank = 32
    base = 2 * REACH * 64

    lane, row = iota((128, 256), 1), iota((128, 256), 0)
    family = (lane & 7) == ((row >> 1) & 7)
    spread = [
        jnp.where(iota((128, 256), 0) == (iota((128, 256), 1) >> 3) + 32 * q, 1.0, 0.0).astype(BF)
        for q in range(4)
    ]
    for m in range(rank // 4):
        turned = pad_lanes(transfer_ref[m * 4 * rank : (m + 1) * 4 * rank, :].astype(F32)).T.astype(BF)
        for q in range(4):
            rows32[m * 4 + q] = jnp.where(family, dot(turned, spread[q], NN), 0.0)
    for k in range(16):
        weights_ref[k] = rows32[:, k * 8 : k * 8 + 8, :].reshape(256, 256).astype(BF)
    coeffs = [message_ref[:, base + g * 256 : base + (g + 1) * 256] for g in range(8)] + [None] * 8
    for n in range(7):
        lifted = dot(coeffs[2 * n], weights_ref[2 * n], NN) + dot(coeffs[2 * n + 1], weights_ref[2 * n + 1], NN)
        coeffs[8 + n] = lifted.astype(BF)
    four = dot(coeffs[14], weights_ref[14], NN)
    five = dot(four.astype(BF), weights_ref[15], NN)
    six = dot((four + five).astype(BF), weights_ref[15], NN)
    coeffs[15] = (four + six).astype(BF)
    width = top_ref.shape[1]
    slot = lax.axis_index("leaf") // 2 * rank
    row, lane = iota((256, width), 0), iota((256, width), 1) - slot
    root = jnp.where((row == lane * 8 + 6) & (lane >= 0), 1.0, 0.0).astype(BF)
    top_ref[...] = dot(coeffs[15], root, NN).astype(BF)
    for g in range(8):
        lifted_ref[:, g * 256 : (g + 1) * 256] = coeffs[8 + g]


def lane_numbers(rows):
    return iota((rows, 128), 1).astype(F32).astype(BF)


def near_group(leaves_ref, lists_ref, blocks, first, base, columns):
    lane_left = lane_numbers(columns) < 64
    picked = []
    for i in range(4):
        spots = [lists_ref[s, first + i] - base for s in range(4)]
        halves = []
        for s in (0, 2):
            even = leaves_ref[spots[s]]
            odd = leaves_ref[spots[s + 1] ^ 1]
            halves.append(jnp.where(lane_left, even, odd))
        picked.append(jnp.concatenate(halves, axis=1))
    out = dot(jnp.concatenate(picked, axis=0), blocks, NT)
    leaf_of_lane = iota((columns, 256), 1) >> 6
    total = out[:columns]
    for i in range(1, 4):
        total = jnp.where(leaf_of_lane == i, out[i * columns : (i + 1) * columns], total)
    return total


def place_leaves(leaves_ref, first, chunk):
    leaves_ref[first] = chunk
    leaves_ref[first + 1] = pltpu.roll(chunk.astype(F32), 64, 1).astype(BF)


def matrices_kernel(
    coupling_ref, lists_ref, order_ref, matrices_ref, spots_ref, hot_ref, blocks_ref, rows32,
):
    rank = 32
    device = lax.axis_index("leaf")
    count = 64
    chunks = hot_ref.shape[0]

    within = iota((16, 256), 1).astype(F32)
    inverse = jnp.zeros((32, 256), F32)
    for c in range(chunks):
        high, low = split_ids(order_ref, c, chunks * 256)
        hit = iota((16, 256), 0) == jnp.broadcast_to(high, (16, 256))
        marks = jnp.concatenate([jnp.where(hit, float(c), 0.0), jnp.where(hit, within, 0.0)], axis=0)
        inverse = inverse + dot(marks.astype(BF), one_hot(low), NT)
    inverse = inverse.astype(jnp.int32)
    blocks_ref[...] = inverse[:16]
    for c in range(chunks):
        hot_ref[c] = one_hot(inverse[16 + c : 17 + c, :])

    node = iota((1, 128), 1)
    size = jnp.full((1, 128), count, jnp.int32)
    start = jnp.zeros((1, 128), jnp.int32)
    offset = 0
    for level in range(LEVELS):
        size = jnp.where(node >= offset, count >> level, size)
        start = jnp.where(node >= offset, offset, start)
        offset += count >> level
    entries = pad_lanes(lists_ref[...])
    for s in range(6):
        entry = entries[s : s + 1]
        place = entry - device * size + size
        side = jnp.where(place >= size, 1, 0) + jnp.where(place >= 2 * size, 1, 0)
        spot = side * 128 + start + place - side * size
        used = (entry >= 0) & (node < offset)
        spots_ref[pl.ds(s, 1), :] = jnp.where(used, spot, 3 * 128)
    spots_ref[pl.ds(6, 2), :] = jnp.zeros((2, 128), jnp.int32)

    for a in range(rank):
        one = [coupling_ref[s, a * rank : (a + 1) * rank, :].astype(F32) for s in range(6)]
        full = pad_lanes(jnp.concatenate(one, axis=0))
        turned = jnp.concatenate([full[:128].T, pad_lanes(full[128:].T)], axis=1)
        rows32[a] = turned
    for g in range(16):
        matrices_ref[g] = rows32[:, g * 8 : g * 8 + 8, :].reshape(256, 256).astype(BF)


def near_kernel(ordered_ref, blocks_ref, near_ref, near_out, leaves):
    columns, points = ordered_ref.shape
    count = blocks_ref.shape[0]
    device = lax.axis_index("leaf")
    for c in range(count // 2):
        place_leaves(leaves, c * 2, ordered_ref[:, c * 128 : (c + 1) * 128])
    edge = REACH // 4
    near_out[:, : edge * 256] = jnp.zeros((columns, edge * 256), F32)
    near_out[:, points - edge * 256 :] = jnp.zeros((columns, edge * 256), F32)

    def near(g, carry):
        blocks = blocks_ref[pl.ds(g * 4, 4)].reshape(256, 256)
        at = pl.multiple_of(g * 256, 256)
        near_out[:, pl.ds(at, 256)] = near_group(
            leaves, near_ref, blocks, g * 4, device * count, columns
        )
        return carry

    lax.fori_loop(edge, count // 4 - edge, near, 0, unroll=4)


def root_kernel(own_ref, other_ref, transfer_ref, coupling_ref, lists_ref, six_ref, coeffs):
    columns, rank = own_ref.shape[0], 32
    node_count = lists_ref.shape[1] // 2 + 1
    device = lax.axis_index("leaf")
    total = 2 * node_count - 1
    coeffs[total] = jnp.zeros((columns, rank), F32)
    for q in range(node_count):
        ref = own_ref if q % 2 == 0 else other_ref
        at = q // 2 * rank
        coeffs[q ^ (device & 1)] = ref[:, at : at + rank].astype(F32)
    values = [coeffs[j].astype(BF) for j in range(node_count)]
    start, count = 0, node_count
    starts = [(0, node_count)]
    while count > 1:
        for j in range(count // 2):
            left, right = start + 2 * j, start + 2 * j + 1
            lifted = dot(values[left], transfer_ref[left], NN) + dot(values[right], transfer_ref[right], NN)
            values.append(lifted.astype(BF))
            coeffs[start + count + j] = values[-1].astype(F32)
        start, count = start + count, count // 2
        starts.append((start, count))
    fields = []
    for level, (start, count) in enumerate(starts):
        node = start + (device >> level)
        field = None
        for s in range(6):
            entry = lists_ref[s, node]
            spot = jnp.where(entry >= 0, start + entry, total)
            term = dot(coeffs[spot].astype(BF), coupling_ref[s, node], NT)
            field = term if field is None else field + term
        fields.append((node, field))
    down = fields.pop()[1].astype(BF)
    for node, field in reversed(fields):
        down = (field + dot(down, transfer_ref[node], NT)).astype(BF)
    sixth = jnp.where(iota((32, 256), 1) == iota((32, 256), 0) * 8 + 6, 1.0, 0.0).astype(BF)
    six_ref[...] = dot(down, sixth, NN)


def outer_kernel(
    ordered_ref, own0_ref, own1_ref, first0_ref, first1_ref, second0_ref, second1_ref, near_in, blocks_ref,
    near_ref, matrices_ref, spots_ref, inverse_ref, weights_ref, masked_ref, hot_ref, six_ref,
    applied_hbm,
    applied_ref, leaves, nodes, far, stacked, stacked_nodes, edges, sems, out_sems,
):
    columns, points = ordered_ref.shape
    halo = REACH * 64
    device = lax.axis_index("leaf")
    count = points // 64
    copies = [
        pltpu.make_async_copy(blocks_ref.at[pl.ds(at, REACH)], edges.at[i], sems.at[i])
        for i, at in enumerate((0, count - REACH))
    ]
    for copy in copies:
        copy.start()

    odd = device % 2
    for ref, right in ((first0_ref, 1 - odd), (second0_ref, odd)):
        for c in range(halo // 128):
            at = pl.multiple_of((1 - right) * halo + c * 128, 128)
            place_leaves(leaves, right * (REACH + count) + c * 2, ref[:, pl.ds(at, 128)])
    near_ends = REACH * 64 * 2 // 128
    for c in list(range(near_ends)) + list(range(count // 2 - near_ends, count // 2)):
        place_leaves(leaves, REACH + c * 2, ordered_ref[:, c * 128 : (c + 1) * 128])

    nodes[3 * 128] = jnp.zeros((columns, 128), BF)
    lane, row = iota((256, 1024), 1), iota((256, 1024), 0)
    spread = jnp.where(row == (lane & 31) * 8 + (lane >> 7), 1.0, 0.0).astype(BF)
    sources = (
        (1, own0_ref, own1_ref), (2 - 2 * odd, first0_ref, first1_ref), (2 * odd, second0_ref, second1_ref),
    )
    for side, ref0, ref1 in sources:
        for n in range(8):
            at = 2 * halo + n * 256
            stacked_nodes[n * columns : (n + 1) * columns, :] = ref0[:, at : at + 256]
            stacked_nodes[(8 + n) * columns : (9 + n) * columns, :] = ref1[:, n * 256 : (n + 1) * 256]
        for c in range(0, 8, 2):
            out = dot(stacked_nodes[...], spread[:, c * 128 : (c + 2) * 128], NN)
            for n in range(16):
                both = out[n * columns : (n + 1) * columns].astype(BF)
                nodes[side * 128 + n * 8 + c] = both[:, :128]
                nodes[side * 128 + n * 8 + c + 1] = both[:, 128:]

    lane = lane_numbers(columns)
    lane_node = iota((columns, 256), 1) & 7

    for g in range(16):
        picked = []
        for i in range(8):
            parts = [nodes[spots_ref[s, g * 8 + i]] for s in range(6)]
            front = jnp.where(lane < 32, parts[0], parts[1])
            front = jnp.where(lane < 64, front, jnp.where(lane < 96, parts[2], parts[3]))
            back = jnp.where(lane < 32, parts[4], parts[5])
            back = jnp.where(lane < 64, back, jnp.zeros((), BF))
            picked.append(jnp.concatenate([front, back], axis=1))
        out = dot(jnp.concatenate(picked, axis=0), matrices_ref[g], NT)
        total = out[:columns]
        for i in range(1, 8):
            total = jnp.where(lane_node == i, out[i * columns : (i + 1) * columns], total)
        far[:, g * 256 : (g + 1) * 256] = total

    for copy in copies:
        copy.wait()
    six = six_ref[...]
    down = [None] * 16
    last = far[:, 15 * 256 :]
    five = last + dot(six.astype(BF), weights_ref[15], NT)
    five = jnp.where(lane_node >= 4, five, 0.0) + six
    down[15] = (last + dot(five.astype(BF), weights_ref[15], NT)).astype(BF)
    for k in reversed(range(15)):
        down[k] = (far[:, k * 256 : (k + 1) * 256] + dot(down[8 + k // 2], weights_ref[k], NT)).astype(BF)
    groups = count // 4
    edge = REACH // 4
    for g in range(groups):
        if g < edge:
            blocks = edges[0, g * 4 : g * 4 + 4].reshape(256, 256)
        elif g >= groups - edge:
            at = (g - groups + edge) * 4
            blocks = edges[1, at : at + 4].reshape(256, 256)
        else:
            blocks = None
        if blocks is None:
            near = near_in[:, g * 256 : (g + 1) * 256]
        else:
            near = near_group(leaves, near_ref, blocks, g * 4, device * count - REACH, columns)
        if g % 2 == 0:
            at_points = dot(down[g // 2], masked_ref[g // 2], NN)
        half = at_points[:, g % 2 * 256 : (g % 2 + 1) * 256]
        stacked[g * columns : (g + 1) * columns, :] = (near + half).astype(BF)

    writes = []
    for c in range(points // 256):
        applied_ref[:, c * 256 : (c + 1) * 256] = pick(
            stacked[...], hot_ref[c], inverse_ref[c : c + 1, :], columns
        )
        if c % 4 == 3:
            at = pl.ds((c - 3) * 256, 1024)
            writes.append(pltpu.make_async_copy(applied_ref.at[:, at], applied_hbm.at[:, at], out_sems.at[c // 4]))
            writes[-1].start()
    for write in writes:
        write.wait()


VMEM = pl.BlockSpec(memory_space=pltpu.VMEM)
SMEM = pl.BlockSpec(memory_space=pltpu.SMEM)


def in_hbm(x):
    return pltpu.with_memory_space_constraint(x, pltpu.HBM)


def call(kernel, outs, scratch, specs, flops, name, args, mib=16, out_specs=None):
    size = sum(a.size * a.dtype.itemsize for a in args)
    return pl.pallas_call(
        kernel,
        out_shape=[jax.ShapeDtypeStruct(s, t) for s, t in outs],
        in_specs=specs,
        out_specs=out_specs or [VMEM] * len(outs),
        scratch_shapes=scratch,
        compiler_params=pltpu.CompilerParams(vmem_limit_bytes=mib * 2**20),
        cost_estimate=pl.CostEstimate(flops=flops, bytes_accessed=0, transcendentals=0),
        name=name,
    )(*args)


def local(
    vectors, tree_order, leaf_basis, near_blocks, near_lists, transfers, couplings, coupling_lists,
    top_transfers, top_couplings, top_lists,
):
    columns, points = vectors.shape
    rank = leaf_basis.shape[0]
    devices = lax.axis_size("leaf")
    halo = REACH * near_blocks.shape[1]
    order = tree_order.reshape(points // 128, 128)
    near_t = jnp.transpose(near_lists)
    lists_t = jnp.transpose(coupling_lists)
    moves = transfers.reshape(rank * rank, -1)
    matrices = couplings.reshape(6, rank * rank, -1)

    any_spec = pl.BlockSpec(memory_space=pl.ANY)
    tile = max(devices // 2 * rank, 128)
    ordered, own0, masked = call(
        leaf_kernel,
        [((columns, points), BF), ((columns, 2 * halo + 2048), BF), ((points // 512, 256, 512), BF)],
        [
            pltpu.VMEM(vectors.shape, BF), pltpu.VMEM(order.shape, jnp.int32),
            pltpu.VMEM(leaf_basis.shape, BF), pltpu.VMEM((points // 256 * columns, 256), BF),
            pltpu.SemaphoreType.DMA((3,)),
        ],
        [any_spec] * 3, 10**9, "leaf", tuple(in_hbm(x) for x in (vectors, order, leaf_basis)),
    )
    pairs = [(i, i ^ 1) for i in range(devices)]
    onward = [(i, i + 2) for i in range(0, devices - 2, 2)] + [(i, i - 2) for i in range(3, devices, 2)]
    first0 = lax.ppermute(own0, "leaf", pairs)
    own1, top, weights = call(
        lift_kernel,
        [((columns, 2048), BF), ((columns, tile), BF), ((16, 256, 256), BF)],
        [pltpu.VMEM((rank, 128, 256), F32)], [VMEM, VMEM], 10**9, "lift", (own0, moves),
    )
    first1 = lax.ppermute(own1, "leaf", pairs)

    def step(tile_sum, reached):
        return lax.ppermute(tile_sum, "leaf", [(i, i ^ reached) for i in range(devices)])

    steps = [1 << k for k in reversed(range(1, devices.bit_length() - 1))]
    for reached in steps[:-2]:
        top = top + step(top, reached)
    other = step(top, steps[-2])
    coupling_rows, spots, hot, blocks = call(
        matrices_kernel,
        [
            ((16, 256, 256), BF), ((8, 128), jnp.int32), ((points // 256, 256, 256), BF),
            ((points // 256, 256), jnp.int32),
        ],
        [pltpu.VMEM((rank, 128, 256), F32)],
        [VMEM] * 3, 10**6, "matrices", (matrices, lists_t, order),
    )
    first0, blocks, other = lax.optimization_barrier((first0, blocks, other))
    second0 = lax.ppermute(first0, "leaf", onward)
    top = top + other
    other = step(top, steps[-1])
    first1, other = lax.optimization_barrier((first1, other))
    top = top + other
    second1 = lax.ppermute(first1, "leaf", onward)
    other = step(top, 1)
    first1, ordered_late = lax.optimization_barrier((first1, ordered))
    (near_part,) = call(
        near_kernel, [((columns, points), F32)],
        [pltpu.VMEM((points // 64, columns, 128), BF)],
        [VMEM, VMEM, SMEM], 10**6, "near", (ordered_late, near_blocks, near_t),
    )
    other, near_part = lax.optimization_barrier((other, near_part))
    (six,) = call(
        root_kernel, [((columns, 256), F32)], [pltpu.VMEM((2 * devices, columns, 32), F32)],
        [VMEM] * 4 + [SMEM], 10**6, "root",
        (
            top, other, jnp.transpose(top_transfers, (2, 0, 1)), jnp.transpose(top_couplings, (0, 3, 1, 2)),
            jnp.transpose(top_lists),
        ),
    )
    (applied,) = call(
        outer_kernel,
        [((columns, points), F32)],
        [
            pltpu.VMEM((columns, points), F32), pltpu.VMEM((points // 64 + 2 * REACH, columns, 128), BF),
            pltpu.VMEM((385, columns, 128), BF), pltpu.VMEM((columns, 4096), F32),
            pltpu.VMEM((points // 256 * columns, 256), BF), pltpu.VMEM((16 * columns, 256), BF),
            pltpu.VMEM((2, REACH) + near_blocks.shape[1:], BF), pltpu.SemaphoreType.DMA((2,)),
            pltpu.SemaphoreType.DMA((points // 1024,)),
        ],
        [VMEM] * 8 + [any_spec, SMEM, VMEM, SMEM] + [VMEM] * 5,
        4 * 10**9, "outer",
        (
            ordered, own0, own1, first0, first1, second0, second1, near_part, in_hbm(near_blocks),
            near_t, coupling_rows, spots, blocks, weights, masked, hot, six,
        ),
        out_specs=[any_spec],
    )
    return applied


def solution(mesh):
    placed = (
        P("rhs", ("groups", "leaf")),
        P(("groups", "leaf")),
        P(None, ("groups", "leaf")),
        P(("groups", "leaf"), None, None),
        P(("groups", "leaf"), None),
        P(None, None, ("groups", "leaf")),
        P(None, None, None, ("groups", "leaf")),
        P(("groups", "leaf"), None),
        P(None, None, "groups"),
        P(None, None, None, "groups"),
        P("groups", None),
    )
    return jax.shard_map(
        local, mesh=mesh, in_specs=placed, out_specs=P("rhs", ("groups", "leaf")), check_vma=False
    )
```

```python
import functools

import jax
import jax.numpy as jnp
from jax import lax
from jax.experimental import pallas as pl
from jax.experimental.pallas import tpu as pltpu
from jax.sharding import PartitionSpec as P

LEVELS = 6
REACH = 8
BF = jnp.bfloat16
F32 = jnp.float32
NT = (((1,), (1,)), ((), ()))
NN = (((1,), (0,)), ((), ()))


def iota(shape, axis):
    return lax.broadcasted_iota(jnp.int32, shape, axis)


def dot(a, b, dims):
    return lax.dot_general(a, b, dims, preferred_element_type=F32)


def pad_lanes(x):
    short = 128 - x.shape[1]
    return jnp.concatenate([x, jnp.zeros((x.shape[0], short), x.dtype)], axis=1)


def one_hot(ids):
    ids = jnp.broadcast_to(ids.astype(F32), (16, 256)).astype(BF)
    rows = iota((256, 256), 0).astype(F32).astype(BF)
    return jnp.where(rows == jnp.concatenate([ids] * 16, axis=0), jnp.ones((), BF), jnp.zeros((), BF))


def split_ids(order_ref, c, points):
    ids = jnp.concatenate([order_ref[2 * c : 2 * c + 1, :], order_ref[2 * c + 1 : 2 * c + 2, :]], axis=1)
    ids = lax.rem(ids, points)
    return ids >> 8, ids & 255


def pick(stacked, hot, high, rows):
    out = dot(stacked, hot, NN)
    high = jnp.broadcast_to(high, (rows, 256))
    total = out[:rows]
    for block in range(1, stacked.shape[0] // rows):
        total = jnp.where(high == block, out[block * rows : (block + 1) * rows], total)
    return total


def leaf_kernel(
    vec_hbm, order_hbm, basis_hbm, ordered_ref, zero_ref, masked_hbm,
    vec_ref, order_ref, basis_ref, stacked, masked_ref, sems, out_sems,
):
    columns, points = vec_ref.shape
    rank = basis_ref.shape[0]
    pairs = ((order_hbm, order_ref), (vec_hbm, vec_ref), (basis_hbm, basis_ref))
    copies = [pltpu.make_async_copy(src, dst, sems.at[i]) for i, (src, dst) in enumerate(pairs)]
    for copy in copies:
        copy.start()
    copies[0].wait()
    copies[1].wait()
    for block in range(points // 256):
        stacked[block * columns : (block + 1) * columns, :] = vec_ref[:, block * 256 : (block + 1) * 256]
    for c in range(points // 256):
        high, low = split_ids(order_ref, c, points)
        ordered_ref[:, c * 256 : (c + 1) * 256] = pick(stacked[...], one_hot(low), high, columns).astype(BF)

    copies[2].wait()
    mine = (iota((256, 512), 0) & 7) == (iota((256, 512), 1) >> 6)
    writes = []
    for g in range(points // 512):
        one = basis_ref[:, g * 512 : (g + 1) * 512].astype(F32)
        eight = jnp.broadcast_to(one[:, None, :], (rank, 8, 512)).reshape(256, 512)
        masked = jnp.where(mine, eight, 0.0).astype(BF)
        masked_ref[g] = masked
        writes.append(pltpu.make_async_copy(masked_ref.at[g], masked_hbm.at[g], out_sems.at[g]))
        writes[-1].start()
        coeffs = dot(ordered_ref[:, g * 512 : (g + 1) * 512], masked, NT).astype(BF)
        zero_ref[:, g * 256 : (g + 1) * 256] = coeffs
    for write in writes:
        write.wait()


def lift_kernel(
    zero_ref, ordered_ref, transfer_ref, first_ref, second_ref, copies_ref, weights_hbm,
    rows32, weights_ref, sem,
):
    rank = 32
    base = REACH * 64
    points = ordered_ref.shape[1]

    lane, row = iota((128, 256), 1), iota((128, 256), 0)
    family = (lane & 7) == ((row >> 1) & 7)
    spread = [
        jnp.where(iota((128, 256), 0) == (iota((128, 256), 1) >> 3) + 32 * q, 1.0, 0.0).astype(BF)
        for q in range(4)
    ]
    for m in range(rank // 4):
        turned = pad_lanes(transfer_ref[m * 4 * rank : (m + 1) * 4 * rank, :].astype(F32)).T.astype(BF)
        for q in range(4):
            rows32[m * 4 + q] = jnp.where(family, dot(turned, spread[q], NN), 0.0)
    for k in range(16):
        weights_ref[k] = rows32[:, k * 8 : k * 8 + 8, :].reshape(256, 256).astype(BF)
    write = pltpu.make_async_copy(weights_ref, weights_hbm, sem)
    write.start()
    coeffs = [zero_ref[:, g * 256 : (g + 1) * 256] for g in range(8)] + [None] * 8
    for n in range(7):
        lifted = dot(coeffs[2 * n], weights_ref[2 * n], NN) + dot(coeffs[2 * n + 1], weights_ref[2 * n + 1], NN)
        coeffs[8 + n] = lifted.astype(BF)
    four = dot(coeffs[14], weights_ref[14], NN)
    five = dot(four.astype(BF), weights_ref[15], NN)
    six = dot((four + five).astype(BF), weights_ref[15], NN)
    coeffs[15] = (four + six).astype(BF)
    root = jnp.where(iota((256, 128), 0) == iota((256, 128), 1) * 8 + 6, 1.0, 0.0).astype(BF)
    tile = dot(coeffs[15], root, NN).astype(BF)
    for q in range(copies_ref.shape[0]):
        copies_ref[q] = tile
    odd = lax.axis_index("leaf") % 2 == 1
    low, high = ordered_ref[:, :base], ordered_ref[:, points - base :]
    first_ref[:, :base] = jnp.where(odd, low, high)
    second_ref[:, :base] = jnp.where(odd, high, low)
    for g in range(16):
        first_ref[:, base + g * 256 : base + (g + 1) * 256] = coeffs[g]
        second_ref[:, base + g * 256 : base + (g + 1) * 256] = coeffs[g]
    write.wait()


def lane_numbers(rows):
    return iota((rows, 128), 1).astype(F32).astype(BF)


def near_group(leaves_ref, lists_ref, blocks, first, base, columns):
    lane_left = lane_numbers(columns) < 64
    picked = []
    for i in range(4):
        spots = [lists_ref[s, first + i] - base for s in range(4)]
        halves = []
        for s in (0, 2):
            even = leaves_ref[spots[s]]
            odd = leaves_ref[spots[s + 1] ^ 1]
            halves.append(jnp.where(lane_left, even, odd))
        picked.append(jnp.concatenate(halves, axis=1))
    out = dot(jnp.concatenate(picked, axis=0), blocks, NT)
    leaf_of_lane = iota((columns, 256), 1) >> 6
    total = out[:columns]
    for i in range(1, 4):
        total = jnp.where(leaf_of_lane == i, out[i * columns : (i + 1) * columns], total)
    return total


def place_leaves(leaves_ref, first, chunk):
    leaves_ref[first] = chunk
    leaves_ref[first + 1] = pltpu.roll(chunk.astype(F32), 64, 1).astype(BF)


def matrices_kernel(
    coupling_ref, lists_ref, order_ref, matrices_ref, spots_ref, hot_ref, blocks_ref, rows32,
):
    rank = 32
    device = lax.axis_index("leaf")
    count = 64
    chunks = hot_ref.shape[0]

    within = iota((16, 256), 1).astype(F32)
    inverse = jnp.zeros((32, 256), F32)
    for c in range(chunks):
        high, low = split_ids(order_ref, c, chunks * 256)
        hit = iota((16, 256), 0) == jnp.broadcast_to(high, (16, 256))
        marks = jnp.concatenate([jnp.where(hit, float(c), 0.0), jnp.where(hit, within, 0.0)], axis=0)
        inverse = inverse + dot(marks.astype(BF), one_hot(low), NT)
    inverse = inverse.astype(jnp.int32)
    blocks_ref[...] = inverse[:16]
    for c in range(chunks):
        hot_ref[c] = one_hot(inverse[16 + c : 17 + c, :])

    node = iota((1, 128), 1)
    size = jnp.full((1, 128), count, jnp.int32)
    start = jnp.zeros((1, 128), jnp.int32)
    offset = 0
    for level in range(LEVELS):
        size = jnp.where(node >= offset, count >> level, size)
        start = jnp.where(node >= offset, offset, start)
        offset += count >> level
    entries = pad_lanes(lists_ref[...])
    for s in range(6):
        entry = entries[s : s + 1]
        place = entry - device * size + size
        side = jnp.where(place >= size, 1, 0) + jnp.where(place >= 2 * size, 1, 0)
        spot = side * 128 + start + place - side * size
        used = (entry >= 0) & (node < offset)
        spots_ref[pl.ds(s, 1), :] = jnp.where(used, spot, 3 * 128)
    spots_ref[pl.ds(6, 2), :] = jnp.zeros((2, 128), jnp.int32)

    for a in range(rank):
        one = [coupling_ref[s, a * rank : (a + 1) * rank, :].astype(F32) for s in range(6)]
        full = pad_lanes(jnp.concatenate(one, axis=0))
        turned = jnp.concatenate([full[:128].T, pad_lanes(full[128:].T)], axis=1)
        rows32[a] = turned
    for g in range(16):
        matrices_ref[g] = rows32[:, g * 8 : g * 8 + 8, :].reshape(256, 256).astype(BF)


def near_kernel(ordered_ref, blocks_ref, near_ref, near_out, leaves):
    columns, points = ordered_ref.shape
    count = blocks_ref.shape[0]
    device = lax.axis_index("leaf")
    for c in range(count // 2):
        place_leaves(leaves, c * 2, ordered_ref[:, c * 128 : (c + 1) * 128])
    edge = REACH // 4
    near_out[:, : edge * 256] = jnp.zeros((columns, edge * 256), F32)
    near_out[:, points - edge * 256 :] = jnp.zeros((columns, edge * 256), F32)

    def near(g, carry):
        blocks = blocks_ref[pl.ds(g * 4, 4)].reshape(256, 256)
        at = pl.multiple_of(g * 256, 256)
        near_out[:, pl.ds(at, 256)] = near_group(
            leaves, near_ref, blocks, g * 4, device * count, columns
        )
        return carry

    lax.fori_loop(edge, count // 4 - edge, near, 0, unroll=4)


def root_kernel(gathered_ref, transfer_ref, coupling_ref, lists_ref, six_ref, coeffs):
    node_count, columns = gathered_ref.shape[:2]
    device = lax.axis_index("leaf")
    total = 2 * node_count - 1
    coeffs[total] = jnp.zeros((columns, 32), F32)
    values = [gathered_ref[q][:, :32] for q in range(node_count)]
    for q in range(node_count):
        coeffs[q] = values[q].astype(F32)
    start, count = 0, node_count
    starts = [(0, node_count)]
    while count > 1:
        for j in range(count // 2):
            left, right = start + 2 * j, start + 2 * j + 1
            lifted = dot(values[left], transfer_ref[left], NN) + dot(values[right], transfer_ref[right], NN)
            values.append(lifted.astype(BF))
            coeffs[start + count + j] = values[-1].astype(F32)
        start, count = start + count, count // 2
        starts.append((start, count))
    fields = []
    for level, (start, count) in enumerate(starts):
        node = start + (device >> level)
        field = None
        for s in range(6):
            entry = lists_ref[s, node]
            spot = jnp.where(entry >= 0, start + entry, total)
            term = dot(coeffs[spot].astype(BF), coupling_ref[s, node], NT)
            field = term if field is None else field + term
        fields.append((node, field))
    down = fields.pop()[1].astype(BF)
    for node, field in reversed(fields):
        down = (field + dot(down, transfer_ref[node], NT)).astype(BF)
    sixth = jnp.where(iota((32, 256), 1) == iota((32, 256), 0) * 8 + 6, 1.0, 0.0).astype(BF)
    six_ref[...] = dot(down, sixth, NN)


def outer_kernel(
    ordered_ref, own_ref, first_ref, second_ref, near_in, blocks_ref,
    near_ref, matrices_ref, spots_ref, inverse_ref, weights_hbm, masked_hbm, hot_ref, six_ref,
    applied_hbm,
    applied_ref, leaves, nodes, far, stacked, stacked_nodes, edges, weights_ref, masked_ref, sems, out_sems,
):
    columns, points = ordered_ref.shape
    halo = REACH * 64
    device = lax.axis_index("leaf")
    count = points // 64
    copies = [
        pltpu.make_async_copy(blocks_ref.at[pl.ds(at, REACH)], edges.at[i], sems.at[i])
        for i, at in enumerate((0, count - REACH))
    ]
    copies.append(pltpu.make_async_copy(weights_hbm, weights_ref, sems.at[2]))
    copies.append(pltpu.make_async_copy(masked_hbm, masked_ref, sems.at[3]))
    for copy in copies:
        copy.start()

    odd = device % 2
    for ref, right in ((first_ref, 1 - odd), (second_ref, odd)):
        for c in range(halo // 128):
            place_leaves(leaves, right * (REACH + count) + c * 2, ref[:, c * 128 : (c + 1) * 128])
    near_ends = REACH * 64 * 2 // 128
    for c in list(range(near_ends)) + list(range(count // 2 - near_ends, count // 2)):
        place_leaves(leaves, REACH + c * 2, ordered_ref[:, c * 128 : (c + 1) * 128])

    nodes[3 * 128] = jnp.zeros((columns, 128), BF)
    lane, row = iota((256, 1024), 1), iota((256, 1024), 0)
    spread = jnp.where(row == (lane & 31) * 8 + (lane >> 7), 1.0, 0.0).astype(BF)
    for side, ref in ((1, own_ref), (2 - 2 * odd, first_ref), (2 * odd, second_ref)):
        for n in range(16):
            stacked_nodes[n * columns : (n + 1) * columns, :] = ref[:, halo + n * 256 : halo + (n + 1) * 256]
        for c in range(0, 8, 2):
            out = dot(stacked_nodes[...], spread[:, c * 128 : (c + 2) * 128], NN)
            for n in range(16):
                both = out[n * columns : (n + 1) * columns].astype(BF)
                nodes[side * 128 + n * 8 + c] = both[:, :128]
                nodes[side * 128 + n * 8 + c + 1] = both[:, 128:]

    lane = lane_numbers(columns)
    lane_node = iota((columns, 256), 1) & 7

    for g in range(16):
        picked = []
        for i in range(8):
            parts = [nodes[spots_ref[s, g * 8 + i]] for s in range(6)]
            front = jnp.where(lane < 32, parts[0], parts[1])
            front = jnp.where(lane < 64, front, jnp.where(lane < 96, parts[2], parts[3]))
            back = jnp.where(lane < 32, parts[4], parts[5])
            back = jnp.where(lane < 64, back, jnp.zeros((), BF))
            picked.append(jnp.concatenate([front, back], axis=1))
        out = dot(jnp.concatenate(picked, axis=0), matrices_ref[g], NT)
        total = out[:columns]
        for i in range(1, 8):
            total = jnp.where(lane_node == i, out[i * columns : (i + 1) * columns], total)
        far[:, g * 256 : (g + 1) * 256] = total

    for copy in copies:
        copy.wait()
    six = six_ref[...]
    down = [None] * 16
    last = far[:, 15 * 256 :]
    five = last + dot(six.astype(BF), weights_ref[15], NT)
    five = jnp.where(lane_node >= 4, five, 0.0) + six
    down[15] = (last + dot(five.astype(BF), weights_ref[15], NT)).astype(BF)
    for k in reversed(range(15)):
        down[k] = (far[:, k * 256 : (k + 1) * 256] + dot(down[8 + k // 2], weights_ref[k], NT)).astype(BF)
    groups = count // 4
    edge = REACH // 4
    for g in range(groups):
        if g < edge:
            blocks = edges[0, g * 4 : g * 4 + 4].reshape(256, 256)
        elif g >= groups - edge:
            at = (g - groups + edge) * 4
            blocks = edges[1, at : at + 4].reshape(256, 256)
        else:
            blocks = None
        if blocks is None:
            near = near_in[:, g * 256 : (g + 1) * 256]
        else:
            near = near_group(leaves, near_ref, blocks, g * 4, device * count - REACH, columns)
        if g % 2 == 0:
            at_points = dot(down[g // 2], masked_ref[g // 2], NN)
        half = at_points[:, g % 2 * 256 : (g % 2 + 1) * 256]
        stacked[g * columns : (g + 1) * columns, :] = (near + half).astype(BF)

    writes = []
    for c in range(points // 256):
        applied_ref[:, c * 256 : (c + 1) * 256] = pick(
            stacked[...], hot_ref[c], inverse_ref[c : c + 1, :], columns
        )
        if c % 4 == 3:
            at = pl.ds((c - 3) * 256, 1024)
            writes.append(pltpu.make_async_copy(applied_ref.at[:, at], applied_hbm.at[:, at], out_sems.at[c // 4]))
            writes[-1].start()
    for write in writes:
        write.wait()


VMEM = pl.BlockSpec(memory_space=pltpu.VMEM)
SMEM = pl.BlockSpec(memory_space=pltpu.SMEM)


def in_hbm(x):
    return pltpu.with_memory_space_constraint(x, pltpu.HBM)


def call(kernel, outs, scratch, specs, flops, name, args, mib=16, out_specs=None):
    size = sum(a.size * a.dtype.itemsize for a in args)
    return pl.pallas_call(
        kernel,
        out_shape=[jax.ShapeDtypeStruct(*o) if isinstance(o, tuple) else o for o in outs],
        in_specs=specs,
        out_specs=out_specs or [VMEM] * len(outs),
        scratch_shapes=scratch,
        compiler_params=pltpu.CompilerParams(vmem_limit_bytes=mib * 2**20),
        cost_estimate=pl.CostEstimate(flops=flops, bytes_accessed=0, transcendentals=0),
        name=name,
    )(*args)


def local(
    vectors, tree_order, leaf_basis, near_blocks, near_lists, transfers, couplings, coupling_lists,
    top_transfers, top_couplings, top_lists,
):
    columns, points = vectors.shape
    rank = leaf_basis.shape[0]
    devices = lax.axis_size("leaf")
    halo = REACH * near_blocks.shape[1]
    order = tree_order.reshape(points // 128, 128)
    near_t = jnp.transpose(near_lists)
    lists_t = jnp.transpose(coupling_lists)
    moves = transfers.reshape(rank * rank, -1)
    matrices = couplings.reshape(6, rank * rank, -1)

    any_spec = pl.BlockSpec(memory_space=pl.ANY)
    ordered, zero, masked = call(
        leaf_kernel,
        [((columns, points), BF), ((columns, 2048), BF), pltpu.HBM((points // 512, 256, 512), BF)],
        [
            pltpu.VMEM(vectors.shape, BF), pltpu.VMEM(order.shape, jnp.int32),
            pltpu.VMEM(leaf_basis.shape, BF), pltpu.VMEM((points // 256 * columns, 256), BF),
            pltpu.VMEM((points // 512, 256, 512), BF), pltpu.SemaphoreType.DMA((3,)),
            pltpu.SemaphoreType.DMA((points // 512,)),
        ],
        [any_spec] * 3, 10**9, "leaf", tuple(in_hbm(x) for x in (vectors, order, leaf_basis)),
        out_specs=[VMEM, VMEM, any_spec],
    )
    pairs = [(i, i ^ 1) for i in range(devices)]
    odds = [(i, i + 1) for i in range(1, devices - 1, 2)]
    to_first, to_second, copies, weights = call(
        lift_kernel,
        [
            ((columns, halo + 4096), BF), ((columns, halo + 4096), BF), ((devices, columns, 128), BF),
            pltpu.HBM((16, 256, 256), BF),
        ],
        [
            pltpu.VMEM((rank, 128, 256), F32), pltpu.VMEM((16, 256, 256), BF),
            pltpu.SemaphoreType.DMA(()),
        ],
        [VMEM] * 3, 10**6, "lift", (zero, ordered, moves), out_specs=[VMEM] * 3 + [any_spec],
    )
    first = lax.ppermute(to_first, "leaf", pairs)
    second = lax.ppermute(to_second, "leaf", odds + [(j, i) for i, j in odds])
    gathered = lax.all_to_all(copies, "leaf", 0, 0)
    gathered, order, ordered_late = lax.optimization_barrier((gathered, order, ordered))
    coupling_rows, spots, hot, blocks = call(
        matrices_kernel,
        [
            ((16, 256, 256), BF), ((8, 128), jnp.int32), ((points // 256, 256, 256), BF),
            ((points // 256, 256), jnp.int32),
        ],
        [pltpu.VMEM((rank, 128, 256), F32)],
        [VMEM] * 3, 10**6, "matrices", (matrices, lists_t, order),
    )
    (near_part,) = call(
        near_kernel, [((columns, points), F32)],
        [pltpu.VMEM((points // 64, columns, 128), BF)],
        [VMEM, VMEM, SMEM], 10**6, "near", (ordered_late, near_blocks, near_t),
    )
    (six,) = call(
        root_kernel, [((columns, 256), F32)], [pltpu.VMEM((2 * devices, columns, 32), F32)],
        [VMEM] * 3 + [SMEM], 10**6, "root",
        (
            gathered, jnp.transpose(top_transfers, (2, 0, 1)), jnp.transpose(top_couplings, (0, 3, 1, 2)),
            jnp.transpose(top_lists),
        ),
    )
    (applied,) = call(
        outer_kernel,
        [((columns, points), F32)],
        [
            pltpu.VMEM((columns, points), F32), pltpu.VMEM((points // 64 + 2 * REACH, columns, 128), BF),
            pltpu.VMEM((385, columns, 128), BF), pltpu.VMEM((columns, 4096), F32),
            pltpu.VMEM((points // 256 * columns, 256), BF), pltpu.VMEM((16 * columns, 256), BF),
            pltpu.VMEM((2, REACH) + near_blocks.shape[1:], BF), pltpu.VMEM((16, 256, 256), BF),
            pltpu.VMEM((points // 512, 256, 512), BF), pltpu.SemaphoreType.DMA((4,)),
            pltpu.SemaphoreType.DMA((points // 1024,)),
        ],
        [VMEM] * 5 + [any_spec, SMEM, VMEM, SMEM, VMEM, any_spec, any_spec, VMEM, VMEM],
        4 * 10**9, "outer",
        (
            ordered_late, to_first, first, second, near_part, in_hbm(near_blocks),
            near_t, coupling_rows, spots, blocks, in_hbm(weights), in_hbm(masked), hot, six,
        ),
        out_specs=[any_spec],
    )
    return applied


def solution(mesh):
    placed = (
        P("rhs", ("groups", "leaf")),
        P(("groups", "leaf")),
        P(None, ("groups", "leaf")),
        P(("groups", "leaf"), None, None),
        P(("groups", "leaf"), None),
        P(None, None, ("groups", "leaf")),
        P(None, None, None, ("groups", "leaf")),
        P(("groups", "leaf"), None),
        P(None, None, "groups"),
        P(None, None, None, "groups"),
        P("groups", None),
    )
    return jax.shard_map(
        local, mesh=mesh, in_specs=placed, out_specs=P("rhs", ("groups", "leaf")), check_vma=False
    )
```

```python
import functools

import jax
import jax.numpy as jnp
from jax import lax
from jax.experimental import pallas as pl
from jax.experimental.pallas import tpu as pltpu
from jax.sharding import PartitionSpec as P

LEVELS = 6
REACH = 8
BF = jnp.bfloat16
F32 = jnp.float32
NT = (((1,), (1,)), ((), ()))
NN = (((1,), (0,)), ((), ()))


def iota(shape, axis):
    return lax.broadcasted_iota(jnp.int32, shape, axis)


def dot(a, b, dims):
    return lax.dot_general(a, b, dims, preferred_element_type=F32)


def pad_lanes(x):
    short = 128 - x.shape[1]
    return jnp.concatenate([x, jnp.zeros((x.shape[0], short), x.dtype)], axis=1)


def one_hot(ids):
    ids = jnp.broadcast_to(ids.astype(F32), (16, 256)).astype(BF)
    rows = iota((256, 256), 0).astype(F32).astype(BF)
    return jnp.where(rows == jnp.concatenate([ids] * 16, axis=0), jnp.ones((), BF), jnp.zeros((), BF))


def split_ids(order_ref, c, points):
    ids = jnp.concatenate([order_ref[2 * c : 2 * c + 1, :], order_ref[2 * c + 1 : 2 * c + 2, :]], axis=1)
    ids = lax.rem(ids, points)
    return ids >> 8, ids & 255


def pick(stacked, hot, high, rows):
    out = dot(stacked, hot, NN)
    high = jnp.broadcast_to(high, (rows, 256))
    total = out[:rows]
    for block in range(1, stacked.shape[0] // rows):
        total = jnp.where(high == block, out[block * rows : (block + 1) * rows], total)
    return total


def leaf_kernel(
    vec_hbm, order_hbm, basis_hbm, ordered_ref, message_ref, masked_ref,
    vec_ref, order_ref, basis_ref, stacked, sems,
):
    columns, points = vec_ref.shape
    rank = basis_ref.shape[0]
    halo = REACH * 64
    pairs = ((order_hbm, order_ref), (vec_hbm, vec_ref), (basis_hbm, basis_ref))
    copies = [pltpu.make_async_copy(src, dst, sems.at[i]) for i, (src, dst) in enumerate(pairs)]
    for copy in copies:
        copy.start()
    copies[0].wait()
    copies[1].wait()
    for block in range(points // 256):
        stacked[block * columns : (block + 1) * columns, :] = vec_ref[:, block * 256 : (block + 1) * 256]
    for c in range(points // 256):
        high, low = split_ids(order_ref, c, points)
        ordered_ref[:, c * 256 : (c + 1) * 256] = pick(stacked[...], one_hot(low), high, columns).astype(BF)

    copies[2].wait()
    mine = (iota((256, 512), 0) & 7) == (iota((256, 512), 1) >> 6)
    for g in range(points // 512):
        one = basis_ref[:, g * 512 : (g + 1) * 512].astype(F32)
        eight = jnp.broadcast_to(one[:, None, :], (rank, 8, 512)).reshape(256, 512)
        masked = jnp.where(mine, eight, 0.0).astype(BF)
        masked_ref[g] = masked
        coeffs = dot(ordered_ref[:, g * 512 : (g + 1) * 512], masked, NT).astype(BF)
        message_ref[:, halo + g * 256 : halo + (g + 1) * 256] = coeffs
    odd = lax.axis_index("leaf") % 2 == 1
    message_ref[:, :halo] = jnp.where(odd, ordered_ref[:, :halo], ordered_ref[:, points - halo :])


def lift_kernel(
    message_ref, ordered_ref, transfer_ref, lifted_ref, second_ref, copies_ref, weights_ref, rows32,
):
    rank = 32
    base = REACH * 64
    points = ordered_ref.shape[1]

    lane, row = iota((128, 256), 1), iota((128, 256), 0)
    family = (lane & 7) == ((row >> 1) & 7)
    spread = [
        jnp.where(iota((128, 256), 0) == (iota((128, 256), 1) >> 3) + 32 * q, 1.0, 0.0).astype(BF)
        for q in range(4)
    ]
    for m in range(rank // 4):
        turned = pad_lanes(transfer_ref[m * 4 * rank : (m + 1) * 4 * rank, :].astype(F32)).T.astype(BF)
        for q in range(4):
            rows32[m * 4 + q] = jnp.where(family, dot(turned, spread[q], NN), 0.0)
    for k in range(16):
        weights_ref[k] = rows32[:, k * 8 : k * 8 + 8, :].reshape(256, 256).astype(BF)
    coeffs = [message_ref[:, base + g * 256 : base + (g + 1) * 256] for g in range(8)] + [None] * 8
    for n in range(7):
        lifted = dot(coeffs[2 * n], weights_ref[2 * n], NN) + dot(coeffs[2 * n + 1], weights_ref[2 * n + 1], NN)
        coeffs[8 + n] = lifted.astype(BF)
    four = dot(coeffs[14], weights_ref[14], NN)
    five = dot(four.astype(BF), weights_ref[15], NN)
    six = dot((four + five).astype(BF), weights_ref[15], NN)
    coeffs[15] = (four + six).astype(BF)
    root = jnp.where(iota((256, 128), 0) == iota((256, 128), 1) * 8 + 6, 1.0, 0.0).astype(BF)
    tile = dot(coeffs[15], root, NN).astype(BF)
    for q in range(copies_ref.shape[0]):
        copies_ref[q] = tile
    odd = lax.axis_index("leaf") % 2 == 1
    second_ref[:, :base] = jnp.where(odd, ordered_ref[:, points - base :], ordered_ref[:, :base])
    for g in range(16):
        second_ref[:, base + g * 256 : base + (g + 1) * 256] = coeffs[g]
    for g in range(8):
        lifted_ref[:, g * 256 : (g + 1) * 256] = coeffs[8 + g]


def lane_numbers(rows):
    return iota((rows, 128), 1).astype(F32).astype(BF)


def near_group(leaves_ref, lists_ref, blocks, first, base, columns):
    lane_left = lane_numbers(columns) < 64
    picked = []
    for i in range(4):
        spots = [lists_ref[s, first + i] - base for s in range(4)]
        halves = []
        for s in (0, 2):
            even = leaves_ref[spots[s]]
            odd = leaves_ref[spots[s + 1] ^ 1]
            halves.append(jnp.where(lane_left, even, odd))
        picked.append(jnp.concatenate(halves, axis=1))
    out = dot(jnp.concatenate(picked, axis=0), blocks, NT)
    leaf_of_lane = iota((columns, 256), 1) >> 6
    total = out[:columns]
    for i in range(1, 4):
        total = jnp.where(leaf_of_lane == i, out[i * columns : (i + 1) * columns], total)
    return total


def place_leaves(leaves_ref, first, chunk):
    leaves_ref[first] = chunk
    leaves_ref[first + 1] = pltpu.roll(chunk.astype(F32), 64, 1).astype(BF)


def matrices_kernel(
    coupling_ref, lists_ref, order_ref, matrices_ref, spots_ref, hot_ref, blocks_ref, rows32,
):
    rank = 32
    device = lax.axis_index("leaf")
    count = 64
    chunks = hot_ref.shape[0]

    within = iota((16, 256), 1).astype(F32)
    inverse = jnp.zeros((32, 256), F32)
    for c in range(chunks):
        high, low = split_ids(order_ref, c, chunks * 256)
        hit = iota((16, 256), 0) == jnp.broadcast_to(high, (16, 256))
        marks = jnp.concatenate([jnp.where(hit, float(c), 0.0), jnp.where(hit, within, 0.0)], axis=0)
        inverse = inverse + dot(marks.astype(BF), one_hot(low), NT)
    inverse = inverse.astype(jnp.int32)
    blocks_ref[...] = inverse[:16]
    for c in range(chunks):
        hot_ref[c] = one_hot(inverse[16 + c : 17 + c, :])

    node = iota((1, 128), 1)
    size = jnp.full((1, 128), count, jnp.int32)
    start = jnp.zeros((1, 128), jnp.int32)
    offset = 0
    for level in range(LEVELS):
        size = jnp.where(node >= offset, count >> level, size)
        start = jnp.where(node >= offset, offset, start)
        offset += count >> level
    entries = pad_lanes(lists_ref[...])
    for s in range(6):
        entry = entries[s : s + 1]
        place = entry - device * size + size
        side = jnp.where(place >= size, 1, 0) + jnp.where(place >= 2 * size, 1, 0)
        spot = side * 128 + start + place - side * size
        used = (entry >= 0) & (node < offset)
        spots_ref[pl.ds(s, 1), :] = jnp.where(used, spot, 3 * 128)
    spots_ref[pl.ds(6, 2), :] = jnp.zeros((2, 128), jnp.int32)

    for a in range(rank):
        one = [coupling_ref[s, a * rank : (a + 1) * rank, :].astype(F32) for s in range(6)]
        full = pad_lanes(jnp.concatenate(one, axis=0))
        turned = jnp.concatenate([full[:128].T, pad_lanes(full[128:].T)], axis=1)
        rows32[a] = turned
    for g in range(16):
        matrices_ref[g] = rows32[:, g * 8 : g * 8 + 8, :].reshape(256, 256).astype(BF)


def near_kernel(ordered_ref, blocks_ref, near_ref, near_out, leaves):
    columns, points = ordered_ref.shape
    count = blocks_ref.shape[0]
    device = lax.axis_index("leaf")
    for c in range(count // 2):
        place_leaves(leaves, c * 2, ordered_ref[:, c * 128 : (c + 1) * 128])
    edge = REACH // 4
    near_out[:, : edge * 256] = jnp.zeros((columns, edge * 256), F32)
    near_out[:, points - edge * 256 :] = jnp.zeros((columns, edge * 256), F32)

    def near(g, carry):
        blocks = blocks_ref[pl.ds(g * 4, 4)].reshape(256, 256)
        at = pl.multiple_of(g * 256, 256)
        near_out[:, pl.ds(at, 256)] = near_group(
            leaves, near_ref, blocks, g * 4, device * count, columns
        )
        return carry

    lax.fori_loop(edge, count // 4 - edge, near, 0, unroll=4)


def root_kernel(gathered_ref, transfer_ref, coupling_ref, lists_ref, six_ref, coeffs):
    node_count, columns = gathered_ref.shape[:2]
    device = lax.axis_index("leaf")
    total = 2 * node_count - 1
    coeffs[total] = jnp.zeros((columns, 32), F32)
    values = [gathered_ref[q][:, :32] for q in range(node_count)]
    for q in range(node_count):
        coeffs[q] = values[q].astype(F32)
    start, count = 0, node_count
    starts = [(0, node_count)]
    while count > 1:
        for j in range(count // 2):
            left, right = start + 2 * j, start + 2 * j + 1
            lifted = dot(values[left], transfer_ref[left], NN) + dot(values[right], transfer_ref[right], NN)
            values.append(lifted.astype(BF))
            coeffs[start + count + j] = values[-1].astype(F32)
        start, count = start + count, count // 2
        starts.append((start, count))
    fields = []
    for level, (start, count) in enumerate(starts):
        node = start + (device >> level)
        field = None
        for s in range(6):
            entry = lists_ref[s, node]
            spot = jnp.where(entry >= 0, start + entry, total)
            term = dot(coeffs[spot].astype(BF), coupling_ref[s, node], NT)
            field = term if field is None else field + term
        fields.append((node, field))
    down = fields.pop()[1].astype(BF)
    for node, field in reversed(fields):
        down = (field + dot(down, transfer_ref[node], NT)).astype(BF)
    sixth = jnp.where(iota((32, 256), 1) == iota((32, 256), 0) * 8 + 6, 1.0, 0.0).astype(BF)
    six_ref[...] = dot(down, sixth, NN)


def outer_kernel(
    ordered_ref, own_ref, first0_ref, first1_ref, second_ref, near_in, blocks_ref,
    near_ref, matrices_ref, spots_ref, inverse_ref, weights_ref, masked_ref, hot_ref, six_ref,
    applied_hbm,
    applied_ref, leaves, nodes, far, stacked, stacked_nodes, edges, sems, out_sems,
):
    columns, points = ordered_ref.shape
    halo = REACH * 64
    device = lax.axis_index("leaf")
    count = points // 64
    copies = [
        pltpu.make_async_copy(blocks_ref.at[pl.ds(at, REACH)], edges.at[i], sems.at[i])
        for i, at in enumerate((0, count - REACH))
    ]
    for copy in copies:
        copy.start()

    odd = device % 2
    for ref, right in ((first0_ref, 1 - odd), (second_ref, odd)):
        for c in range(halo // 128):
            place_leaves(leaves, right * (REACH + count) + c * 2, ref[:, c * 128 : (c + 1) * 128])
    near_ends = REACH * 64 * 2 // 128
    for c in list(range(near_ends)) + list(range(count // 2 - near_ends, count // 2)):
        place_leaves(leaves, REACH + c * 2, ordered_ref[:, c * 128 : (c + 1) * 128])

    nodes[3 * 128] = jnp.zeros((columns, 128), BF)
    lane, row = iota((256, 1024), 1), iota((256, 1024), 0)
    spread = jnp.where(row == (lane & 31) * 8 + (lane >> 7), 1.0, 0.0).astype(BF)
    for side, ref in ((1, own_ref), (2 - 2 * odd, None), (2 * odd, second_ref)):
        for n in range(16):
            if ref is not None:
                chunk = ref[:, halo + n * 256 : halo + (n + 1) * 256]
            elif n < 8:
                chunk = first0_ref[:, halo + n * 256 : halo + (n + 1) * 256]
            else:
                chunk = first1_ref[:, (n - 8) * 256 : (n - 7) * 256]
            stacked_nodes[n * columns : (n + 1) * columns, :] = chunk
        for c in range(0, 8, 2):
            out = dot(stacked_nodes[...], spread[:, c * 128 : (c + 2) * 128], NN)
            for n in range(16):
                both = out[n * columns : (n + 1) * columns].astype(BF)
                nodes[side * 128 + n * 8 + c] = both[:, :128]
                nodes[side * 128 + n * 8 + c + 1] = both[:, 128:]

    lane = lane_numbers(columns)
    lane_node = iota((columns, 256), 1) & 7

    for g in range(16):
        picked = []
        for i in range(8):
            parts = [nodes[spots_ref[s, g * 8 + i]] for s in range(6)]
            front = jnp.where(lane < 32, parts[0], parts[1])
            front = jnp.where(lane < 64, front, jnp.where(lane < 96, parts[2], parts[3]))
            back = jnp.where(lane < 32, parts[4], parts[5])
            back = jnp.where(lane < 64, back, jnp.zeros((), BF))
            picked.append(jnp.concatenate([front, back], axis=1))
        out = dot(jnp.concatenate(picked, axis=0), matrices_ref[g], NT)
        total = out[:columns]
        for i in range(1, 8):
            total = jnp.where(lane_node == i, out[i * columns : (i + 1) * columns], total)
        far[:, g * 256 : (g + 1) * 256] = total

    for copy in copies:
        copy.wait()
    six = six_ref[...]
    down = [None] * 16
    last = far[:, 15 * 256 :]
    five = last + dot(six.astype(BF), weights_ref[15], NT)
    five = jnp.where(lane_node >= 4, five, 0.0) + six
    down[15] = (last + dot(five.astype(BF), weights_ref[15], NT)).astype(BF)
    for k in reversed(range(15)):
        down[k] = (far[:, k * 256 : (k + 1) * 256] + dot(down[8 + k // 2], weights_ref[k], NT)).astype(BF)
    groups = count // 4
    edge = REACH // 4
    for g in range(groups):
        if g < edge:
            blocks = edges[0, g * 4 : g * 4 + 4].reshape(256, 256)
        elif g >= groups - edge:
            at = (g - groups + edge) * 4
            blocks = edges[1, at : at + 4].reshape(256, 256)
        else:
            blocks = None
        if blocks is None:
            near = near_in[:, g * 256 : (g + 1) * 256]
        else:
            near = near_group(leaves, near_ref, blocks, g * 4, device * count - REACH, columns)
        if g % 2 == 0:
            at_points = dot(down[g // 2], masked_ref[g // 2], NN)
        half = at_points[:, g % 2 * 256 : (g % 2 + 1) * 256]
        stacked[g * columns : (g + 1) * columns, :] = (near + half).astype(BF)

    writes = []
    for c in range(points // 256):
        applied_ref[:, c * 256 : (c + 1) * 256] = pick(
            stacked[...], hot_ref[c], inverse_ref[c : c + 1, :], columns
        )
        if c % 4 == 3:
            at = pl.ds((c - 3) * 256, 1024)
            writes.append(pltpu.make_async_copy(applied_ref.at[:, at], applied_hbm.at[:, at], out_sems.at[c // 4]))
            writes[-1].start()
    for write in writes:
        write.wait()


VMEM = pl.BlockSpec(memory_space=pltpu.VMEM)
SMEM = pl.BlockSpec(memory_space=pltpu.SMEM)


def in_hbm(x):
    return pltpu.with_memory_space_constraint(x, pltpu.HBM)


def call(kernel, outs, scratch, specs, flops, name, args, mib=16, out_specs=None):
    size = sum(a.size * a.dtype.itemsize for a in args)
    return pl.pallas_call(
        kernel,
        out_shape=[jax.ShapeDtypeStruct(*o) if isinstance(o, tuple) else o for o in outs],
        in_specs=specs,
        out_specs=out_specs or [VMEM] * len(outs),
        scratch_shapes=scratch,
        compiler_params=pltpu.CompilerParams(vmem_limit_bytes=mib * 2**20),
        cost_estimate=pl.CostEstimate(flops=flops, bytes_accessed=0, transcendentals=0),
        name=name,
    )(*args)


def local(
    vectors, tree_order, leaf_basis, near_blocks, near_lists, transfers, couplings, coupling_lists,
    top_transfers, top_couplings, top_lists,
):
    columns, points = vectors.shape
    rank = leaf_basis.shape[0]
    devices = lax.axis_size("leaf")
    halo = REACH * near_blocks.shape[1]
    order = tree_order.reshape(points // 128, 128)
    near_t = jnp.transpose(near_lists)
    lists_t = jnp.transpose(coupling_lists)
    moves = transfers.reshape(rank * rank, -1)
    matrices = couplings.reshape(6, rank * rank, -1)

    any_spec = pl.BlockSpec(memory_space=pl.ANY)
    ordered, own0, masked = call(
        leaf_kernel,
        [((columns, points), BF), ((columns, halo + 2048), BF), ((points // 512, 256, 512), BF)],
        [
            pltpu.VMEM(vectors.shape, BF), pltpu.VMEM(order.shape, jnp.int32),
            pltpu.VMEM(leaf_basis.shape, BF), pltpu.VMEM((points // 256 * columns, 256), BF),
            pltpu.SemaphoreType.DMA((3,)),
        ],
        [any_spec] * 3, 10**9, "leaf", tuple(in_hbm(x) for x in (vectors, order, leaf_basis)),
    )
    pairs = [(i, i ^ 1) for i in range(devices)]
    odds = [(i, i + 1) for i in range(1, devices - 1, 2)]
    first0 = lax.ppermute(own0, "leaf", pairs)
    own1, own, copies, weights = call(
        lift_kernel,
        [
            ((columns, 2048), BF), ((columns, halo + 4096), BF), ((devices, columns, 128), BF),
            ((16, 256, 256), BF),
        ],
        [pltpu.VMEM((rank, 128, 256), F32)], [VMEM] * 3, 2 * 10**9, "lift", (own0, ordered, moves),
    )
    first1 = lax.ppermute(own1, "leaf", pairs)
    second = lax.ppermute(own, "leaf", odds + [(j, i) for i, j in odds])
    first0, order, ordered = lax.optimization_barrier((first0, order, ordered))
    coupling_rows, spots, hot, blocks = call(
        matrices_kernel,
        [
            ((16, 256, 256), BF), ((8, 128), jnp.int32), ((points // 256, 256, 256), BF),
            ((points // 256, 256), jnp.int32),
        ],
        [pltpu.VMEM((rank, 128, 256), F32)],
        [VMEM] * 3, 4 * 10**9, "matrices", (matrices, lists_t, order),
    )
    (near_part,) = call(
        near_kernel, [((columns, points), F32)],
        [pltpu.VMEM((points // 64, columns, 128), BF)],
        [VMEM, VMEM, SMEM], 4 * 10**9, "near", (ordered, near_blocks, near_t),
    )
    copies, near_part, blocks = lax.optimization_barrier((copies, near_part, blocks))
    gathered = lax.all_to_all(copies, "leaf", 0, 0)
    (six,) = call(
        root_kernel, [((columns, 256), F32)], [pltpu.VMEM((2 * devices, columns, 32), F32)],
        [VMEM] * 3 + [SMEM], 2 * 10**9, "root",
        (
            gathered, jnp.transpose(top_transfers, (2, 0, 1)), jnp.transpose(top_couplings, (0, 3, 1, 2)),
            jnp.transpose(top_lists),
        ),
    )
    (applied,) = call(
        outer_kernel,
        [((columns, points), F32)],
        [
            pltpu.VMEM((columns, points), F32), pltpu.VMEM((points // 64 + 2 * REACH, columns, 128), BF),
            pltpu.VMEM((385, columns, 128), BF), pltpu.VMEM((columns, 4096), F32),
            pltpu.VMEM((points // 256 * columns, 256), BF), pltpu.VMEM((16 * columns, 256), BF),
            pltpu.VMEM((2, REACH) + near_blocks.shape[1:], BF), pltpu.SemaphoreType.DMA((2,)),
            pltpu.SemaphoreType.DMA((points // 1024,)),
        ],
        [VMEM] * 6 + [any_spec, SMEM, VMEM, SMEM] + [VMEM] * 5,
        4 * 10**9, "outer",
        (
            ordered, own, first0, first1, second, near_part, in_hbm(near_blocks),
            near_t, coupling_rows, spots, blocks, weights, masked, hot, six,
        ),
        out_specs=[any_spec],
    )
    return applied


def solution(mesh):
    placed = (
        P("rhs", ("groups", "leaf")),
        P(("groups", "leaf")),
        P(None, ("groups", "leaf")),
        P(("groups", "leaf"), None, None),
        P(("groups", "leaf"), None),
        P(None, None, ("groups", "leaf")),
        P(None, None, None, ("groups", "leaf")),
        P(("groups", "leaf"), None),
        P(None, None, "groups"),
        P(None, None, None, "groups"),
        P("groups", None),
    )
    return jax.shard_map(
        local, mesh=mesh, in_specs=placed, out_specs=P("rhs", ("groups", "leaf")), check_vma=False
    )
```

```python
import functools

import jax
import jax.numpy as jnp
from jax import lax
from jax.experimental import pallas as pl
from jax.experimental.pallas import tpu as pltpu
from jax.sharding import PartitionSpec as P

LEVELS = 6
REACH = 8
BF = jnp.bfloat16
F32 = jnp.float32
NT = (((1,), (1,)), ((), ()))
NN = (((1,), (0,)), ((), ()))


def iota(shape, axis):
    return lax.broadcasted_iota(jnp.int32, shape, axis)


def dot(a, b, dims):
    return lax.dot_general(a, b, dims, preferred_element_type=F32)


def pad_lanes(x):
    short = 128 - x.shape[1]
    return jnp.concatenate([x, jnp.zeros((x.shape[0], short), x.dtype)], axis=1)


def one_hot(ids):
    ids = jnp.broadcast_to(ids.astype(F32), (16, 256)).astype(BF)
    rows = iota((256, 256), 0).astype(F32).astype(BF)
    return jnp.where(rows == jnp.concatenate([ids] * 16, axis=0), jnp.ones((), BF), jnp.zeros((), BF))


def split_ids(order_ref, c, points):
    ids = jnp.concatenate([order_ref[2 * c : 2 * c + 1, :], order_ref[2 * c + 1 : 2 * c + 2, :]], axis=1)
    ids = lax.rem(ids, points)
    return ids >> 8, ids & 255


def pick(stacked, hot, high, rows):
    out = dot(stacked, hot, NN)
    high = jnp.broadcast_to(high, (rows, 256))
    total = out[:rows]
    for block in range(1, stacked.shape[0] // rows):
        total = jnp.where(high == block, out[block * rows : (block + 1) * rows], total)
    return total


def leaf_kernel(
    vec_hbm, order_hbm, basis_hbm, ordered_ref, message_ref, masked_ref,
    vec_ref, order_ref, basis_ref, stacked, sems,
):
    columns, points = vec_ref.shape
    rank = basis_ref.shape[0]
    halo = REACH * 64
    pairs = ((order_hbm, order_ref), (vec_hbm, vec_ref), (basis_hbm, basis_ref))
    copies = [pltpu.make_async_copy(src, dst, sems.at[i]) for i, (src, dst) in enumerate(pairs)]
    for copy in copies:
        copy.start()
    copies[0].wait()
    copies[1].wait()
    for block in range(points // 256):
        stacked[block * columns : (block + 1) * columns, :] = vec_ref[:, block * 256 : (block + 1) * 256]
    for c in range(points // 256):
        high, low = split_ids(order_ref, c, points)
        ordered_ref[:, c * 256 : (c + 1) * 256] = pick(stacked[...], one_hot(low), high, columns).astype(BF)

    copies[2].wait()
    mine = (iota((256, 512), 0) & 7) == (iota((256, 512), 1) >> 6)
    for g in range(points // 512):
        one = basis_ref[:, g * 512 : (g + 1) * 512].astype(F32)
        eight = jnp.broadcast_to(one[:, None, :], (rank, 8, 512)).reshape(256, 512)
        masked = jnp.where(mine, eight, 0.0).astype(BF)
        masked_ref[g] = masked
        coeffs = dot(ordered_ref[:, g * 512 : (g + 1) * 512], masked, NT).astype(BF)
        message_ref[:, halo + g * 256 : halo + (g + 1) * 256] = coeffs
    odd = lax.axis_index("leaf") % 2 == 1
    message_ref[:, :halo] = jnp.where(odd, ordered_ref[:, :halo], ordered_ref[:, points - halo :])


def lift_kernel(message_ref, ordered_ref, transfer_ref, lifted_ref, top_ref, weights_ref, rows32):
    rank = 32
    base = REACH * 64
    points = ordered_ref.shape[1]
    odd = lax.axis_index("leaf") % 2 == 1
    lifted_ref[:, 2048:] = jnp.where(odd, ordered_ref[:, points - base :], ordered_ref[:, :base])

    lane, row = iota((128, 256), 1), iota((128, 256), 0)
    family = (lane & 7) == ((row >> 1) & 7)
    spread = [
        jnp.where(iota((128, 256), 0) == (iota((128, 256), 1) >> 3) + 32 * q, 1.0, 0.0).astype(BF)
        for q in range(4)
    ]
    for m in range(rank // 4):
        turned = pad_lanes(transfer_ref[m * 4 * rank : (m + 1) * 4 * rank, :].astype(F32)).T.astype(BF)
        for q in range(4):
            rows32[m * 4 + q] = jnp.where(family, dot(turned, spread[q], NN), 0.0)
    for k in range(16):
        weights_ref[k] = rows32[:, k * 8 : k * 8 + 8, :].reshape(256, 256).astype(BF)
    coeffs = [message_ref[:, base + g * 256 : base + (g + 1) * 256] for g in range(8)] + [None] * 8
    for n in range(7):
        lifted = dot(coeffs[2 * n], weights_ref[2 * n], NN) + dot(coeffs[2 * n + 1], weights_ref[2 * n + 1], NN)
        coeffs[8 + n] = lifted.astype(BF)
    four = dot(coeffs[14], weights_ref[14], NN)
    five = dot(four.astype(BF), weights_ref[15], NN)
    six = dot((four + five).astype(BF), weights_ref[15], NN)
    coeffs[15] = (four + six).astype(BF)
    width = top_ref.shape[1]
    slot = lax.axis_index("leaf") // 2 * rank
    row, lane = iota((256, width), 0), iota((256, width), 1) - slot
    root = jnp.where((row == lane * 8 + 6) & (lane >= 0), 1.0, 0.0).astype(BF)
    top_ref[...] = dot(coeffs[15], root, NN).astype(BF)
    for g in range(8):
        lifted_ref[:, g * 256 : (g + 1) * 256] = coeffs[8 + g]


def lane_numbers(rows):
    return iota((rows, 128), 1).astype(F32).astype(BF)


def near_group(leaves_ref, lists_ref, blocks, first, base, columns):
    lane_left = lane_numbers(columns) < 64
    picked = []
    for i in range(4):
        spots = [lists_ref[s, first + i] - base for s in range(4)]
        halves = []
        for s in (0, 2):
            even = leaves_ref[spots[s]]
            odd = leaves_ref[spots[s + 1] ^ 1]
            halves.append(jnp.where(lane_left, even, odd))
        picked.append(jnp.concatenate(halves, axis=1))
    out = dot(jnp.concatenate(picked, axis=0), blocks, NT)
    leaf_of_lane = iota((columns, 256), 1) >> 6
    total = out[:columns]
    for i in range(1, 4):
        total = jnp.where(leaf_of_lane == i, out[i * columns : (i + 1) * columns], total)
    return total


def place_leaves(leaves_ref, first, chunk):
    leaves_ref[first] = chunk
    leaves_ref[first + 1] = pltpu.roll(chunk.astype(F32), 64, 1).astype(BF)


def matrices_kernel(
    coupling_ref, lists_ref, order_ref, matrices_ref, spots_ref, hot_ref, blocks_ref, rows32,
):
    rank = 32
    device = lax.axis_index("leaf")
    count = 64
    chunks = hot_ref.shape[0]

    within = iota((16, 256), 1).astype(F32)
    inverse = jnp.zeros((32, 256), F32)
    for c in range(chunks):
        high, low = split_ids(order_ref, c, chunks * 256)
        hit = iota((16, 256), 0) == jnp.broadcast_to(high, (16, 256))
        marks = jnp.concatenate([jnp.where(hit, float(c), 0.0), jnp.where(hit, within, 0.0)], axis=0)
        inverse = inverse + dot(marks.astype(BF), one_hot(low), NT)
    inverse = inverse.astype(jnp.int32)
    blocks_ref[...] = inverse[:16]
    for c in range(chunks):
        hot_ref[c] = one_hot(inverse[16 + c : 17 + c, :])

    node = iota((1, 128), 1)
    size = jnp.full((1, 128), count, jnp.int32)
    start = jnp.zeros((1, 128), jnp.int32)
    offset = 0
    for level in range(LEVELS):
        size = jnp.where(node >= offset, count >> level, size)
        start = jnp.where(node >= offset, offset, start)
        offset += count >> level
    entries = pad_lanes(lists_ref[...])
    for s in range(6):
        entry = entries[s : s + 1]
        place = entry - device * size + size
        side = jnp.where(place >= size, 1, 0) + jnp.where(place >= 2 * size, 1, 0)
        spot = side * 128 + start + place - side * size
        used = (entry >= 0) & (node < offset)
        spots_ref[pl.ds(s, 1), :] = jnp.where(used, spot, 3 * 128)
    spots_ref[pl.ds(6, 2), :] = jnp.zeros((2, 128), jnp.int32)

    for a in range(rank):
        one = [coupling_ref[s, a * rank : (a + 1) * rank, :].astype(F32) for s in range(6)]
        full = pad_lanes(jnp.concatenate(one, axis=0))
        turned = jnp.concatenate([full[:128].T, pad_lanes(full[128:].T)], axis=1)
        rows32[a] = turned
    for g in range(16):
        matrices_ref[g] = rows32[:, g * 8 : g * 8 + 8, :].reshape(256, 256).astype(BF)


def near_kernel(ordered_ref, blocks_ref, near_ref, near_out, leaves):
    columns, points = ordered_ref.shape
    count = blocks_ref.shape[0]
    device = lax.axis_index("leaf")
    for c in range(count // 2):
        place_leaves(leaves, c * 2, ordered_ref[:, c * 128 : (c + 1) * 128])
    edge = REACH // 4
    near_out[:, : edge * 256] = jnp.zeros((columns, edge * 256), F32)
    near_out[:, points - edge * 256 :] = jnp.zeros((columns, edge * 256), F32)

    def near(g, carry):
        blocks = blocks_ref[pl.ds(g * 4, 4)].reshape(256, 256)
        at = pl.multiple_of(g * 256, 256)
        near_out[:, pl.ds(at, 256)] = near_group(
            leaves, near_ref, blocks, g * 4, device * count, columns
        )
        return carry

    lax.fori_loop(edge, count // 4 - edge, near, 0, unroll=4)


def root_kernel(own_ref, other_ref, transfer_ref, coupling_ref, lists_ref, six_ref, coeffs):
    columns, rank = own_ref.shape[0], 32
    node_count = lists_ref.shape[1] // 2 + 1
    device = lax.axis_index("leaf")
    total = 2 * node_count - 1
    coeffs[total] = jnp.zeros((columns, rank), F32)
    for q in range(node_count):
        ref = own_ref if q % 2 == 0 else other_ref
        at = q // 2 * rank
        coeffs[q ^ (device & 1)] = ref[:, at : at + rank].astype(F32)
    values = [coeffs[j].astype(BF) for j in range(node_count)]
    start, count = 0, node_count
    starts = [(0, node_count)]
    while count > 1:
        for j in range(count // 2):
            left, right = start + 2 * j, start + 2 * j + 1
            lifted = dot(values[left], transfer_ref[left], NN) + dot(values[right], transfer_ref[right], NN)
            values.append(lifted.astype(BF))
            coeffs[start + count + j] = values[-1].astype(F32)
        start, count = start + count, count // 2
        starts.append((start, count))
    fields = []
    for level, (start, count) in enumerate(starts):
        node = start + (device >> level)
        field = None
        for s in range(6):
            entry = lists_ref[s, node]
            spot = jnp.where(entry >= 0, start + entry, total)
            term = dot(coeffs[spot].astype(BF), coupling_ref[s, node], NT)
            field = term if field is None else field + term
        fields.append((node, field))
    down = fields.pop()[1].astype(BF)
    for node, field in reversed(fields):
        down = (field + dot(down, transfer_ref[node], NT)).astype(BF)
    sixth = jnp.where(iota((32, 256), 1) == iota((32, 256), 0) * 8 + 6, 1.0, 0.0).astype(BF)
    six_ref[...] = dot(down, sixth, NN)


def outer_kernel(
    ordered_ref, own0_ref, own1_ref, first0_ref, first1_ref, second0_ref, second1_ref, near_in, blocks_ref,
    near_ref, matrices_ref, spots_ref, inverse_ref, weights_ref, masked_ref, hot_ref, six_ref,
    applied_hbm,
    applied_ref, leaves, nodes, far, stacked, stacked_nodes, edges, sems, out_sems,
):
    columns, points = ordered_ref.shape
    halo = REACH * 64
    device = lax.axis_index("leaf")
    count = points // 64
    copies = [
        pltpu.make_async_copy(blocks_ref.at[pl.ds(at, REACH)], edges.at[i], sems.at[i])
        for i, at in enumerate((0, count - REACH))
    ]
    for copy in copies:
        copy.start()

    odd = device % 2
    for ref, start, right in ((first0_ref, 0, 1 - odd), (second1_ref, 2048, odd)):
        for c in range(halo // 128):
            at = start + c * 128
            place_leaves(leaves, right * (REACH + count) + c * 2, ref[:, at : at + 128])
    near_ends = REACH * 64 * 2 // 128
    for c in list(range(near_ends)) + list(range(count // 2 - near_ends, count // 2)):
        place_leaves(leaves, REACH + c * 2, ordered_ref[:, c * 128 : (c + 1) * 128])

    nodes[3 * 128] = jnp.zeros((columns, 128), BF)
    lane, row = iota((256, 1024), 1), iota((256, 1024), 0)
    spread = jnp.where(row == (lane & 31) * 8 + (lane >> 7), 1.0, 0.0).astype(BF)
    sources = (
        (1, own0_ref, own1_ref), (2 - 2 * odd, first0_ref, first1_ref), (2 * odd, second0_ref, second1_ref),
    )
    for side, ref0, ref1 in sources:
        for n in range(8):
            at = halo + n * 256
            stacked_nodes[n * columns : (n + 1) * columns, :] = ref0[:, at : at + 256]
            stacked_nodes[(8 + n) * columns : (9 + n) * columns, :] = ref1[:, n * 256 : (n + 1) * 256]
        for c in range(0, 8, 2):
            out = dot(stacked_nodes[...], spread[:, c * 128 : (c + 2) * 128], NN)
            for n in range(16):
                both = out[n * columns : (n + 1) * columns].astype(BF)
                nodes[side * 128 + n * 8 + c] = both[:, :128]
                nodes[side * 128 + n * 8 + c + 1] = both[:, 128:]

    lane = lane_numbers(columns)
    lane_node = iota((columns, 256), 1) & 7

    for g in range(16):
        picked = []
        for i in range(8):
            parts = [nodes[spots_ref[s, g * 8 + i]] for s in range(6)]
            front = jnp.where(lane < 32, parts[0], parts[1])
            front = jnp.where(lane < 64, front, jnp.where(lane < 96, parts[2], parts[3]))
            back = jnp.where(lane < 32, parts[4], parts[5])
            back = jnp.where(lane < 64, back, jnp.zeros((), BF))
            picked.append(jnp.concatenate([front, back], axis=1))
        out = dot(jnp.concatenate(picked, axis=0), matrices_ref[g], NT)
        total = out[:columns]
        for i in range(1, 8):
            total = jnp.where(lane_node == i, out[i * columns : (i + 1) * columns], total)
        far[:, g * 256 : (g + 1) * 256] = total

    for copy in copies:
        copy.wait()
    six = six_ref[...]
    down = [None] * 16
    last = far[:, 15 * 256 :]
    five = last + dot(six.astype(BF), weights_ref[15], NT)
    five = jnp.where(lane_node >= 4, five, 0.0) + six
    down[15] = (last + dot(five.astype(BF), weights_ref[15], NT)).astype(BF)
    for k in reversed(range(15)):
        down[k] = (far[:, k * 256 : (k + 1) * 256] + dot(down[8 + k // 2], weights_ref[k], NT)).astype(BF)
    groups = count // 4
    edge = REACH // 4
    for g in range(groups):
        if g < edge:
            blocks = edges[0, g * 4 : g * 4 + 4].reshape(256, 256)
        elif g >= groups - edge:
            at = (g - groups + edge) * 4
            blocks = edges[1, at : at + 4].reshape(256, 256)
        else:
            blocks = None
        if blocks is None:
            near = near_in[:, g * 256 : (g + 1) * 256]
        else:
            near = near_group(leaves, near_ref, blocks, g * 4, device * count - REACH, columns)
        if g % 2 == 0:
            at_points = dot(down[g // 2], masked_ref[g // 2], NN)
        half = at_points[:, g % 2 * 256 : (g % 2 + 1) * 256]
        stacked[g * columns : (g + 1) * columns, :] = (near + half).astype(BF)

    writes = []
    for c in range(points // 256):
        applied_ref[:, c * 256 : (c + 1) * 256] = pick(
            stacked[...], hot_ref[c], inverse_ref[c : c + 1, :], columns
        )
        if c % 4 == 3:
            at = pl.ds((c - 3) * 256, 1024)
            writes.append(pltpu.make_async_copy(applied_ref.at[:, at], applied_hbm.at[:, at], out_sems.at[c // 4]))
            writes[-1].start()
    for write in writes:
        write.wait()


VMEM = pl.BlockSpec(memory_space=pltpu.VMEM)
SMEM = pl.BlockSpec(memory_space=pltpu.SMEM)


def in_hbm(x):
    return pltpu.with_memory_space_constraint(x, pltpu.HBM)


def call(kernel, outs, scratch, specs, flops, name, args, mib=16, out_specs=None):
    size = sum(a.size * a.dtype.itemsize for a in args)
    return pl.pallas_call(
        kernel,
        out_shape=[jax.ShapeDtypeStruct(s, t) for s, t in outs],
        in_specs=specs,
        out_specs=out_specs or [VMEM] * len(outs),
        scratch_shapes=scratch,
        compiler_params=pltpu.CompilerParams(vmem_limit_bytes=mib * 2**20),
        cost_estimate=pl.CostEstimate(flops=flops, bytes_accessed=0, transcendentals=0),
        name=name,
    )(*args)


def local(
    vectors, tree_order, leaf_basis, near_blocks, near_lists, transfers, couplings, coupling_lists,
    top_transfers, top_couplings, top_lists,
):
    columns, points = vectors.shape
    rank = leaf_basis.shape[0]
    devices = lax.axis_size("leaf")
    halo = REACH * near_blocks.shape[1]
    order = tree_order.reshape(points // 128, 128)
    near_t = jnp.transpose(near_lists)
    lists_t = jnp.transpose(coupling_lists)
    moves = transfers.reshape(rank * rank, -1)
    matrices = couplings.reshape(6, rank * rank, -1)

    any_spec = pl.BlockSpec(memory_space=pl.ANY)
    tile = max(devices // 2 * rank, 128)
    ordered, own0, masked = call(
        leaf_kernel,
        [((columns, points), BF), ((columns, halo + 2048), BF), ((points // 512, 256, 512), BF)],
        [
            pltpu.VMEM(vectors.shape, BF), pltpu.VMEM(order.shape, jnp.int32),
            pltpu.VMEM(leaf_basis.shape, BF), pltpu.VMEM((points // 256 * columns, 256), BF),
            pltpu.SemaphoreType.DMA((3,)),
        ],
        [any_spec] * 3, 10**9, "leaf", tuple(in_hbm(x) for x in (vectors, order, leaf_basis)),
    )
    pairs = [(i, i ^ 1) for i in range(devices)]
    onward = [(i, i + 2) for i in range(0, devices - 2, 2)] + [(i, i - 2) for i in range(3, devices, 2)]
    first0 = lax.ppermute(own0, "leaf", pairs)
    own1, top, weights = call(
        lift_kernel,
        [((columns, halo + 2048), BF), ((columns, tile), BF), ((16, 256, 256), BF)],
        [pltpu.VMEM((rank, 128, 256), F32)], [VMEM] * 3, 10**9, "lift", (own0, ordered, moves),
    )

    def step(tile_sum, reached):
        return lax.ppermute(tile_sum, "leaf", [(i, i ^ reached) for i in range(devices)])

    steps = [1 << k for k in reversed(range(1, devices.bit_length() - 1))]
    for reached in steps[:-2]:
        top = top + step(top, reached)
    other = step(top, steps[-2])
    coupling_rows, spots, hot, blocks = call(
        matrices_kernel,
        [
            ((16, 256, 256), BF), ((8, 128), jnp.int32), ((points // 256, 256, 256), BF),
            ((points // 256, 256), jnp.int32),
        ],
        [pltpu.VMEM((rank, 128, 256), F32)],
        [VMEM] * 3, 10**6, "matrices", (matrices, lists_t, order),
    )
    first1 = lax.ppermute(own1, "leaf", pairs)
    first0, top, blocks = lax.optimization_barrier((first0, top + other, blocks))
    other = step(top, steps[-1])
    second0 = lax.ppermute(first0, "leaf", onward)
    first1, top = lax.optimization_barrier((first1, top + other))
    other = step(top, 1)
    second1 = lax.ppermute(first1, "leaf", onward)
    first1, ordered = lax.optimization_barrier((first1, ordered))
    (near_part,) = call(
        near_kernel, [((columns, points), F32)],
        [pltpu.VMEM((points // 64, columns, 128), BF)],
        [VMEM, VMEM, SMEM], 10**6, "near", (ordered, near_blocks, near_t),
    )
    (six,) = call(
        root_kernel, [((columns, 256), F32)], [pltpu.VMEM((2 * devices, columns, 32), F32)],
        [VMEM] * 4 + [SMEM], 10**6, "root",
        (
            top, other, jnp.transpose(top_transfers, (2, 0, 1)), jnp.transpose(top_couplings, (0, 3, 1, 2)),
            jnp.transpose(top_lists),
        ),
    )
    (applied,) = call(
        outer_kernel,
        [((columns, points), F32)],
        [
            pltpu.VMEM((columns, points), F32), pltpu.VMEM((points // 64 + 2 * REACH, columns, 128), BF),
            pltpu.VMEM((385, columns, 128), BF), pltpu.VMEM((columns, 4096), F32),
            pltpu.VMEM((points // 256 * columns, 256), BF), pltpu.VMEM((16 * columns, 256), BF),
            pltpu.VMEM((2, REACH) + near_blocks.shape[1:], BF), pltpu.SemaphoreType.DMA((2,)),
            pltpu.SemaphoreType.DMA((points // 1024,)),
        ],
        [VMEM] * 8 + [any_spec, SMEM, VMEM, SMEM] + [VMEM] * 5,
        4 * 10**9, "outer",
        (
            ordered, own0, own1, first0, first1, second0, second1, near_part, in_hbm(near_blocks),
            near_t, coupling_rows, spots, blocks, weights, masked, hot, six,
        ),
        out_specs=[any_spec],
    )
    return applied


def solution(mesh):
    placed = (
        P("rhs", ("groups", "leaf")),
        P(("groups", "leaf")),
        P(None, ("groups", "leaf")),
        P(("groups", "leaf"), None, None),
        P(("groups", "leaf"), None),
        P(None, None, ("groups", "leaf")),
        P(None, None, None, ("groups", "leaf")),
        P(("groups", "leaf"), None),
        P(None, None, "groups"),
        P(None, None, None, "groups"),
        P("groups", None),
    )
    return jax.shard_map(
        local, mesh=mesh, in_specs=placed, out_specs=P("rhs", ("groups", "leaf")), check_vma=False
    )
```

```python
import functools

import jax
import jax.numpy as jnp
from jax import lax
from jax.experimental import pallas as pl
from jax.experimental.pallas import tpu as pltpu
from jax.sharding import PartitionSpec as P

LEVELS = 6
REACH = 8
BF = jnp.bfloat16
F32 = jnp.float32
NT = (((1,), (1,)), ((), ()))
NN = (((1,), (0,)), ((), ()))


def iota(shape, axis):
    return lax.broadcasted_iota(jnp.int32, shape, axis)


def dot(a, b, dims):
    return lax.dot_general(a, b, dims, preferred_element_type=F32)


def pad_lanes(x):
    short = 128 - x.shape[1]
    return jnp.concatenate([x, jnp.zeros((x.shape[0], short), x.dtype)], axis=1)


def one_hot(ids):
    ids = jnp.broadcast_to(ids.astype(F32), (16, 256)).astype(BF)
    rows = iota((256, 256), 0).astype(F32).astype(BF)
    return jnp.where(rows == jnp.concatenate([ids] * 16, axis=0), jnp.ones((), BF), jnp.zeros((), BF))


def split_ids(order_ref, c, points):
    ids = jnp.concatenate([order_ref[2 * c : 2 * c + 1, :], order_ref[2 * c + 1 : 2 * c + 2, :]], axis=1)
    ids = lax.rem(ids, points)
    return ids >> 8, ids & 255


def pick(stacked, hot, high, rows):
    out = dot(stacked, hot, NN).reshape(-1, rows // 8, 8, 256)
    high = jnp.broadcast_to(high, (8, 256))
    total = out[0]
    for block in range(1, out.shape[0]):
        total = jnp.where((high == block)[None], out[block], total)
    return total.reshape(rows, 256)


def leaf_kernel(
    vec_hbm, order_hbm, basis_hbm, ordered_ref, message_ref, masked_ref,
    vec_ref, order_ref, basis_ref, stacked, sems,
):
    columns, points = vec_ref.shape
    rank = basis_ref.shape[0]
    halo = REACH * 64
    pairs = ((order_hbm, order_ref), (vec_hbm, vec_ref), (basis_hbm, basis_ref))
    copies = [pltpu.make_async_copy(src, dst, sems.at[i]) for i, (src, dst) in enumerate(pairs)]
    for copy in copies:
        copy.start()
    copies[0].wait()
    copies[1].wait()
    for block in range(points // 256):
        stacked[block * columns : (block + 1) * columns, :] = vec_ref[:, block * 256 : (block + 1) * 256]
    for c in range(points // 256):
        high, low = split_ids(order_ref, c, points)
        ordered_ref[:, c * 256 : (c + 1) * 256] = pick(stacked[...], one_hot(low), high, columns).astype(BF)

    copies[2].wait()
    mine = (iota((256, 512), 0) & 7) == (iota((256, 512), 1) >> 6)
    for g in range(points // 512):
        one = basis_ref[:, g * 512 : (g + 1) * 512].astype(F32)
        eight = jnp.broadcast_to(one[:, None, :], (rank, 8, 512)).reshape(256, 512)
        masked = jnp.where(mine, eight, 0.0).astype(BF)
        masked_ref[g] = masked
        coeffs = dot(ordered_ref[:, g * 512 : (g + 1) * 512], masked, NT).astype(BF)
        message_ref[:, halo + g * 256 : halo + (g + 1) * 256] = coeffs
    odd = lax.axis_index("leaf") % 2 == 1
    message_ref[:, :halo] = jnp.where(odd, ordered_ref[:, :halo], ordered_ref[:, points - halo :])


def lift_kernel(message_ref, ordered_ref, transfer_ref, lifted_ref, top_ref, weights_ref, rows32):
    rank = 32
    base = REACH * 64
    points = ordered_ref.shape[1]
    odd = lax.axis_index("leaf") % 2 == 1
    lifted_ref[:, 2048:] = jnp.where(odd, ordered_ref[:, points - base :], ordered_ref[:, :base])

    lane, row = iota((128, 256), 1), iota((128, 256), 0)
    family = (lane & 7) == ((row >> 1) & 7)
    spread = [
        jnp.where(iota((128, 256), 0) == (iota((128, 256), 1) >> 3) + 32 * q, 1.0, 0.0).astype(BF)
        for q in range(4)
    ]
    for m in range(rank // 4):
        turned = pad_lanes(transfer_ref[m * 4 * rank : (m + 1) * 4 * rank, :].astype(F32)).T.astype(BF)
        for q in range(4):
            rows32[m * 4 + q] = jnp.where(family, dot(turned, spread[q], NN), 0.0)
    for k in range(16):
        weights_ref[k] = rows32[:, k * 8 : k * 8 + 8, :].reshape(256, 256).astype(BF)
    coeffs = [message_ref[:, base + g * 256 : base + (g + 1) * 256] for g in range(8)] + [None] * 8
    for n in range(7):
        lifted = dot(coeffs[2 * n], weights_ref[2 * n], NN) + dot(coeffs[2 * n + 1], weights_ref[2 * n + 1], NN)
        coeffs[8 + n] = lifted.astype(BF)
    four = dot(coeffs[14], weights_ref[14], NN)
    five = dot(four.astype(BF), weights_ref[15], NN)
    six = dot((four + five).astype(BF), weights_ref[15], NN)
    coeffs[15] = (four + six).astype(BF)
    width = top_ref.shape[1]
    slot = lax.axis_index("leaf") // 2 * rank
    row, lane = iota((256, width), 0), iota((256, width), 1) - slot
    root = jnp.where((row == lane * 8 + 6) & (lane >= 0), 1.0, 0.0).astype(BF)
    top_ref[...] = dot(coeffs[15], root, NN).astype(BF)
    for g in range(8):
        lifted_ref[:, g * 256 : (g + 1) * 256] = coeffs[8 + g]


def lane_numbers(rows):
    return iota((rows, 128), 1).astype(F32).astype(BF)


def near_group(leaves_ref, lists_ref, blocks, first, base, columns):
    lane_left = lane_numbers(columns) < 64
    picked = []
    for i in range(4):
        spots = [lists_ref[s, first + i] - base for s in range(4)]
        halves = []
        for s in (0, 2):
            even = leaves_ref[spots[s]]
            odd = leaves_ref[spots[s + 1] ^ 1]
            halves.append(jnp.where(lane_left, even, odd))
        picked.append(jnp.concatenate(halves, axis=1))
    out = dot(jnp.concatenate(picked, axis=0), blocks, NT)
    leaf_of_lane = iota((columns, 256), 1) >> 6
    total = out[:columns]
    for i in range(1, 4):
        total = jnp.where(leaf_of_lane == i, out[i * columns : (i + 1) * columns], total)
    return total


def place_leaves(leaves_ref, first, chunk):
    leaves_ref[first] = chunk
    leaves_ref[first + 1] = pltpu.roll(chunk.astype(F32), 64, 1).astype(BF)


def matrices_kernel(
    coupling_ref, lists_ref, order_ref, matrices_ref, spots_ref, hot_ref, blocks_ref, rows32,
):
    rank = 32
    device = lax.axis_index("leaf")
    count = 64
    chunks = hot_ref.shape[0]

    within = iota((16, 256), 1).astype(F32)
    inverse = jnp.zeros((32, 256), F32)
    for c in range(chunks):
        high, low = split_ids(order_ref, c, chunks * 256)
        hit = iota((16, 256), 0) == jnp.broadcast_to(high, (16, 256))
        marks = jnp.concatenate([jnp.where(hit, float(c), 0.0), jnp.where(hit, within, 0.0)], axis=0)
        inverse = inverse + dot(marks.astype(BF), one_hot(low), NT)
    inverse = inverse.astype(jnp.int32)
    blocks_ref[...] = inverse[:16]
    for c in range(chunks):
        hot_ref[c] = one_hot(inverse[16 + c : 17 + c, :])

    node = iota((1, 128), 1)
    size = jnp.full((1, 128), count, jnp.int32)
    start = jnp.zeros((1, 128), jnp.int32)
    offset = 0
    for level in range(LEVELS):
        size = jnp.where(node >= offset, count >> level, size)
        start = jnp.where(node >= offset, offset, start)
        offset += count >> level
    entries = pad_lanes(lists_ref[...])
    for s in range(6):
        entry = entries[s : s + 1]
        place = entry - device * size + size
        side = jnp.where(place >= size, 1, 0) + jnp.where(place >= 2 * size, 1, 0)
        spot = side * 128 + start + place - side * size
        used = (entry >= 0) & (node < offset)
        spots_ref[pl.ds(s, 1), :] = jnp.where(used, spot, 3 * 128)
    spots_ref[pl.ds(6, 2), :] = jnp.zeros((2, 128), jnp.int32)

    for a in range(rank):
        one = [coupling_ref[s, a * rank : (a + 1) * rank, :].astype(F32) for s in range(6)]
        full = pad_lanes(jnp.concatenate(one, axis=0))
        turned = jnp.concatenate([full[:128].T, pad_lanes(full[128:].T)], axis=1)
        rows32[a] = turned
    for g in range(16):
        matrices_ref[g] = rows32[:, g * 8 : g * 8 + 8, :].reshape(256, 256).astype(BF)


def near_kernel(ordered_ref, blocks_ref, near_ref, near_out, leaves):
    columns, points = ordered_ref.shape
    count = blocks_ref.shape[0]
    device = lax.axis_index("leaf")
    for c in range(count // 2):
        place_leaves(leaves, c * 2, ordered_ref[:, c * 128 : (c + 1) * 128])
    edge = REACH // 4
    near_out[:, : edge * 256] = jnp.zeros((columns, edge * 256), F32)
    near_out[:, points - edge * 256 :] = jnp.zeros((columns, edge * 256), F32)

    def near(g, carry):
        blocks = blocks_ref[pl.ds(g * 4, 4)].reshape(256, 256)
        at = pl.multiple_of(g * 256, 256)
        near_out[:, pl.ds(at, 256)] = near_group(
            leaves, near_ref, blocks, g * 4, device * count, columns
        )
        return carry

    lax.fori_loop(edge, count // 4 - edge, near, 0, unroll=4)


def root_kernel(own_ref, other_ref, transfer_ref, coupling_ref, lists_ref, six_ref, coeffs):
    columns, rank = own_ref.shape[0], 32
    node_count = lists_ref.shape[1] // 2 + 1
    device = lax.axis_index("leaf")
    total = 2 * node_count - 1
    coeffs[total] = jnp.zeros((columns, rank), F32)
    for q in range(node_count):
        ref = own_ref if q % 2 == 0 else other_ref
        at = q // 2 * rank
        coeffs[q ^ (device & 1)] = ref[:, at : at + rank].astype(F32)
    values = [coeffs[j].astype(BF) for j in range(node_count)]
    start, count = 0, node_count
    starts = [(0, node_count)]
    while count > 1:
        for j in range(count // 2):
            left, right = start + 2 * j, start + 2 * j + 1
            lifted = dot(values[left], transfer_ref[left], NN) + dot(values[right], transfer_ref[right], NN)
            values.append(lifted.astype(BF))
            coeffs[start + count + j] = values[-1].astype(F32)
        start, count = start + count, count // 2
        starts.append((start, count))
    fields = []
    for level, (start, count) in enumerate(starts):
        node = start + (device >> level)
        field = None
        for s in range(6):
            entry = lists_ref[s, node]
            spot = jnp.where(entry >= 0, start + entry, total)
            term = dot(coeffs[spot].astype(BF), coupling_ref[s, node], NT)
            field = term if field is None else field + term
        fields.append((node, field))
    down = fields.pop()[1].astype(BF)
    for node, field in reversed(fields):
        down = (field + dot(down, transfer_ref[node], NT)).astype(BF)
    sixth = jnp.where(iota((32, 256), 1) == iota((32, 256), 0) * 8 + 6, 1.0, 0.0).astype(BF)
    six_ref[...] = dot(down, sixth, NN)


def outer_kernel(
    ordered_ref, own0_ref, own1_ref, first0_ref, first1_ref, second0_ref, second1_ref, near_in, blocks_ref,
    near_ref, matrices_ref, spots_ref, inverse_ref, weights_ref, masked_ref, hot_ref, six_ref,
    applied_hbm,
    applied_ref, leaves, nodes, stacked, stacked_nodes, edges, sems, out_sems,
):
    columns, points = ordered_ref.shape
    halo = REACH * 64
    device = lax.axis_index("leaf")
    count = points // 64
    copies = [
        pltpu.make_async_copy(blocks_ref.at[pl.ds(at, REACH)], edges.at[i], sems.at[i])
        for i, at in enumerate((0, count - REACH))
    ]
    for copy in copies:
        copy.start()

    odd = device % 2
    for ref, start, right in ((first0_ref, 0, 1 - odd), (second1_ref, 2048, odd)):
        for c in range(halo // 128):
            at = start + c * 128
            place_leaves(leaves, right * (REACH + count) + c * 2, ref[:, at : at + 128])
    near_ends = REACH * 64 * 2 // 128
    for c in list(range(near_ends)) + list(range(count // 2 - near_ends, count // 2)):
        place_leaves(leaves, REACH + c * 2, ordered_ref[:, c * 128 : (c + 1) * 128])

    nodes[3 * 128] = jnp.zeros((columns, 128), BF)
    lane, row = iota((256, 1024), 1), iota((256, 1024), 0)
    spread = jnp.where(row == (lane & 31) * 8 + (lane >> 7), 1.0, 0.0).astype(BF)
    sources = (
        (1, own0_ref, own1_ref), (2 - 2 * odd, first0_ref, first1_ref), (2 * odd, second0_ref, second1_ref),
    )
    for side, ref0, ref1 in sources:
        for n in range(8):
            at = halo + n * 256
            stacked_nodes[n * columns : (n + 1) * columns, :] = ref0[:, at : at + 256]
            stacked_nodes[(8 + n) * columns : (9 + n) * columns, :] = ref1[:, n * 256 : (n + 1) * 256]
        for c in range(0, 8, 2):
            out = dot(stacked_nodes[...], spread[:, c * 128 : (c + 2) * 128], NN)
            for n in range(16):
                both = out[n * columns : (n + 1) * columns].astype(BF)
                nodes[side * 128 + n * 8 + c] = both[:, :128]
                nodes[side * 128 + n * 8 + c + 1] = both[:, 128:]

    lane = lane_numbers(columns)
    lane_node = iota((columns, 256), 1) & 7

    def couple(g):
        picked = []
        for i in range(8):
            parts = [nodes[spots_ref[s, g * 8 + i]] for s in range(6)]
            front = jnp.where(lane < 32, parts[0], parts[1])
            front = jnp.where(lane < 64, front, jnp.where(lane < 96, parts[2], parts[3]))
            back = jnp.where(lane < 32, parts[4], parts[5])
            back = jnp.where(lane < 64, back, jnp.zeros((), BF))
            picked.append(jnp.concatenate([front, back], axis=1))
        out = dot(jnp.concatenate(picked, axis=0), matrices_ref[g], NT)
        total = out[:columns]
        for i in range(1, 8):
            total = jnp.where(lane_node == i, out[i * columns : (i + 1) * columns], total)
        return total

    six = six_ref[...]
    down, at_points = [None] * 16, [None] * 8
    for k in reversed(range(16)):
        far = couple(k)
        if k == 15:
            five = far + dot(six.astype(BF), weights_ref[15], NT)
            five = jnp.where(lane_node >= 4, five, 0.0) + six
            parent = five.astype(BF)
        else:
            parent = down[8 + k // 2]
        down[k] = (far + dot(parent, weights_ref[k], NT)).astype(BF)
        if k < 8:
            at_points[k] = dot(down[k], masked_ref[k], NN)

    for copy in copies:
        copy.wait()
    groups = count // 4
    edge = REACH // 4
    for g in range(groups):
        if g < edge:
            blocks = edges[0, g * 4 : g * 4 + 4].reshape(256, 256)
        elif g >= groups - edge:
            at = (g - groups + edge) * 4
            blocks = edges[1, at : at + 4].reshape(256, 256)
        else:
            blocks = None
        if blocks is None:
            near = near_in[:, g * 256 : (g + 1) * 256]
        else:
            near = near_group(leaves, near_ref, blocks, g * 4, device * count - REACH, columns)
        half = at_points[g // 2][:, g % 2 * 256 : (g % 2 + 1) * 256]
        stacked[g * columns : (g + 1) * columns, :] = (near + half).astype(BF)

    writes = []
    for c in range(points // 256):
        applied_ref[:, c * 256 : (c + 1) * 256] = pick(
            stacked[...], hot_ref[c], inverse_ref[c : c + 1, :], columns
        )
        if c % 4 == 3:
            at = pl.ds((c - 3) * 256, 1024)
            writes.append(pltpu.make_async_copy(applied_ref.at[:, at], applied_hbm.at[:, at], out_sems.at[c // 4]))
            writes[-1].start()
    for write in writes:
        write.wait()


VMEM = pl.BlockSpec(memory_space=pltpu.VMEM)
SMEM = pl.BlockSpec(memory_space=pltpu.SMEM)


def in_hbm(x):
    return pltpu.with_memory_space_constraint(x, pltpu.HBM)


def call(kernel, outs, scratch, specs, flops, name, args, mib=16, out_specs=None):
    size = sum(a.size * a.dtype.itemsize for a in args)
    return pl.pallas_call(
        kernel,
        out_shape=[jax.ShapeDtypeStruct(s, t) for s, t in outs],
        in_specs=specs,
        out_specs=out_specs or [VMEM] * len(outs),
        scratch_shapes=scratch,
        compiler_params=pltpu.CompilerParams(vmem_limit_bytes=mib * 2**20),
        cost_estimate=pl.CostEstimate(flops=flops, bytes_accessed=0, transcendentals=0),
        name=name,
    )(*args)


def local(
    vectors, tree_order, leaf_basis, near_blocks, near_lists, transfers, couplings, coupling_lists,
    top_transfers, top_couplings, top_lists,
):
    columns, points = vectors.shape
    rank = leaf_basis.shape[0]
    devices = lax.axis_size("leaf")
    halo = REACH * near_blocks.shape[1]
    order = tree_order.reshape(points // 128, 128)
    near_t = jnp.transpose(near_lists)
    lists_t = jnp.transpose(coupling_lists)
    moves = transfers.reshape(rank * rank, -1)
    matrices = couplings.reshape(6, rank * rank, -1)

    any_spec = pl.BlockSpec(memory_space=pl.ANY)
    tile = max(devices // 2 * rank, 128)
    ordered, own0, masked = call(
        leaf_kernel,
        [((columns, points), BF), ((columns, halo + 2048), BF), ((points // 512, 256, 512), BF)],
        [
            pltpu.VMEM(vectors.shape, BF), pltpu.VMEM(order.shape, jnp.int32),
            pltpu.VMEM(leaf_basis.shape, BF), pltpu.VMEM((points // 256 * columns, 256), BF),
            pltpu.SemaphoreType.DMA((3,)),
        ],
        [any_spec] * 3, 10**9, "leaf", tuple(in_hbm(x) for x in (vectors, order, leaf_basis)),
    )
    pairs = [(i, i ^ 1) for i in range(devices)]
    onward = [(i, i + 2) for i in range(0, devices - 2, 2)] + [(i, i - 2) for i in range(3, devices, 2)]
    first0 = lax.ppermute(own0, "leaf", pairs)
    own1, top, weights = call(
        lift_kernel,
        [((columns, halo + 2048), BF), ((columns, tile), BF), ((16, 256, 256), BF)],
        [pltpu.VMEM((rank, 128, 256), F32)], [VMEM] * 3, 10**9, "lift", (own0, ordered, moves),
    )

    def step(tile_sum, reached):
        return lax.ppermute(tile_sum, "leaf", [(i, i ^ reached) for i in range(devices)])

    steps = [1 << k for k in reversed(range(1, devices.bit_length() - 1))]
    for reached in steps[:-2]:
        top = top + step(top, reached)
    other = step(top, steps[-2])
    coupling_rows, spots, hot, blocks = call(
        matrices_kernel,
        [
            ((16, 256, 256), BF), ((8, 128), jnp.int32), ((points // 256, 256, 256), BF),
            ((points // 256, 256), jnp.int32),
        ],
        [pltpu.VMEM((rank, 128, 256), F32)],
        [VMEM] * 3, 10**6, "matrices", (matrices, lists_t, order),
    )
    first1 = lax.ppermute(own1, "leaf", pairs)
    first0, top, blocks = lax.optimization_barrier((first0, top + other, blocks))
    other = step(top, steps[-1])
    second0 = lax.ppermute(first0, "leaf", onward)
    first1, top = lax.optimization_barrier((first1, top + other))
    other = step(top, 1)
    second1 = lax.ppermute(first1, "leaf", onward)
    first1, ordered = lax.optimization_barrier((first1, ordered))
    (near_part,) = call(
        near_kernel, [((columns, points), F32)],
        [pltpu.VMEM((points // 64, columns, 128), BF)],
        [VMEM, VMEM, SMEM], 10**6, "near", (ordered, near_blocks, near_t),
    )
    (six,) = call(
        root_kernel, [((columns, 256), F32)], [pltpu.VMEM((2 * devices, columns, 32), F32)],
        [VMEM] * 4 + [SMEM], 10**6, "root",
        (
            top, other, jnp.transpose(top_transfers, (2, 0, 1)), jnp.transpose(top_couplings, (0, 3, 1, 2)),
            jnp.transpose(top_lists),
        ),
    )
    (applied,) = call(
        outer_kernel,
        [((columns, points), F32)],
        [
            pltpu.VMEM((columns, points), F32), pltpu.VMEM((points // 64 + 2 * REACH, columns, 128), BF),
            pltpu.VMEM((385, columns, 128), BF),
            pltpu.VMEM((points // 256 * columns, 256), BF), pltpu.VMEM((16 * columns, 256), BF),
            pltpu.VMEM((2, REACH) + near_blocks.shape[1:], BF), pltpu.SemaphoreType.DMA((2,)),
            pltpu.SemaphoreType.DMA((points // 1024,)),
        ],
        [VMEM] * 8 + [any_spec, SMEM, VMEM, SMEM] + [VMEM] * 5,
        4 * 10**9, "outer",
        (
            ordered, own0, own1, first0, first1, second0, second1, near_part, in_hbm(near_blocks),
            near_t, coupling_rows, spots, blocks, weights, masked, hot, six,
        ),
        out_specs=[any_spec],
    )
    return applied


def solution(mesh):
    placed = (
        P("rhs", ("groups", "leaf")),
        P(("groups", "leaf")),
        P(None, ("groups", "leaf")),
        P(("groups", "leaf"), None, None),
        P(("groups", "leaf"), None),
        P(None, None, ("groups", "leaf")),
        P(None, None, None, ("groups", "leaf")),
        P(("groups", "leaf"), None),
        P(None, None, "groups"),
        P(None, None, None, "groups"),
        P("groups", None),
    )
    return jax.shard_map(
        local, mesh=mesh, in_specs=placed, out_specs=P("rhs", ("groups", "leaf")), check_vma=False
    )
```

```python
import functools

import jax
import jax.numpy as jnp
from jax import lax
from jax.experimental import pallas as pl
from jax.experimental.pallas import tpu as pltpu
from jax.sharding import PartitionSpec as P

LEVELS = 6
REACH = 8
BF = jnp.bfloat16
F32 = jnp.float32
NT = (((1,), (1,)), ((), ()))
NN = (((1,), (0,)), ((), ()))


def iota(shape, axis):
    return lax.broadcasted_iota(jnp.int32, shape, axis)


def dot(a, b, dims):
    return lax.dot_general(a, b, dims, preferred_element_type=F32)


def pad_lanes(x):
    short = 128 - x.shape[1]
    return jnp.concatenate([x, jnp.zeros((x.shape[0], short), x.dtype)], axis=1)


def one_hot(ids):
    ids = jnp.broadcast_to(ids.astype(F32), (16, 256)).astype(BF)
    rows = iota((256, 256), 0).astype(F32).astype(BF)
    return jnp.where(rows == jnp.concatenate([ids] * 16, axis=0), jnp.ones((), BF), jnp.zeros((), BF))


def split_ids(order_ref, c, points):
    ids = jnp.concatenate([order_ref[2 * c : 2 * c + 1, :], order_ref[2 * c + 1 : 2 * c + 2, :]], axis=1)
    ids = lax.rem(ids, points)
    return ids >> 8, ids & 255


def pick(stacked, hot, high, rows):
    out = dot(stacked, hot, NN).reshape(-1, rows // 8, 8, 256)
    high = jnp.broadcast_to(high, (8, 256))
    total = out[0]
    for block in range(1, out.shape[0]):
        total = jnp.where((high == block)[None], out[block], total)
    return total.reshape(rows, 256)


def leaf_kernel(
    vec_hbm, order_hbm, basis_hbm, ordered_ref, message_ref, masked_ref,
    vec_ref, order_ref, basis_ref, stacked, sems,
):
    columns, points = vec_ref.shape
    rank = basis_ref.shape[0]
    halo = REACH * 64
    pairs = ((order_hbm, order_ref), (vec_hbm, vec_ref), (basis_hbm, basis_ref))
    copies = [pltpu.make_async_copy(src, dst, sems.at[i]) for i, (src, dst) in enumerate(pairs)]
    for copy in copies:
        copy.start()
    copies[0].wait()
    copies[1].wait()
    for block in range(points // 256):
        stacked[block * columns : (block + 1) * columns, :] = vec_ref[:, block * 256 : (block + 1) * 256]
    for c in range(points // 256):
        high, low = split_ids(order_ref, c, points)
        ordered_ref[:, c * 256 : (c + 1) * 256] = pick(stacked[...], one_hot(low), high, columns).astype(BF)

    copies[2].wait()
    mine = (iota((256, 512), 0) & 7) == (iota((256, 512), 1) >> 6)
    for g in range(points // 512):
        one = basis_ref[:, g * 512 : (g + 1) * 512].astype(F32)
        eight = jnp.broadcast_to(one[:, None, :], (rank, 8, 512)).reshape(256, 512)
        masked = jnp.where(mine, eight, 0.0).astype(BF)
        masked_ref[g] = masked
        coeffs = dot(ordered_ref[:, g * 512 : (g + 1) * 512], masked, NT).astype(BF)
        message_ref[:, halo + g * 256 : halo + (g + 1) * 256] = coeffs
    odd = lax.axis_index("leaf") % 2 == 1
    message_ref[:, :halo] = jnp.where(odd, ordered_ref[:, :halo], ordered_ref[:, points - halo :])


def lift_kernel(message_ref, ordered_ref, transfer_ref, lifted_ref, top_ref, weights_ref, rows32):
    rank = 32
    base = REACH * 64
    points = ordered_ref.shape[1]
    odd = lax.axis_index("leaf") % 2 == 1
    lifted_ref[:, 2048:] = jnp.where(odd, ordered_ref[:, points - base :], ordered_ref[:, :base])

    lane, row = iota((128, 256), 1), iota((128, 256), 0)
    family = (lane & 7) == ((row >> 1) & 7)
    spread = [
        jnp.where(iota((128, 256), 0) == (iota((128, 256), 1) >> 3) + 32 * q, 1.0, 0.0).astype(BF)
        for q in range(4)
    ]
    for m in range(rank // 4):
        turned = pad_lanes(transfer_ref[m * 4 * rank : (m + 1) * 4 * rank, :].astype(F32)).T.astype(BF)
        for q in range(4):
            rows32[m * 4 + q] = jnp.where(family, dot(turned, spread[q], NN), 0.0)
    for k in range(16):
        weights_ref[k] = rows32[:, k * 8 : k * 8 + 8, :].reshape(256, 256).astype(BF)
    coeffs = [message_ref[:, base + g * 256 : base + (g + 1) * 256] for g in range(8)] + [None] * 8
    for n in range(7):
        lifted = dot(coeffs[2 * n], weights_ref[2 * n], NN) + dot(coeffs[2 * n + 1], weights_ref[2 * n + 1], NN)
        coeffs[8 + n] = lifted.astype(BF)
    four = dot(coeffs[14], weights_ref[14], NN)
    five = dot(four.astype(BF), weights_ref[15], NN)
    six = dot((four + five).astype(BF), weights_ref[15], NN)
    coeffs[15] = (four + six).astype(BF)
    width = top_ref.shape[1]
    slot = lax.axis_index("leaf") // 2 * rank
    row, lane = iota((256, width), 0), iota((256, width), 1) - slot
    root = jnp.where((row == lane * 8 + 6) & (lane >= 0), 1.0, 0.0).astype(BF)
    top_ref[...] = dot(coeffs[15], root, NN).astype(BF)
    for g in range(8):
        lifted_ref[:, g * 256 : (g + 1) * 256] = coeffs[8 + g]


def lane_numbers(rows):
    return iota((rows, 128), 1).astype(F32).astype(BF)


def near_group(leaves_ref, lists_ref, blocks, first, base, columns):
    lane_left = lane_numbers(columns) < 64
    picked = []
    for i in range(4):
        spots = [lists_ref[s, first + i] - base for s in range(4)]
        halves = []
        for s in (0, 2):
            even = leaves_ref[spots[s]]
            odd = leaves_ref[spots[s + 1] ^ 1]
            halves.append(jnp.where(lane_left, even, odd))
        picked.append(jnp.concatenate(halves, axis=1))
    out = dot(jnp.concatenate(picked, axis=0), blocks, NT)
    leaf_of_lane = iota((columns, 256), 1) >> 6
    total = out[:columns]
    for i in range(1, 4):
        total = jnp.where(leaf_of_lane == i, out[i * columns : (i + 1) * columns], total)
    return total


def place_leaves(leaves_ref, first, chunk):
    leaves_ref[first] = chunk
    leaves_ref[first + 1] = pltpu.roll(chunk.astype(F32), 64, 1).astype(BF)


def matrices_kernel(
    coupling_ref, lists_ref, order_ref, matrices_ref, spots_ref, hot_ref, blocks_ref, rows32,
):
    rank = 32
    device = lax.axis_index("leaf")
    count = 64
    chunks = hot_ref.shape[0]

    within = iota((16, 256), 1).astype(F32)
    inverse = jnp.zeros((32, 256), F32)
    for c in range(chunks):
        high, low = split_ids(order_ref, c, chunks * 256)
        hit = iota((16, 256), 0) == jnp.broadcast_to(high, (16, 256))
        marks = jnp.concatenate([jnp.where(hit, float(c), 0.0), jnp.where(hit, within, 0.0)], axis=0)
        inverse = inverse + dot(marks.astype(BF), one_hot(low), NT)
    inverse = inverse.astype(jnp.int32)
    blocks_ref[...] = inverse[:16]
    for c in range(chunks):
        hot_ref[c] = one_hot(inverse[16 + c : 17 + c, :])

    node = iota((1, 128), 1)
    size = jnp.full((1, 128), count, jnp.int32)
    start = jnp.zeros((1, 128), jnp.int32)
    offset = 0
    for level in range(LEVELS):
        size = jnp.where(node >= offset, count >> level, size)
        start = jnp.where(node >= offset, offset, start)
        offset += count >> level
    entries = pad_lanes(lists_ref[...])
    for s in range(6):
        entry = entries[s : s + 1]
        place = entry - device * size + size
        side = jnp.where(place >= size, 1, 0) + jnp.where(place >= 2 * size, 1, 0)
        spot = side * 128 + start + place - side * size
        used = (entry >= 0) & (node < offset)
        spots_ref[pl.ds(s, 1), :] = jnp.where(used, spot, 3 * 128)
    spots_ref[pl.ds(6, 2), :] = jnp.zeros((2, 128), jnp.int32)

    for a in range(rank):
        one = [coupling_ref[s, a * rank : (a + 1) * rank, :].astype(F32) for s in range(6)]
        full = pad_lanes(jnp.concatenate(one, axis=0))
        turned = jnp.concatenate([full[:128].T, pad_lanes(full[128:].T)], axis=1)
        rows32[a] = turned
    for g in range(16):
        matrices_ref[g] = rows32[:, g * 8 : g * 8 + 8, :].reshape(256, 256).astype(BF)


def near_kernel(ordered_ref, blocks_ref, near_ref, near_out, leaves):
    columns, points = ordered_ref.shape
    count = blocks_ref.shape[0]
    device = lax.axis_index("leaf")
    for c in range(count // 2):
        place_leaves(leaves, c * 2, ordered_ref[:, c * 128 : (c + 1) * 128])
    edge = REACH // 4
    near_out[:, : edge * 256] = jnp.zeros((columns, edge * 256), F32)
    near_out[:, points - edge * 256 :] = jnp.zeros((columns, edge * 256), F32)

    def near(g, carry):
        blocks = blocks_ref[pl.ds(g * 4, 4)].reshape(256, 256)
        at = pl.multiple_of(g * 256, 256)
        near_out[:, pl.ds(at, 256)] = near_group(
            leaves, near_ref, blocks, g * 4, device * count, columns
        )
        return carry

    lax.fori_loop(edge, count // 4 - edge, near, 0, unroll=4)


def root_kernel(own_ref, other_ref, transfer_ref, coupling_ref, lists_ref, six_ref, coeffs):
    columns, rank = own_ref.shape[0], 32
    node_count = lists_ref.shape[1] // 2 + 1
    device = lax.axis_index("leaf")
    total = 2 * node_count - 1
    coeffs[total] = jnp.zeros((columns, rank), F32)
    for q in range(node_count):
        ref = own_ref if q % 2 == 0 else other_ref
        at = q // 2 * rank
        coeffs[q ^ (device & 1)] = ref[:, at : at + rank].astype(F32)
    values = [coeffs[j].astype(BF) for j in range(node_count)]
    start, count = 0, node_count
    starts = [(0, node_count)]
    while count > 1:
        for j in range(count // 2):
            left, right = start + 2 * j, start + 2 * j + 1
            lifted = dot(values[left], transfer_ref[left], NN) + dot(values[right], transfer_ref[right], NN)
            values.append(lifted.astype(BF))
            coeffs[start + count + j] = values[-1].astype(F32)
        start, count = start + count, count // 2
        starts.append((start, count))
    fields = []
    for level, (start, count) in enumerate(starts):
        node = start + (device >> level)
        field = None
        for s in range(6):
            entry = lists_ref[s, node]
            spot = jnp.where(entry >= 0, start + entry, total)
            term = dot(coeffs[spot].astype(BF), coupling_ref[s, node], NT)
            field = term if field is None else field + term
        fields.append((node, field))
    down = fields.pop()[1].astype(BF)
    for node, field in reversed(fields):
        down = (field + dot(down, transfer_ref[node], NT)).astype(BF)
    sixth = jnp.where(iota((32, 256), 1) == iota((32, 256), 0) * 8 + 6, 1.0, 0.0).astype(BF)
    six_ref[...] = dot(down, sixth, NN)


def far_kernel(
    ordered_ref, own0_ref, own1_ref, first0_ref, first1_ref, second0_ref, second1_ref, blocks_ref,
    near_ref, matrices_ref, spots_ref,
    far, edge_out,
    leaves, nodes, stacked_nodes, edges, sems,
):
    columns, points = ordered_ref.shape
    halo = REACH * 64
    device = lax.axis_index("leaf")
    count = points // 64
    copies = [
        pltpu.make_async_copy(blocks_ref.at[pl.ds(at, REACH)], edges.at[i], sems.at[i])
        for i, at in enumerate((0, count - REACH))
    ]
    for copy in copies:
        copy.start()

    odd = device % 2
    for ref, start, right in ((first0_ref, 0, 1 - odd), (second1_ref, 2048, odd)):
        for c in range(halo // 128):
            at = start + c * 128
            place_leaves(leaves, right * (REACH + count) + c * 2, ref[:, at : at + 128])
    near_ends = REACH * 64 * 2 // 128
    for c in list(range(near_ends)) + list(range(count // 2 - near_ends, count // 2)):
        place_leaves(leaves, REACH + c * 2, ordered_ref[:, c * 128 : (c + 1) * 128])

    nodes[3 * 128] = jnp.zeros((columns, 128), BF)
    lane, row = iota((256, 1024), 1), iota((256, 1024), 0)
    spread = jnp.where(row == (lane & 31) * 8 + (lane >> 7), 1.0, 0.0).astype(BF)
    sources = (
        (1, own0_ref, own1_ref), (2 - 2 * odd, first0_ref, first1_ref), (2 * odd, second0_ref, second1_ref),
    )
    for side, ref0, ref1 in sources:
        for n in range(8):
            at = halo + n * 256
            stacked_nodes[n * columns : (n + 1) * columns, :] = ref0[:, at : at + 256]
            stacked_nodes[(8 + n) * columns : (9 + n) * columns, :] = ref1[:, n * 256 : (n + 1) * 256]
        for c in range(0, 8, 2):
            out = dot(stacked_nodes[...], spread[:, c * 128 : (c + 2) * 128], NN)
            for n in range(16):
                both = out[n * columns : (n + 1) * columns].astype(BF)
                nodes[side * 128 + n * 8 + c] = both[:, :128]
                nodes[side * 128 + n * 8 + c + 1] = both[:, 128:]

    lane = lane_numbers(columns)
    lane_node = iota((columns, 256), 1) & 7

    for g in range(16):
        picked = []
        for i in range(8):
            parts = [nodes[spots_ref[s, g * 8 + i]] for s in range(6)]
            front = jnp.where(lane < 32, parts[0], parts[1])
            front = jnp.where(lane < 64, front, jnp.where(lane < 96, parts[2], parts[3]))
            back = jnp.where(lane < 32, parts[4], parts[5])
            back = jnp.where(lane < 64, back, jnp.zeros((), BF))
            picked.append(jnp.concatenate([front, back], axis=1))
        out = dot(jnp.concatenate(picked, axis=0), matrices_ref[g], NT)
        total = out[:columns]
        for i in range(1, 8):
            total = jnp.where(lane_node == i, out[i * columns : (i + 1) * columns], total)
        far[:, g * 256 : (g + 1) * 256] = total

    for copy in copies:
        copy.wait()
    groups = count // 4
    edge = REACH // 4
    for e in range(2 * edge):
        g = e if e < edge else groups - 2 * edge + e
        at = e % edge * 4
        blocks = edges[e // edge, at : at + 4].reshape(256, 256)
        edge_out[:, e * 256 : (e + 1) * 256] = near_group(
            leaves, near_ref, blocks, g * 4, device * count - REACH, columns
        )


def down_kernel(
    far, near_in, edge_in, six_ref, inverse_ref, weights_ref, masked_ref, hot_ref,
    applied_hbm,
    applied_ref, stacked, out_sems,
):
    columns, points = near_in.shape
    lane_node = iota((columns, 256), 1) & 7
    six = six_ref[...]
    down = [None] * 16
    last = far[:, 15 * 256 :]
    five = last + dot(six.astype(BF), weights_ref[15], NT)
    five = jnp.where(lane_node >= 4, five, 0.0) + six
    down[15] = (last + dot(five.astype(BF), weights_ref[15], NT)).astype(BF)
    for k in reversed(range(15)):
        down[k] = (far[:, k * 256 : (k + 1) * 256] + dot(down[8 + k // 2], weights_ref[k], NT)).astype(BF)
    groups = points // 256
    edge = REACH // 4
    for g in range(groups):
        if g < edge:
            near = edge_in[:, g * 256 : (g + 1) * 256]
        elif g >= groups - edge:
            at = (g - groups + 2 * edge) * 256
            near = edge_in[:, at : at + 256]
        else:
            near = near_in[:, g * 256 : (g + 1) * 256]
        if g % 2 == 0:
            at_points = dot(down[g // 2], masked_ref[g // 2], NN)
        half = at_points[:, g % 2 * 256 : (g % 2 + 1) * 256]
        stacked[g * columns : (g + 1) * columns, :] = (near + half).astype(BF)

    writes = []
    for c in range(points // 256):
        applied_ref[:, c * 256 : (c + 1) * 256] = pick(
            stacked[...], hot_ref[c], inverse_ref[c : c + 1, :], columns
        )
        if c % 4 == 3:
            at = pl.ds((c - 3) * 256, 1024)
            writes.append(pltpu.make_async_copy(applied_ref.at[:, at], applied_hbm.at[:, at], out_sems.at[c // 4]))
            writes[-1].start()
    for write in writes:
        write.wait()


VMEM = pl.BlockSpec(memory_space=pltpu.VMEM)
SMEM = pl.BlockSpec(memory_space=pltpu.SMEM)


def in_hbm(x):
    return pltpu.with_memory_space_constraint(x, pltpu.HBM)


def call(kernel, outs, scratch, specs, flops, name, args, mib=16, out_specs=None):
    size = sum(a.size * a.dtype.itemsize for a in args)
    return pl.pallas_call(
        kernel,
        out_shape=[jax.ShapeDtypeStruct(s, t) for s, t in outs],
        in_specs=specs,
        out_specs=out_specs or [VMEM] * len(outs),
        scratch_shapes=scratch,
        compiler_params=pltpu.CompilerParams(vmem_limit_bytes=mib * 2**20),
        cost_estimate=pl.CostEstimate(flops=flops, bytes_accessed=0, transcendentals=0),
        name=name,
    )(*args)


def local(
    vectors, tree_order, leaf_basis, near_blocks, near_lists, transfers, couplings, coupling_lists,
    top_transfers, top_couplings, top_lists,
):
    columns, points = vectors.shape
    rank = leaf_basis.shape[0]
    devices = lax.axis_size("leaf")
    halo = REACH * near_blocks.shape[1]
    order = tree_order.reshape(points // 128, 128)
    near_t = jnp.transpose(near_lists)
    lists_t = jnp.transpose(coupling_lists)
    moves = transfers.reshape(rank * rank, -1)
    matrices = couplings.reshape(6, rank * rank, -1)

    any_spec = pl.BlockSpec(memory_space=pl.ANY)
    tile = max(devices // 2 * rank, 128)
    ordered, own0, masked = call(
        leaf_kernel,
        [((columns, points), BF), ((columns, halo + 2048), BF), ((points // 512, 256, 512), BF)],
        [
            pltpu.VMEM(vectors.shape, BF), pltpu.VMEM(order.shape, jnp.int32),
            pltpu.VMEM(leaf_basis.shape, BF), pltpu.VMEM((points // 256 * columns, 256), BF),
            pltpu.SemaphoreType.DMA((3,)),
        ],
        [any_spec] * 3, 10**9, "leaf", tuple(in_hbm(x) for x in (vectors, order, leaf_basis)),
    )
    pairs = [(i, i ^ 1) for i in range(devices)]
    onward = [(i, i + 2) for i in range(0, devices - 2, 2)] + [(i, i - 2) for i in range(3, devices, 2)]
    first0 = lax.ppermute(own0, "leaf", pairs)
    own1, top, weights = call(
        lift_kernel,
        [((columns, halo + 2048), BF), ((columns, tile), BF), ((16, 256, 256), BF)],
        [pltpu.VMEM((rank, 128, 256), F32)], [VMEM] * 3, 10**9, "lift", (own0, ordered, moves),
    )

    def step(tile_sum, reached):
        return lax.ppermute(tile_sum, "leaf", [(i, i ^ reached) for i in range(devices)])

    steps = [1 << k for k in reversed(range(1, devices.bit_length() - 1))]
    for reached in steps[:-2]:
        top = top + step(top, reached)
    other = step(top, steps[-2])
    coupling_rows, spots, hot, blocks = call(
        matrices_kernel,
        [
            ((16, 256, 256), BF), ((8, 128), jnp.int32), ((points // 256, 256, 256), BF),
            ((points // 256, 256), jnp.int32),
        ],
        [pltpu.VMEM((rank, 128, 256), F32)],
        [VMEM] * 3, 10**6, "matrices", (matrices, lists_t, order),
    )
    first1 = lax.ppermute(own1, "leaf", pairs)
    first0, top, blocks = lax.optimization_barrier((first0, top + other, blocks))
    other = step(top, steps[-1])
    second0 = lax.ppermute(first0, "leaf", onward)
    first1, top = lax.optimization_barrier((first1, top + other))
    other = step(top, 1)
    second1 = lax.ppermute(first1, "leaf", onward)
    first1, ordered = lax.optimization_barrier((first1, ordered))
    (near_part,) = call(
        near_kernel, [((columns, points), F32)],
        [pltpu.VMEM((points // 64, columns, 128), BF)],
        [VMEM, VMEM, SMEM], 10**6, "near", (ordered, near_blocks, near_t),
    )
    far, edge_part = call(
        far_kernel, [((columns, 4096), F32), ((columns, 2 * halo), F32)],
        [
            pltpu.VMEM((points // 64 + 2 * REACH, columns, 128), BF),
            pltpu.VMEM((385, columns, 128), BF), pltpu.VMEM((16 * columns, 256), BF),
            pltpu.VMEM((2, REACH) + near_blocks.shape[1:], BF), pltpu.SemaphoreType.DMA((2,)),
        ],
        [VMEM] * 7 + [any_spec, SMEM, VMEM, SMEM], 4 * 10**9, "far",
        (
            ordered, own0, own1, first0, first1, second0, second1, in_hbm(near_blocks),
            near_t, coupling_rows, spots,
        ),
    )
    other, far = lax.optimization_barrier((other, far))
    (six,) = call(
        root_kernel, [((columns, 256), F32)], [pltpu.VMEM((2 * devices, columns, 32), F32)],
        [VMEM] * 4 + [SMEM], 10**6, "root",
        (
            top, other, jnp.transpose(top_transfers, (2, 0, 1)), jnp.transpose(top_couplings, (0, 3, 1, 2)),
            jnp.transpose(top_lists),
        ),
    )
    (applied,) = call(
        down_kernel, [((columns, points), F32)],
        [
            pltpu.VMEM((columns, points), F32), pltpu.VMEM((points // 256 * columns, 256), BF),
            pltpu.SemaphoreType.DMA((points // 1024,)),
        ],
        [VMEM] * 8, 4 * 10**9, "down", (far, near_part, edge_part, six, blocks, weights, masked, hot),
        out_specs=[any_spec],
    )
    return applied


def solution(mesh):
    placed = (
        P("rhs", ("groups", "leaf")),
        P(("groups", "leaf")),
        P(None, ("groups", "leaf")),
        P(("groups", "leaf"), None, None),
        P(("groups", "leaf"), None),
        P(None, None, ("groups", "leaf")),
        P(None, None, None, ("groups", "leaf")),
        P(("groups", "leaf"), None),
        P(None, None, "groups"),
        P(None, None, None, "groups"),
        P("groups", None),
    )
    return jax.shard_map(
        local, mesh=mesh, in_specs=placed, out_specs=P("rhs", ("groups", "leaf")), check_vma=False
    )
```

```python
import functools

import jax
import jax.numpy as jnp
from jax import lax
from jax.experimental import pallas as pl
from jax.experimental.pallas import tpu as pltpu
from jax.sharding import PartitionSpec as P

LEVELS = 6
REACH = 8
BF = jnp.bfloat16
F32 = jnp.float32
NT = (((1,), (1,)), ((), ()))
NN = (((1,), (0,)), ((), ()))


def iota(shape, axis):
    return lax.broadcasted_iota(jnp.int32, shape, axis)


def dot(a, b, dims):
    return lax.dot_general(a, b, dims, preferred_element_type=F32)


def pad_lanes(x):
    short = 128 - x.shape[1]
    return jnp.concatenate([x, jnp.zeros((x.shape[0], short), x.dtype)], axis=1)


def one_hot(ids):
    ids = jnp.broadcast_to(ids.astype(F32), (16, 256)).astype(BF)
    rows = iota((256, 256), 0).astype(F32).astype(BF)
    return jnp.where(rows == jnp.concatenate([ids] * 16, axis=0), jnp.ones((), BF), jnp.zeros((), BF))


def split_ids(order_ref, c, points):
    ids = jnp.concatenate([order_ref[2 * c : 2 * c + 1, :], order_ref[2 * c + 1 : 2 * c + 2, :]], axis=1)
    ids = lax.rem(ids, points)
    return ids >> 8, ids & 255


def pick(stacked, hot, high, rows):
    out = dot(stacked, hot, NN).reshape(-1, rows // 8, 8, 256)
    high = jnp.broadcast_to(high, (8, 256))
    total = out[0]
    for block in range(1, out.shape[0]):
        total = jnp.where((high == block)[None], out[block], total)
    return total.reshape(rows, 256)


def leaf_kernel(
    vec_hbm, order_hbm, basis_hbm, ordered_ref, zero_ref, masked_ref,
    vec_ref, order_ref, basis_ref, stacked, sems,
):
    columns, points = vec_ref.shape
    rank = basis_ref.shape[0]
    pairs = ((order_hbm, order_ref), (vec_hbm, vec_ref), (basis_hbm, basis_ref))
    copies = [pltpu.make_async_copy(src, dst, sems.at[i]) for i, (src, dst) in enumerate(pairs)]
    for copy in copies:
        copy.start()
    for copy in copies:
        copy.wait()
    for block in range(points // 256):
        stacked[block * columns : (block + 1) * columns, :] = vec_ref[:, block * 256 : (block + 1) * 256]
    for c in range(points // 256):
        high, low = split_ids(order_ref, c, points)
        ordered_ref[:, c * 256 : (c + 1) * 256] = pick(stacked[...], one_hot(low), high, columns).astype(BF)

    mine = (iota((256, 512), 0) & 7) == (iota((256, 512), 1) >> 6)
    for g in range(points // 512):
        one = basis_ref[:, g * 512 : (g + 1) * 512].astype(F32)
        eight = jnp.broadcast_to(one[:, None, :], (rank, 8, 512)).reshape(256, 512)
        masked = jnp.where(mine, eight, 0.0).astype(BF)
        masked_ref[g] = masked
        coeffs = dot(ordered_ref[:, g * 512 : (g + 1) * 512], masked, NT).astype(BF)
        zero_ref[:, g * 256 : (g + 1) * 256] = coeffs
    halo = zero_ref.shape[1] - 2048
    odd = lax.axis_index("leaf") % 2 == 1
    zero_ref[:, 2048:] = jnp.where(odd, ordered_ref[:, points - halo :], ordered_ref[:, :halo])


def lift_kernel(zero_ref, ordered_ref, transfer_ref, lifted_ref, top_ref, last_ref, weights_ref, rows32):
    rank = 32
    base = REACH * 64
    points = ordered_ref.shape[1]
    odd = lax.axis_index("leaf") % 2 == 1
    low, high = ordered_ref[:, :base], ordered_ref[:, points - base :]
    last_ref[:, top_ref.shape[1] :] = jnp.where(odd, low, high)
    last_ref[:, : top_ref.shape[1]] = jnp.zeros(top_ref.shape, BF)

    lane, row = iota((128, 256), 1), iota((128, 256), 0)
    family = (lane & 7) == ((row >> 1) & 7)
    spread = [
        jnp.where(iota((128, 256), 0) == (iota((128, 256), 1) >> 3) + 32 * q, 1.0, 0.0).astype(BF)
        for q in range(4)
    ]
    for m in range(rank // 4):
        turned = pad_lanes(transfer_ref[m * 4 * rank : (m + 1) * 4 * rank, :].astype(F32)).T.astype(BF)
        for q in range(4):
            rows32[m * 4 + q] = jnp.where(family, dot(turned, spread[q], NN), 0.0)
    for k in range(16):
        weights_ref[k] = rows32[:, k * 8 : k * 8 + 8, :].reshape(256, 256).astype(BF)
    coeffs = [zero_ref[:, g * 256 : (g + 1) * 256] for g in range(8)] + [None] * 8
    for n in range(7):
        lifted = dot(coeffs[2 * n], weights_ref[2 * n], NN) + dot(coeffs[2 * n + 1], weights_ref[2 * n + 1], NN)
        coeffs[8 + n] = lifted.astype(BF)
    four = dot(coeffs[14], weights_ref[14], NN)
    five = dot(four.astype(BF), weights_ref[15], NN)
    six = dot((four + five).astype(BF), weights_ref[15], NN)
    coeffs[15] = (four + six).astype(BF)
    width = top_ref.shape[1]
    slot = lax.axis_index("leaf") // 2 * rank
    row, lane = iota((256, width), 0), iota((256, width), 1) - slot
    root = jnp.where((row == lane * 8 + 6) & (lane >= 0), 1.0, 0.0).astype(BF)
    top_ref[...] = dot(coeffs[15], root, NN).astype(BF)
    for g in range(8):
        lifted_ref[:, g * 256 : (g + 1) * 256] = coeffs[8 + g]


def lane_numbers(rows):
    return iota((rows, 128), 1).astype(F32).astype(BF)


def near_group(leaves_ref, lists_ref, blocks, first, base, columns):
    lane_left = lane_numbers(columns) < 64
    picked = []
    for i in range(4):
        spots = [lists_ref[s, first + i] - base for s in range(4)]
        halves = []
        for s in (0, 2):
            even = leaves_ref[spots[s]]
            odd = leaves_ref[spots[s + 1] ^ 1]
            halves.append(jnp.where(lane_left, even, odd))
        picked.append(jnp.concatenate(halves, axis=1))
    out = dot(jnp.concatenate(picked, axis=0), blocks, NT)
    leaf_of_lane = iota((columns, 256), 1) >> 6
    total = out[:columns]
    for i in range(1, 4):
        total = jnp.where(leaf_of_lane == i, out[i * columns : (i + 1) * columns], total)
    return total


def place_leaves(leaves_ref, first, chunk):
    leaves_ref[first] = chunk
    leaves_ref[first + 1] = pltpu.roll(chunk.astype(F32), 64, 1).astype(BF)


def matrices_kernel(
    coupling_ref, lists_ref, order_ref, matrices_ref, spots_ref, hot_ref, blocks_ref, rows32,
):
    rank = 32
    device = lax.axis_index("leaf")
    count = 64
    chunks = hot_ref.shape[0]

    within = iota((16, 256), 1).astype(F32)
    inverse = jnp.zeros((32, 256), F32)
    for c in range(chunks):
        high, low = split_ids(order_ref, c, chunks * 256)
        hit = iota((16, 256), 0) == jnp.broadcast_to(high, (16, 256))
        marks = jnp.concatenate([jnp.where(hit, float(c), 0.0), jnp.where(hit, within, 0.0)], axis=0)
        inverse = inverse + dot(marks.astype(BF), one_hot(low), NT)
    inverse = inverse.astype(jnp.int32)
    blocks_ref[...] = inverse[:16]
    for c in range(chunks):
        hot_ref[c] = one_hot(inverse[16 + c : 17 + c, :])

    node = iota((1, 128), 1)
    size = jnp.full((1, 128), count, jnp.int32)
    start = jnp.zeros((1, 128), jnp.int32)
    offset = 0
    for level in range(LEVELS):
        size = jnp.where(node >= offset, count >> level, size)
        start = jnp.where(node >= offset, offset, start)
        offset += count >> level
    entries = pad_lanes(lists_ref[...])
    for s in range(6):
        entry = entries[s : s + 1]
        place = entry - device * size + size
        side = jnp.where(place >= size, 1, 0) + jnp.where(place >= 2 * size, 1, 0)
        spot = side * 128 + start + place - side * size
        used = (entry >= 0) & (node < offset)
        spots_ref[pl.ds(s, 1), :] = jnp.where(used, spot, 3 * 128)
    spots_ref[pl.ds(6, 2), :] = jnp.zeros((2, 128), jnp.int32)

    for a in range(rank):
        one = [coupling_ref[s, a * rank : (a + 1) * rank, :].astype(F32) for s in range(6)]
        full = pad_lanes(jnp.concatenate(one, axis=0))
        turned = jnp.concatenate([full[:128].T, pad_lanes(full[128:].T)], axis=1)
        rows32[a] = turned
    for g in range(16):
        matrices_ref[g] = rows32[:, g * 8 : g * 8 + 8, :].reshape(256, 256).astype(BF)


def near_kernel(ordered_ref, blocks_ref, near_ref, near_out, leaves):
    columns, points = ordered_ref.shape
    count = blocks_ref.shape[0]
    device = lax.axis_index("leaf")
    for c in range(count // 2):
        place_leaves(leaves, c * 2, ordered_ref[:, c * 128 : (c + 1) * 128])
    edge = REACH // 4
    near_out[:, : edge * 256] = jnp.zeros((columns, edge * 256), F32)
    near_out[:, points - edge * 256 :] = jnp.zeros((columns, edge * 256), F32)

    def near(g, carry):
        blocks = blocks_ref[pl.ds(g * 4, 4)].reshape(256, 256)
        at = pl.multiple_of(g * 256, 256)
        near_out[:, pl.ds(at, 256)] = near_group(
            leaves, near_ref, blocks, g * 4, device * count, columns
        )
        return carry

    lax.fori_loop(edge, count // 4 - edge, near, 0, unroll=4)


def root_kernel(own_ref, other_ref, transfer_ref, coupling_ref, lists_ref, six_ref, coeffs):
    columns, rank = own_ref.shape[0], 32
    node_count = lists_ref.shape[1] // 2 + 1
    device = lax.axis_index("leaf")
    total = 2 * node_count - 1
    coeffs[total] = jnp.zeros((columns, rank), F32)
    for q in range(node_count):
        ref = own_ref if q % 2 == 0 else other_ref
        at = q // 2 * rank
        coeffs[q ^ (device & 1)] = ref[:, at : at + rank].astype(F32)
    values = [coeffs[j].astype(BF) for j in range(node_count)]
    start, count = 0, node_count
    starts = [(0, node_count)]
    while count > 1:
        for j in range(count // 2):
            left, right = start + 2 * j, start + 2 * j + 1
            lifted = dot(values[left], transfer_ref[left], NN) + dot(values[right], transfer_ref[right], NN)
            values.append(lifted.astype(BF))
            coeffs[start + count + j] = values[-1].astype(F32)
        start, count = start + count, count // 2
        starts.append((start, count))
    fields = []
    for level, (start, count) in enumerate(starts):
        node = start + (device >> level)
        field = None
        for s in range(6):
            entry = lists_ref[s, node]
            spot = jnp.where(entry >= 0, start + entry, total)
            term = dot(coeffs[spot].astype(BF), coupling_ref[s, node], NT)
            field = term if field is None else field + term
        fields.append((node, field))
    down = fields.pop()[1].astype(BF)
    for node, field in reversed(fields):
        down = (field + dot(down, transfer_ref[node], NT)).astype(BF)
    sixth = jnp.where(iota((32, 256), 1) == iota((32, 256), 0) * 8 + 6, 1.0, 0.0).astype(BF)
    six_ref[...] = dot(down, sixth, NN)


def far_kernel(
    own0_ref, own1_ref, first0_ref, first1_ref, second0_ref, second1_ref, matrices_ref, spots_ref,
    far, nodes, stacked_nodes,
):
    columns = far.shape[0]
    odd = lax.axis_index("leaf") % 2

    nodes[3 * 128] = jnp.zeros((columns, 128), BF)
    lane, row = iota((256, 1024), 1), iota((256, 1024), 0)
    spread = jnp.where(row == (lane & 31) * 8 + (lane >> 7), 1.0, 0.0).astype(BF)
    sources = (
        (1, own0_ref, own1_ref), (2 - 2 * odd, first0_ref, first1_ref), (2 * odd, second0_ref, second1_ref),
    )
    for side, ref0, ref1 in sources:
        for n in range(8):
            stacked_nodes[n * columns : (n + 1) * columns, :] = ref0[:, n * 256 : (n + 1) * 256]
            stacked_nodes[(8 + n) * columns : (9 + n) * columns, :] = ref1[:, n * 256 : (n + 1) * 256]
        for c in range(0, 8, 2):
            out = dot(stacked_nodes[...], spread[:, c * 128 : (c + 2) * 128], NN)
            for n in range(16):
                both = out[n * columns : (n + 1) * columns].astype(BF)
                nodes[side * 128 + n * 8 + c] = both[:, :128]
                nodes[side * 128 + n * 8 + c + 1] = both[:, 128:]

    lane = lane_numbers(columns)
    lane_node = iota((columns, 256), 1) & 7

    for g in range(16):
        picked = []
        for i in range(8):
            parts = [nodes[spots_ref[s, g * 8 + i]] for s in range(6)]
            front = jnp.where(lane < 32, parts[0], parts[1])
            front = jnp.where(lane < 64, front, jnp.where(lane < 96, parts[2], parts[3]))
            back = jnp.where(lane < 32, parts[4], parts[5])
            back = jnp.where(lane < 64, back, jnp.zeros((), BF))
            picked.append(jnp.concatenate([front, back], axis=1))
        out = dot(jnp.concatenate(picked, axis=0), matrices_ref[g], NT)
        total = out[:columns]
        for i in range(1, 8):
            total = jnp.where(lane_node == i, out[i * columns : (i + 1) * columns], total)
        far[:, g * 256 : (g + 1) * 256] = total


def down_kernel(
    far, near_in, ordered_ref, last_ref, second0_ref, blocks_ref, near_ref,
    six_ref, inverse_ref, weights_ref, masked_ref, hot_ref,
    applied_hbm,
    applied_ref, leaves, stacked, edges, sems, out_sems,
):
    columns, points = near_in.shape
    halo = REACH * 64
    device = lax.axis_index("leaf")
    count = points // 64
    copies = [
        pltpu.make_async_copy(blocks_ref.at[pl.ds(at, REACH)], edges.at[i], sems.at[i])
        for i, at in enumerate((0, count - REACH))
    ]
    for copy in copies:
        copy.start()

    odd = device % 2
    for ref, start, right in ((last_ref, last_ref.shape[1] - halo, 1 - odd), (second0_ref, 2048, odd)):
        for c in range(halo // 128):
            at = start + c * 128
            place_leaves(leaves, right * (REACH + count) + c * 2, ref[:, at : at + 128])
    near_ends = REACH * 64 * 2 // 128
    for c in list(range(near_ends)) + list(range(count // 2 - near_ends, count // 2)):
        place_leaves(leaves, REACH + c * 2, ordered_ref[:, c * 128 : (c + 1) * 128])

    lane_node = iota((columns, 256), 1) & 7
    six = six_ref[...]
    down = [None] * 16
    last = far[:, 15 * 256 :]
    five = last + dot(six.astype(BF), weights_ref[15], NT)
    five = jnp.where(lane_node >= 4, five, 0.0) + six
    down[15] = (last + dot(five.astype(BF), weights_ref[15], NT)).astype(BF)
    for k in reversed(range(15)):
        down[k] = (far[:, k * 256 : (k + 1) * 256] + dot(down[8 + k // 2], weights_ref[k], NT)).astype(BF)
    for copy in copies:
        copy.wait()
    groups = points // 256
    edge = REACH // 4
    for g in range(groups):
        if edge <= g < groups - edge:
            near = near_in[:, g * 256 : (g + 1) * 256]
        else:
            at = g if g < edge else g - groups + edge
            blocks = edges[0 if g < edge else 1, at * 4 : at * 4 + 4].reshape(256, 256)
            near = near_group(leaves, near_ref, blocks, g * 4, device * count - REACH, columns)
        if g % 2 == 0:
            at_points = dot(down[g // 2], masked_ref[g // 2], NN)
        half = at_points[:, g % 2 * 256 : (g % 2 + 1) * 256]
        stacked[g * columns : (g + 1) * columns, :] = (near + half).astype(BF)

    writes = []
    for c in range(points // 256):
        applied_ref[:, c * 256 : (c + 1) * 256] = pick(
            stacked[...], hot_ref[c], inverse_ref[c : c + 1, :], columns
        )
        if c % 4 == 3:
            at = pl.ds((c - 3) * 256, 1024)
            writes.append(pltpu.make_async_copy(applied_ref.at[:, at], applied_hbm.at[:, at], out_sems.at[c // 4]))
            writes[-1].start()
    for write in writes:
        write.wait()


VMEM = pl.BlockSpec(memory_space=pltpu.VMEM)
SMEM = pl.BlockSpec(memory_space=pltpu.SMEM)


def in_hbm(x):
    return pltpu.with_memory_space_constraint(x, pltpu.HBM)


def call(kernel, outs, scratch, specs, flops, name, args, mib=16, out_specs=None):
    size = sum(a.size * a.dtype.itemsize for a in args)
    return pl.pallas_call(
        kernel,
        out_shape=[jax.ShapeDtypeStruct(s, t) for s, t in outs],
        in_specs=specs,
        out_specs=out_specs or [VMEM] * len(outs),
        scratch_shapes=scratch,
        compiler_params=pltpu.CompilerParams(vmem_limit_bytes=mib * 2**20),
        cost_estimate=pl.CostEstimate(flops=flops, bytes_accessed=0, transcendentals=0),
        name=name,
    )(*args)


def local(
    vectors, tree_order, leaf_basis, near_blocks, near_lists, transfers, couplings, coupling_lists,
    top_transfers, top_couplings, top_lists,
):
    columns, points = vectors.shape
    rank = leaf_basis.shape[0]
    devices = lax.axis_size("leaf")
    halo = REACH * near_blocks.shape[1]
    order = tree_order.reshape(points // 128, 128)
    near_t = jnp.transpose(near_lists)
    lists_t = jnp.transpose(coupling_lists)
    moves = transfers.reshape(rank * rank, -1)
    matrices = couplings.reshape(6, rank * rank, -1)

    any_spec = pl.BlockSpec(memory_space=pl.ANY)
    tile = max(devices // 2 * rank, 128)
    ordered, own0, masked = call(
        leaf_kernel,
        [((columns, points), BF), ((columns, 2048 + halo), BF), ((points // 512, 256, 512), BF)],
        [
            pltpu.VMEM(vectors.shape, BF), pltpu.VMEM(order.shape, jnp.int32),
            pltpu.VMEM(leaf_basis.shape, BF), pltpu.VMEM((points // 256 * columns, 256), BF),
            pltpu.SemaphoreType.DMA((3,)),
        ],
        [any_spec] * 3, 10**9, "leaf", tuple(in_hbm(x) for x in (vectors, order, leaf_basis)),
    )
    pairs = [(i, i ^ 1) for i in range(devices)]
    onward = [(i, i + 2) for i in range(0, devices - 2, 2)] + [(i, i - 2) for i in range(3, devices, 2)]
    first0 = lax.ppermute(own0, "leaf", pairs)
    own1, top, last, weights = call(
        lift_kernel,
        [
            ((columns, 2048), BF), ((columns, tile), BF), ((columns, tile + halo), BF),
            ((16, 256, 256), BF),
        ],
        [pltpu.VMEM((rank, 128, 256), F32)], [VMEM] * 3, 10**9, "lift", (own0, ordered, moves),
    )

    def step(tile_sum, reached):
        return lax.ppermute(tile_sum, "leaf", [(i, i ^ reached) for i in range(devices)])

    steps = [1 << k for k in reversed(range(1, devices.bit_length() - 1))]
    for reached in steps[:-2]:
        top = top + step(top, reached)
    other = step(top, steps[-2])
    coupling_rows, spots, hot, blocks = call(
        matrices_kernel,
        [
            ((16, 256, 256), BF), ((8, 128), jnp.int32), ((points // 256, 256, 256), BF),
            ((points // 256, 256), jnp.int32),
        ],
        [pltpu.VMEM((rank, 128, 256), F32)],
        [VMEM] * 3, 10**6, "matrices", (matrices, lists_t, order),
    )
    first1 = lax.ppermute(own1, "leaf", pairs)
    first0, first1, top, blocks = lax.optimization_barrier((first0, first1, top + other, blocks))
    other = step(top, steps[-1])
    second0 = lax.ppermute(first0, "leaf", onward)
    last = lax.dynamic_update_slice(last, top + other, (0, 0))
    first1, last = lax.optimization_barrier((first1, last))
    other = step(last, 1)
    second1 = lax.ppermute(first1, "leaf", onward)
    first1, ordered = lax.optimization_barrier((first1, ordered))
    (near_part,) = call(
        near_kernel, [((columns, points), F32)],
        [pltpu.VMEM((points // 64, columns, 128), BF)],
        [VMEM, VMEM, SMEM], 10**6, "near", (ordered, near_blocks, near_t),
    )
    (far,) = call(
        far_kernel, [((columns, 4096), F32)],
        [pltpu.VMEM((385, columns, 128), BF), pltpu.VMEM((16 * columns, 256), BF)],
        [VMEM] * 7 + [SMEM], 4 * 10**9, "far",
        (own0, own1, first0, first1, second0, second1, coupling_rows, spots),
    )
    other, far = lax.optimization_barrier((other, far))
    (six,) = call(
        root_kernel, [((columns, 256), F32)], [pltpu.VMEM((2 * devices, columns, 32), F32)],
        [VMEM] * 4 + [SMEM], 10**6, "root",
        (
            last, other, jnp.transpose(top_transfers, (2, 0, 1)), jnp.transpose(top_couplings, (0, 3, 1, 2)),
            jnp.transpose(top_lists),
        ),
    )
    (applied,) = call(
        down_kernel, [((columns, points), F32)],
        [
            pltpu.VMEM((columns, points), F32), pltpu.VMEM((points // 64 + 2 * REACH, columns, 128), BF),
            pltpu.VMEM((points // 256 * columns, 256), BF), pltpu.VMEM((2, REACH) + near_blocks.shape[1:], BF),
            pltpu.SemaphoreType.DMA((2,)), pltpu.SemaphoreType.DMA((points // 1024,)),
        ],
        [VMEM] * 5 + [any_spec, SMEM] + [VMEM] * 5, 4 * 10**9, "down",
        (
            far, near_part, ordered, other, second0, in_hbm(near_blocks), near_t,
            six, blocks, weights, masked, hot,
        ),
        out_specs=[any_spec],
    )
    return applied


def solution(mesh):
    placed = (
        P("rhs", ("groups", "leaf")),
        P(("groups", "leaf")),
        P(None, ("groups", "leaf")),
        P(("groups", "leaf"), None, None),
        P(("groups", "leaf"), None),
        P(None, None, ("groups", "leaf")),
        P(None, None, None, ("groups", "leaf")),
        P(("groups", "leaf"), None),
        P(None, None, "groups"),
        P(None, None, None, "groups"),
        P("groups", None),
    )
    return jax.shard_map(
        local, mesh=mesh, in_specs=placed, out_specs=P("rhs", ("groups", "leaf")), check_vma=False
    )
```
